32 devices in a mesh: gx: 4 (over y, core), gy: 8 (over z, x).
Axes of the slice: x: 2, y: 2, z: 4, core: 2. Of those that a mesh axis runs over, the one named last changes fastest.
Arguments:
- log_perm: float32 [1, 32, 128, 2048], P(None, None, 'gx', 'gy'), may hold values from -4 to 4
- source: float32 [1, 32, 128, 2048], P(None, None, 'gx', 'gy'), may hold values from -24 to 24
Outputs:
- pressure: float32 [1, 32, 128, 2048], P(None, None, 'gx', 'gy')
- residual: float32 [1, 32, 128, 2048], P(None, None, 'gx', 'gy')
- flux_east: float32 [1, 32, 128, 2048], P(None, None, 'gx', 'gy')
- flux_north: float32 [1, 32, 128, 2048], P(None, None, 'gx', 'gy')
The draws below stay inside these ranges and needn't reach their ends.
All inputs are finite; a program needn't handle non-finite values.
Results may differ from the reference program's by a relative error of at most 0.0003.
Values sent between devices are 32-bit elements; how exact they have to be, the bound alone decides.
No kernel may reach another device: no remote copies, remote signals or barrier semaphores. Data moves between devices by JAX's collectives and lax.ppermute only.
A program may use at most 128 MiB of HBM per device.

```python
import jax
import jax.numpy as jnp
from jax import lax

SAMPLES = 1
NZ = 32
OUTER = 2
NX = 128
NY = 2048


def levels(own_key, extent, shards, smallest, top_value):
    def one(dim, shards_of):
        heights = jax.random.uniform(jax.random.fold_in(jax.random.fold_in(own_key, 6), dim), (shards_of,), jnp.float32, smallest / len(shards), top_value / len(shards))
        return jnp.repeat(jnp.exp(heights), extent[dim] // shards_of).reshape((-1,) + (1,) * (len(extent) - dim - 1))

    loudness = one(*shards[0])
    for cut in shards[1:]:
        loudness = loudness * one(*cut)
    return loudness


def centred(key, extent, spread, bound, cuts=(), kind=jnp.bfloat16):
    loudness = levels(key, extent, cuts, -0.22, 0.18) if cuts else 1.0
    values = jax.random.normal(key, extent, jnp.float32) * spread * loudness
    return jnp.minimum(jnp.maximum(values, -bound), bound).astype(kind)


def setup_inputs(seed: int = 0) -> dict:
    key_list = jax.random.split(jax.random.key(seed), 3)
    return {
        "log_perm": centred(key_list[0], (SAMPLES, NZ, NX, NY), 1.0, 4.0, ((2, 4), (3, 8)), jnp.float32),
        "source": centred(key_list[1], (SAMPLES, NZ, NX, NY), 4.0, 24.0, ((2, 4), (3, 8)), jnp.float32),
    }


exact_mode = lax.Precision.HIGHEST


def harmonic(first_perm, second_perm):
    return 2.0 * first_perm * second_perm / (first_perm + second_perm)


def operator_terms(log_values):
    padded = jnp.exp(jnp.pad(log_values, ((0, 0), (1, 1), (1, 1))))
    trans_x = harmonic(padded[:, 1:, 1:-1], padded[:, :-1, 1:-1])
    trans_y = harmonic(padded[:, 1:-1, 1:], padded[:, 1:-1, :-1])
    interior = padded[:, 1:-1, 1:-1]
    trans_z = jnp.pad(harmonic(interior[1:], interior[:-1]), ((1, 1), (0, 0), (0, 0)))
    return trans_x, trans_y, trans_z


def apply_operator(field_in, transmit):
    trans_x, trans_y, trans_z = transmit
    padded = jnp.pad(field_in, ((0, 0), (1, 1), (1, 1)))
    vertical = jnp.pad(field_in, ((1, 1), (0, 0), (0, 0)))
    result = trans_x[:, 1:] * (field_in - padded[:, 2:, 1:-1]) + trans_x[:, :-1] * (field_in - padded[:, :-2, 1:-1])
    result = result + trans_y[:, :, 1:] * (field_in - padded[:, 1:-1, 2:]) + trans_y[:, :, :-1] * (field_in - padded[:, 1:-1, :-2])
    result = result + trans_z[1:] * (field_in - vertical[2:]) + trans_z[:-1] * (field_in - vertical[:-2])
    return result


def recurrence(gram_matrix):
    batch_count = gram_matrix.shape[0]
    identity = jnp.eye(5, dtype=jnp.float32)
    direc_coef = jnp.broadcast_to(identity[0], (batch_count, 5))
    resid_coef = jnp.broadcast_to(identity[3], (batch_count, 5))
    sol_coef = jnp.zeros((batch_count, 5), jnp.float32)
    zero_col = jnp.zeros((batch_count,), jnp.float32)

    def shifted(coef_in):
        return jnp.stack([zero_col, coef_in[:, 0], coef_in[:, 1], zero_col, coef_in[:, 3]], axis=1)

    def quadratic(left_coef, right_coef):
        return jnp.einsum("si,sij,sj->s", left_coef, gram_matrix, right_coef, precision=exact_mode)

    for inner_turn in range(2):
        images = shifted(direc_coef)
        rho_old = quadratic(resid_coef, resid_coef)
        step_size = (rho_old / quadratic(direc_coef, images))[:, None]
        sol_coef = sol_coef + step_size * direc_coef
        resid_coef = resid_coef - step_size * images
        ratio_new = (quadratic(resid_coef, resid_coef) / rho_old)[:, None]
        direc_coef = resid_coef + ratio_new * direc_coef
    return sol_coef, resid_coef, direc_coef


def one_sample(sample_pair):
    log_values, source_field = sample_pair
    transmit = operator_terms(log_values)
    pressure = jnp.zeros_like(source_field)
    resid_field = source_field
    direc_field = source_field
    for outer_turn in range(OUTER):
        power_one = apply_operator(direc_field, transmit)
        power_two = apply_operator(power_one, transmit)
        resid_image = apply_operator(resid_field, transmit)
        basis = jnp.stack([direc_field, power_one, power_two, resid_field, resid_image])
        gram_matrix = jnp.einsum("izxy,jzxy->ij", basis, basis, precision=exact_mode)
        sol_coef, resid_coef, direc_coef = recurrence(gram_matrix[None])
        pressure = pressure + jnp.einsum("i,izxy->zxy", sol_coef[0], basis, precision=exact_mode)
        resid_field = jnp.einsum("i,izxy->zxy", resid_coef[0], basis, precision=exact_mode)
        direc_field = jnp.einsum("i,izxy->zxy", direc_coef[0], basis, precision=exact_mode)
    residual = source_field - apply_operator(pressure, transmit)
    padded = jnp.pad(pressure, ((0, 0), (1, 1), (1, 1)))
    flux_east = transmit[0][:, 1:] * (pressure - padded[:, 2:, 1:-1])
    flux_north = transmit[1][:, :, 1:] * (pressure - padded[:, 1:-1, 2:])
    return pressure, residual, flux_east, flux_north


def reference(log_perm, source):
    pressure, residual, flux_east, flux_north = lax.map(one_sample, (log_perm, source))
    return (pressure, residual, flux_east, flux_north)
```

```python
import functools

import jax
import jax.numpy as jnp
from jax import lax
from jax.experimental import pallas as pl
from jax.experimental.pallas import tpu as pltpu
from jax.sharding import PartitionSpec as P

DEPTH = 4
LANES = 128
SUB = 8
LO = 8
GROUP = 4 * DEPTH
F32 = jnp.float32
VMEM_SPEC = pl.BlockSpec(memory_space=pltpu.VMEM)
ANY_SPEC = pl.BlockSpec(memory_space=pl.ANY)


def in_vmem(*shape):
    return pltpu.VMEM(shape, F32)


def params(limit):
    return pltpu.CompilerParams(vmem_limit_bytes=limit * 1024 * 1024)


def lane_ids():
    return lax.broadcasted_iota(jnp.int32, (SUB, LANES), 1)


def row_ids():
    return lax.broadcasted_iota(jnp.int32, (SUB, LANES), 0)


def turn(value, shift):
    return pltpu.roll(value, shift % LANES, 1)


def reciprocal(value):
    return 1.0 / value


def load_kernel(log_hbm, src_hbm, log_ref, src_ref, head_ref, tail_ref, sems):
    _, layers, rows, cols = log_hbm.shape
    tiles = cols // LANES
    copies = []
    for index, (hbm, ref) in enumerate(((log_hbm, log_ref), (src_hbm, src_ref))):
        for tile in range(tiles):
            copies.append(
                pltpu.make_async_copy(
                    hbm.at[0, :, :, pl.ds(tile * LANES, LANES)],
                    ref.at[:, tile, pl.ds(LO, rows), :],
                    sems.at[index, tile],
                )
            )
            copies[-1].start()
    for copy in copies:
        copy.wait()
    for index, ref in enumerate((log_ref, src_ref)):
        for tile in range(tiles):
            place = pl.ds(tile * DEPTH, DEPTH)
            head_ref[index, :, place, :] = ref[:, tile, LO : LO + DEPTH, :]
            tail_ref[index, :, place, :] = ref[:, tile, LO + rows - DEPTH : LO + rows, :]


def halo_block(past_ref, before_ref, index, layer, tile):
    place = pl.ds(tile * DEPTH, DEPTH)
    return jnp.concatenate([past_ref[index, layer, place, :], before_ref[index, layer, place, :]], axis=0)


def edge_kernel(log_ref, src_ref, past_ref, before_ref, last_ref, first_ref):
    layers, tiles, height, _ = log_ref.shape
    rows = height - 3 * SUB
    lanes = lane_ids()
    for index, ref in enumerate((log_ref, src_ref)):
        for block in range(rows // SUB + 1):
            for out_ref, tile, lane in ((last_ref, tiles - 1, LANES - DEPTH), (first_ref, 0, 0)):
                total = jnp.zeros((SUB, LANES), F32)
                for layer in range(layers):
                    if block < rows // SUB:
                        value = ref[layer, tile, LO + block * SUB : LO + (block + 1) * SUB, :]
                    else:
                        value = halo_block(past_ref, before_ref, index, layer, tile)
                    moved = turn(value, layer * DEPTH - lane)
                    total = jnp.where(lanes // DEPTH == layer, moved, total)
                out_ref[index, block * SUB : (block + 1) * SUB, :] = total


def basis_kernel(
    log_ref,
    src_ref,
    past_ref,
    before_ref,
    last_ref,
    first_ref,
    right_ref,
    left_ref,
    base_ref,
    one_ref,
    two_ref,
    three_ref,
    four_ref,
    face_x_ref,
    face_y_ref,
    rims_ref,
    sums_ref,
    inverse_ref,
    face_w_ref,
    face_z_ref,
    diag_ref,
    strip_ref,
    strip_inv_ref,
    strip_x_ref,
    strip_y_ref,
    strip_w_ref,
    strip_z_ref,
    strip_d_ref,
    rim_ref,
):
    layers, tiles, height, _ = log_ref.shape
    rows = height - 3 * SUB
    slots = layers // (LANES // GROUP)
    blocks = rows // SUB
    ring = LO + rows + SUB
    lanes = lane_ids()
    place = lanes % GROUP
    subs = row_ids()
    here_x, here_y = lax.axis_index("gx"), lax.axis_index("gy")
    past_x, before_x = here_x < lax.axis_size("gx") - 1, here_x > 0
    past_y, before_y = here_y < lax.axis_size("gy") - 1, here_y > 0
    inside_rows = jnp.where(subs < DEPTH, past_x.astype(jnp.int32), before_x.astype(jnp.int32)) > 0
    inside_cols = (
        jnp.where(
            (place >= DEPTH) & (place < 2 * DEPTH),
            past_y.astype(jnp.int32),
            jnp.where((place >= 2 * DEPTH) & (place < 3 * DEPTH), before_y.astype(jnp.int32), 1),
        )
        > 0
    )
    inside_both = inside_rows & inside_cols
    first_lane, last_lane = lanes == 0, lanes == LANES - 1

    def at(block):
        return pl.ds(LO + block * SUB, SUB)

    def shifted(block, step):
        return pl.ds(LO + block * SUB + step, SUB)

    def close_ring(ref, index, block, value):
        if block == 0:
            ref[(*index, pl.ds(ring, 1), slice(None))] = value[0:1]
        if block == blocks:
            ref[(*index, pl.ds(LO - 1, 1), slice(None))] = value[SUB - 1 : SUB]

    def spread(index, block):
        part = pl.ds(block * SUB, SUB)
        packed = [ref[index, part, :] for ref in (last_ref, right_ref, left_ref, first_ref)]
        found = []
        for slot in range(slots):
            moved = [turn(value, (kind - slot) * DEPTH) for kind, value in enumerate(packed)]
            found.append(
                jnp.where(
                    place < 2 * DEPTH,
                    jnp.where(place < DEPTH, moved[0], moved[1]),
                    jnp.where(place < 3 * DEPTH, moved[2], moved[3]),
                )
            )
        return found

    def put_strip(ref, block, values):
        ref[0, at(block), :] = turn(values[-1], GROUP)
        ref[slots + 1, at(block), :] = turn(values[0], -GROUP)
        for slot, value in enumerate(values):
            ref[slot + 1, at(block), :] = value
            close_ring(ref, (slot + 1,), block, value)

    def put_rim(number, block, values):
        for slot, value in enumerate(values):
            other = turn(value, 2 - 2 * DEPTH)
            rim = jnp.where(place == DEPTH, value, other)
            if number is None:
                rim_ref[slot, at(block), :] = rim
            else:
                rims_ref[number, slot, at(block), :] = rim

    def rim_of(ref, index, group, slot, block):
        found = ref[(*index, slot, at(block), slice(None))]
        return pltpu.roll(found, LANES - 1 - DEPTH - group * GROUP, 1)

    def east(values, rim):
        moved = [turn(value, -1) for value in values] + [rim]
        return [jnp.where(last_lane, moved[tile + 1], moved[tile]) for tile in range(tiles)]

    def west(values, rim):
        moved = [rim] + [turn(value, 1) for value in values]
        return [jnp.where(first_lane, moved[tile], moved[tile + 1]) for tile in range(tiles)]

    for block in range(blocks + 1):
        values = spread(1, block)
        put_strip(strip_ref.at[0], block, values)
        put_rim(0, block, values)
        values = [0.5 * jnp.exp(-value) for value in spread(0, block)]
        put_strip(strip_inv_ref, block, values)
        put_rim(None, block, values)
    top, bottom = lanes >= LANES - GROUP, lanes < GROUP
    for block in range(blocks + 1):
        for slot in range(1, slots + 1):
            value = strip_inv_ref[slot, at(block), :]
            face = reciprocal(value + strip_inv_ref[slot, shifted(block, 1), :])
            strip_x_ref[slot - 1, at(block), :] = face
            close_ring(strip_x_ref, (slot - 1,), block, face)
            face = reciprocal(value + turn(value, -1))
            strip_y_ref[slot - 1, at(block), :] = face
            strip_w_ref[slot - 1, at(block), :] = turn(face, 1)
        for slot in range(slots + 1):
            face = reciprocal(strip_inv_ref[slot, at(block), :] + strip_inv_ref[slot + 1, at(block), :])
            if slot == 0:
                face = jnp.where(bottom, 0.0, face)
            if slot == slots:
                face = jnp.where(top, 0.0, face)
            strip_z_ref[slot, at(block), :] = face
    for block in range(blocks + 1):
        for slot in range(slots):
            strip_d_ref[slot, at(block), :] = (
                (strip_x_ref[slot, at(block), :] + strip_x_ref[slot, shifted(block, -1), :])
                + (strip_y_ref[slot, at(block), :] + strip_w_ref[slot, at(block), :])
                + (strip_z_ref[slot, at(block), :] + strip_z_ref[slot + 1, at(block), :])
            )

    for power in range(1, DEPTH):
        old, new = strip_ref.at[power - 1], strip_ref.at[power]
        for block in range(blocks + 1):
            values = []
            for slot in range(slots):
                value = old[slot + 1, at(block), :]
                result = (
                    strip_d_ref[slot, at(block), :] * value
                    - (
                        strip_x_ref[slot, at(block), :] * old[slot + 1, shifted(block, 1), :]
                        + strip_x_ref[slot, shifted(block, -1), :] * old[slot + 1, shifted(block, -1), :]
                    )
                    - (
                        strip_y_ref[slot, at(block), :] * turn(value, -1)
                        + strip_w_ref[slot, at(block), :] * turn(value, 1)
                    )
                    - (
                        strip_z_ref[slot + 1, at(block), :] * old[slot + 2, at(block), :]
                        + strip_z_ref[slot, at(block), :] * old[slot, at(block), :]
                    )
                )
                values.append(jnp.where(inside_both if block == blocks else inside_cols, result, 0.0))
            put_strip(new, block, values)
            put_rim(power, block, values)

    def fill(layer, _):
        for tile in range(tiles):
            for block in range(blocks + 1):
                if block == blocks:
                    value = halo_block(past_ref, before_ref, 0, layer, tile)
                    source = halo_block(past_ref, before_ref, 1, layer, tile)
                    base_ref[layer, tile, at(block), :] = source
                    close_ring(base_ref, (layer, tile), block, source)
                else:
                    value = log_ref[layer, tile, at(block), :]
                if block == 0:
                    close_ring(base_ref, (layer, tile), 0, base_ref[layer, tile, at(0), :])
                value = 0.5 * jnp.exp(-value)
                inverse_ref[layer, tile, at(block), :] = value
                close_ring(inverse_ref, (layer, tile), block, value)
        return 0

    lax.fori_loop(0, layers, fill, 0)

    zero = jnp.zeros((SUB, LANES), F32)
    for tile in range(tiles):
        for block in range(blocks + 1):
            face_z_ref[0, tile, at(block), :] = zero
            face_z_ref[layers, tile, at(block), :] = zero

    def faces(group, _):
        for slot in range(slots):
            layer = group * slots + slot
            for block in range(blocks + 1):
                values = [inverse_ref[layer, tile, at(block), :] for tile in range(tiles)]
                rim = rim_of(rim_ref, (), group, slot, block)
                nexts = east(values, rim)
                ys = [reciprocal(value + other) for value, other in zip(values, nexts, strict=True)]
                before = reciprocal(values[0] + rim)
                ws = west(ys, before)
                for tile in range(tiles):
                    face = reciprocal(values[tile] + inverse_ref[layer, tile, shifted(block, 1), :])
                    face_x_ref[layer, tile, at(block), :] = face
                    close_ring(face_x_ref, (layer, tile), block, face)
                    face_y_ref[layer, tile, at(block), :] = ys[tile]
                    face_w_ref[layer, tile, at(block), :] = ws[tile]

        return 0

    lax.fori_loop(0, layers // slots, faces, 0)

    def faces_z(layer, _):
        for tile in range(tiles):
            for block in range(blocks + 1):
                face_z_ref[layer, tile, at(block), :] = reciprocal(
                    inverse_ref[layer - 1, tile, at(block), :] + inverse_ref[layer, tile, at(block), :]
                )
        return 0

    lax.fori_loop(1, layers, faces_z, 0)

    def diagonal(layer, _):
        for tile in range(tiles):
            for block in range(blocks + 1):
                diag_ref[layer, tile, at(block), :] = (
                    (face_x_ref[layer, tile, at(block), :] + face_x_ref[layer, tile, shifted(block, -1), :])
                    + (face_y_ref[layer, tile, at(block), :] + face_w_ref[layer, tile, at(block), :])
                    + (face_z_ref[layer, tile, at(block), :] + face_z_ref[layer + 1, tile, at(block), :])
                )
        return 0

    lax.fori_loop(0, layers, diagonal, 0)

    def power_step(number, old, new):
        last_power = number == DEPTH

        def chunk(group, sums):
            own_sums, next_sums = list(sums[0]), list(sums[1])
            for block in range(blocks if last_power else blocks + 1):
                levels = []
                for slot in range(-1, slots + 1):
                    layer = group * slots + slot
                    if slot < 0:
                        layer = jnp.maximum(layer, 0)
                    if slot == slots:
                        layer = jnp.minimum(layer, layers - 1)
                    levels.append([old[layer, tile, at(block), :] for tile in range(tiles)])
                for slot in range(slots):
                    layer = group * slots + slot
                    values = levels[slot + 1]
                    rim = rim_of(rims_ref, (number - 1,), group, slot, block)
                    easts, wests = east(values, rim), west(values, rim)
                    for tile in range(tiles):
                        value = values[tile]
                        result = (
                            diag_ref[layer, tile, at(block), :] * value
                            - (
                                face_x_ref[layer, tile, at(block), :] * old[layer, tile, shifted(block, 1), :]
                                + face_x_ref[layer, tile, shifted(block, -1), :]
                                * old[layer, tile, shifted(block, -1), :]
                            )
                            - (
                                face_y_ref[layer, tile, at(block), :] * easts[tile]
                                + face_w_ref[layer, tile, at(block), :] * wests[tile]
                            )
                            - (
                                face_z_ref[layer + 1, tile, at(block), :] * levels[slot + 2][tile]
                                + face_z_ref[layer, tile, at(block), :] * levels[slot][tile]
                            )
                        )
                        if block == blocks:
                            result = jnp.where(inside_rows, result, 0.0)
                        else:
                            own_sums[tile] = own_sums[tile] + value * value
                            next_sums[tile] = next_sums[tile] + value * result
                        new[layer, tile, at(block), :] = result
                        if not last_power:
                            close_ring(new, (layer, tile), block, result)
            return tuple(own_sums), tuple(next_sums)

        start = (zero,) * tiles
        own_sums, next_sums = lax.fori_loop(0, layers // slots, chunk, (start, start))
        for which, parts in enumerate((own_sums, next_sums)):
            total = functools.reduce(jnp.add, parts)
            row = 2 * (number - 1) + which
            sums_ref[row : row + 1, :] = jnp.sum(total, axis=0, keepdims=True)

    fields = (base_ref, one_ref, two_ref, three_ref, four_ref)
    for number in range(1, DEPTH + 1):
        power_step(number, fields[number - 1], fields[number])


def two_sum(first, second):
    total = first + second
    part = total - first
    return total, (first - (total - part)) + (second - part)


def quick_sum(first, second):
    total = first + second
    return total, second - (total - first)


def halves(value):
    scaled = 4097.0 * value
    high = scaled - (scaled - value)
    return high, value - high


def two_product(first, second):
    total = first * second
    first_high, first_low = halves(first)
    second_high, second_low = halves(second)
    rest = ((first_high * second_high - total) + first_high * second_low + first_low * second_high) + (
        first_low * second_low
    )
    return total, rest


def pair_add(first, second):
    total, rest = two_sum(first[0], second[0])
    return quick_sum(total, rest + (first[1] + second[1]))


def pair_sub(first, second):
    return pair_add(first, (-second[0], -second[1]))


def pair_mul(first, second):
    total, rest = two_product(first[0], second[0])
    return quick_sum(total, rest + (first[0] * second[1] + first[1] * second[0]))


def pair_div(first, second):
    guess = first[0] / second[0]
    total, rest = two_product(guess, second[0])
    left = ((first[0] - total) - rest) + (first[1] - guess * second[1])
    return quick_sum(guess, left / second[0])


def galerkin(moments):
    count = DEPTH
    matrix = {(i, j): moments[i + j + 1] for i in range(count) for j in range(i + 1)}
    right = [moments[i] for i in range(count)]
    for pivot in range(count):
        for i in range(pivot + 1, count):
            ratio = pair_div(matrix[i, pivot], matrix[pivot, pivot])
            for j in range(pivot + 1, i + 1):
                matrix[i, j] = pair_sub(matrix[i, j], pair_mul(ratio, matrix[j, pivot]))
            right[i] = pair_sub(right[i], pair_mul(ratio, right[pivot]))
    found = [None] * count
    for i in reversed(range(count)):
        value = right[i]
        for j in range(i + 1, count):
            value = pair_sub(value, pair_mul(matrix[j, i], found[j]))
        found[i] = pair_div(value, matrix[i, i])
    return [value[0] for value in found]


def finish_kernel(
    sums_ref,
    base_ref,
    one_ref,
    two_ref,
    three_ref,
    four_ref,
    face_x_ref,
    face_y_ref,
    rims_ref,
    pressure_hbm,
    residual_hbm,
    east_hbm,
    north_hbm,
    pressure_ref,
    residual_ref,
    east_ref,
    north_ref,
    field_ref,
    sems,
):
    layers, tiles, height, _ = base_ref.shape
    rows = height - 3 * SUB
    slots = layers // (LANES // GROUP)
    blocks = rows // SUB
    last_lane = lane_ids() == LANES - 1
    fields = (base_ref, one_ref, two_ref, three_ref, four_ref)

    total, rest = sums_ref[...], jnp.zeros((SUB, LANES), F32)
    step = 1
    while step < LANES:
        total, lost = two_sum(total, turn(total, step))
        rest = rest + turn(rest, step) + lost
        step *= 2
    total, rest = quick_sum(total, rest)
    coefs = galerkin([(total[k : k + 1], rest[k : k + 1]) for k in range(2 * DEPTH)])
    coefs = [jnp.broadcast_to(value, (SUB, LANES)) for value in coefs]

    def at(block, step=0):
        return pl.ds(LO + block * SUB + step, SUB)

    def mix(values):
        return functools.reduce(jnp.add, [coef * value for coef, value in zip(coefs, values, strict=True)])

    outs = (
        (pressure_ref, pressure_hbm),
        (residual_ref, residual_hbm),
        (east_ref, east_hbm),
        (north_ref, north_hbm),
    )

    def copies(group):
        part = pl.ds(group * slots, slots)
        return [
            pltpu.make_async_copy(ref.at[part], hbm.at[0, part], sems.at[index, group])
            for index, (ref, hbm) in enumerate(outs)
        ]

    def chunk(group, _):
        for slot in range(slots):
            layer = group * slots + slot
            for block in range(blocks + 1):
                values = []
                for tile in range(tiles):
                    found = [ref[layer, tile, at(block), :] for ref in fields[: DEPTH + (block < blocks)]]
                    value = mix(found[:DEPTH])
                    values.append(value)
                    field_ref[tile, at(block), :] = value
                    if block < blocks:
                        spot = (layer, pl.ds(block * SUB, SUB), pl.ds(tile * LANES, LANES))
                        pressure_ref[spot] = value
                        residual_ref[spot] = found[0] - mix(found[1:])
                if block < blocks:
                    rim = mix([rims_ref[power, slot, at(block), :] for power in range(DEPTH)])
                    rim = pltpu.roll(rim, LANES - 1 - DEPTH - group * GROUP, 1)
                    moved = [turn(value, -1) for value in values] + [rim]
                    for tile in range(tiles):
                        other = jnp.where(last_lane, moved[tile + 1], moved[tile])
                        spot = (layer, pl.ds(block * SUB, SUB), pl.ds(tile * LANES, LANES))
                        north_ref[spot] = face_y_ref[layer, tile, at(block), :] * (values[tile] - other)
            for block in range(blocks):
                for tile in range(tiles):
                    spot = (layer, pl.ds(block * SUB, SUB), pl.ds(tile * LANES, LANES))
                    east_ref[spot] = face_x_ref[layer, tile, at(block), :] * (
                        field_ref[tile, at(block), :] - field_ref[tile, at(block, 1), :]
                    )
        for copy in copies(group):
            copy.start()
        return 0

    lax.fori_loop(0, layers // slots, chunk, 0)

    def drain(group, _):
        for copy in copies(group):
            copy.wait()
        return 0

    lax.fori_loop(0, layers // slots, drain, 0)


def send(value, axis, step):
    count = lax.axis_size(axis)
    return lax.ppermute(value, axis, [(i, i + step) for i in range(count) if 0 <= i + step < count])


def total_over(value, axis):
    step = 1
    while step < lax.axis_size(axis):
        value = value + lax.ppermute(value, axis, [(i, i ^ step) for i in range(lax.axis_size(axis))])
        step *= 2
    return value


def on_device(log_perm, source):
    _, layers, rows, cols = log_perm.shape
    tiles, slots, blocks = cols // LANES, layers // (LANES // GROUP), rows // SUB
    height = rows + 3 * SUB
    full = (layers, tiles, height, LANES)
    ends = (2, layers, tiles * DEPTH, LANES)
    edges = (2, rows + SUB, LANES)
    log_own, src_own, head, tail = pl.pallas_call(
        load_kernel,
        out_shape=(in_vmem(*full), in_vmem(*full), in_vmem(*ends), in_vmem(*ends)),
        in_specs=[ANY_SPEC] * 2,
        out_specs=[VMEM_SPEC] * 4,
        scratch_shapes=[pltpu.SemaphoreType.DMA((2, tiles))],
        compiler_params=params(16),
        name="load",
    )(log_perm, source)
    past = send(head, "gx", -1)
    before = send(tail, "gx", 1)
    last, first = pl.pallas_call(
        edge_kernel,
        out_shape=(in_vmem(*edges), in_vmem(*edges)),
        in_specs=[VMEM_SPEC] * 4,
        out_specs=[VMEM_SPEC] * 2,
        compiler_params=params(16),
        name="edges",
    )(log_own, src_own, past, before)
    right = send(first, "gy", -1)
    left = send(last, "gy", 1)
    strip = (slots + 2, height, LANES)
    inner = (slots, height, LANES)
    results = pl.pallas_call(
        basis_kernel,
        out_shape=(in_vmem(*full),) * 7 + (in_vmem(DEPTH, *inner), in_vmem(SUB, LANES)),
        in_specs=[VMEM_SPEC] * 8,
        out_specs=[VMEM_SPEC] * 9,
        input_output_aliases={1: 0},
        scratch_shapes=[
            in_vmem(*full),
            in_vmem(*full),
            in_vmem(layers + 1, *full[1:]),
            in_vmem(*full),
            in_vmem(DEPTH, *strip),
            in_vmem(*strip),
            in_vmem(*inner),
            in_vmem(*inner),
            in_vmem(*inner),
            in_vmem(slots + 1, height, LANES),
            in_vmem(*inner),
            in_vmem(*inner),
        ],
        compiler_params=params(24),
        name="basis",
    )(log_own, src_own, past, before, last, first, right, left)
    *fields, sums = results
    sums = total_over(total_over(sums, "gx"), "gy")
    block = (layers, rows, cols)
    return pl.pallas_call(
        finish_kernel,
        out_shape=(jax.ShapeDtypeStruct((1, *block), F32),) * 4,
        in_specs=[VMEM_SPEC] * 9,
        out_specs=[ANY_SPEC] * 4,
        scratch_shapes=[in_vmem(*block)] * 4
        + [in_vmem(tiles, height, LANES), pltpu.SemaphoreType.DMA((4, layers // slots))],
        compiler_params=params(16),
        name="finish",
    )(sums, *fields)


def solution(mesh):
    spec = P(None, None, "gx", "gy")
    return jax.shard_map(on_device, mesh=mesh, in_specs=(spec,) * 2, out_specs=(spec,) * 4, check_vma=False)
```

```python
import functools

import jax
import jax.numpy as jnp
from jax import lax
from jax.experimental import pallas as pl
from jax.experimental.pallas import tpu as pltpu
from jax.sharding import PartitionSpec as P

DEPTH = 4
LANES = 128
SUB = 8
LO = 8
GROUP = 4 * DEPTH
F32 = jnp.float32
HBM_SPEC = pl.BlockSpec(memory_space=pltpu.HBM)
VMEM_SPEC = pl.BlockSpec(memory_space=pltpu.VMEM)
ANY_SPEC = pl.BlockSpec(memory_space=pl.ANY)


def in_vmem(*shape):
    return pltpu.VMEM(shape, F32)


def params(limit):
    return pltpu.CompilerParams(vmem_limit_bytes=limit * 1024 * 1024)


def lane_ids():
    return lax.broadcasted_iota(jnp.int32, (SUB, LANES), 1)


def row_ids():
    return lax.broadcasted_iota(jnp.int32, (SUB, LANES), 0)


def turn(value, shift):
    return pltpu.roll(value, shift % LANES, 1)


def reciprocal(value):
    return 1.0 / value


def even(axis):
    return lax.rem(lax.axis_index(axis), 2) == 0


def ends_kernel(log_hbm, src_hbm, near_ref, far_ref, rows_ref, sems):
    _, _, rows, cols = log_hbm.shape
    copies = []
    for index, hbm in enumerate((log_hbm, src_hbm)):
        for end, start in enumerate((0, rows - SUB)):
            for tile in range(cols // LANES):
                copies.append(
                    pltpu.make_async_copy(
                        hbm.at[0, :, pl.ds(start, SUB), pl.ds(tile * LANES, LANES)],
                        rows_ref.at[index, end, tile],
                        sems.at[index, end, tile],
                    )
                )
                copies[-1].start()
    for copy in copies:
        copy.wait()
    first = even("gx")
    for tile in range(cols // LANES):
        head = rows_ref[:, 0, tile, :, 0:DEPTH, :]
        tail = rows_ref[:, 1, tile, :, SUB - DEPTH : SUB, :]
        part = pl.ds(tile * DEPTH, DEPTH)
        near_ref[:, :, part, :] = jnp.where(first, tail, head)
        far_ref[:, :, part, :] = jnp.where(first, head, tail)


def pack(blocks_of, lane):
    lanes = lane_ids()
    total = None
    for layer, value in enumerate(blocks_of):
        moved = turn(value, layer * DEPTH - lane)
        total = moved if total is None else jnp.where(lanes // DEPTH == layer, moved, total)
    return total


def own_kernel(
    log_hbm,
    src_hbm,
    base_ref,
    inverse_ref,
    face_x_ref,
    face_y_ref,
    face_z_ref,
    last_ref,
    first_ref,
    log_ref,
    sems,
):
    _, layers, rows, cols = log_hbm.shape
    tiles, blocks = cols // LANES, rows // SUB
    slots = layers // (LANES // GROUP)
    ring = LO + rows + SUB
    last_lane = lane_ids() == LANES - 1
    copies = []
    for index, (hbm, ref) in enumerate(((log_hbm, log_ref), (src_hbm, base_ref))):
        for tile in range(tiles):
            copies.append(
                pltpu.make_async_copy(
                    hbm.at[0, :, :, pl.ds(tile * LANES, LANES)],
                    ref.at[:, tile, pl.ds(LO, rows), :],
                    sems.at[index, tile],
                )
            )
            copies[-1].start()
    for copy in copies[:tiles]:
        copy.wait()

    def at(block, step=0):
        return pl.ds(LO + block * SUB + step, SUB)

    def fill(layer, _):
        for tile in range(tiles):
            for block in range(blocks):
                value = 0.5 * jnp.exp(-log_ref[layer, tile, at(block), :])
                inverse_ref[layer, tile, at(block), :] = value
                if block == 0:
                    inverse_ref[layer, tile, pl.ds(ring, 1), :] = value[0:1]
        return 0

    lax.fori_loop(0, layers, fill, 0, unroll=slots)

    zero = jnp.zeros((SUB, LANES), F32)
    for tile in range(tiles):
        for block in range(blocks + 1):
            face_z_ref[0, tile, at(block), :] = zero
            face_z_ref[layers, tile, at(block), :] = zero

    def faces(layer, _):
        for block in range(blocks):
            values = [inverse_ref[layer, tile, at(block), :] for tile in range(tiles)]
            moved = [turn(value, -1) for value in values]
            for tile in range(tiles):
                other = moved[tile]
                if tile < tiles - 1:
                    other = jnp.where(last_lane, moved[tile + 1], other)
                face_y_ref[layer, tile, at(block), :] = reciprocal(values[tile] + other)
                face_x_ref[layer, tile, at(block), :] = reciprocal(
                    values[tile] + inverse_ref[layer, tile, at(block, 1), :]
                )
        return 0

    lax.fori_loop(0, layers, faces, 0, unroll=slots)

    def faces_z(layer, _):
        for tile in range(tiles):
            for block in range(blocks):
                face_z_ref[layer, tile, at(block), :] = reciprocal(
                    inverse_ref[layer - 1, tile, at(block), :] + inverse_ref[layer, tile, at(block), :]
                )
        return 0

    lax.fori_loop(1, layers, faces_z, 0, unroll=slots)

    for copy in copies[tiles:]:
        copy.wait()

    base_ref[:, :, pl.ds(ring, 1), :] = base_ref[:, :, pl.ds(LO, 1), :]
    for index, ref in enumerate((log_ref, base_ref)):
        for block in range(blocks):
            part = pl.ds(block * SUB, SUB)
            last_ref[index, part, :] = pack(
                [ref[layer, tiles - 1, at(block), :] for layer in range(layers)], LANES - DEPTH
            )
            first_ref[index, part, :] = pack([ref[layer, 0, at(block), :] for layer in range(layers)], 0)


def edge_kernel(near_in, far_in, last_in, first_in, last_ref, first_ref, near_ref, far_ref, halo_ref):
    del last_in, first_in
    _, layers, tiles, _, _ = halo_ref.shape
    height = last_ref.shape[1]
    one, two = even("gx"), even("gy")
    for tile in range(tiles):
        part = pl.ds(tile * DEPTH, DEPTH)
        near, far = near_in[:, :, part, :], far_in[:, :, part, :]
        halo_ref[:, :, tile, 0:DEPTH, :] = jnp.where(one, near, far)
        halo_ref[:, :, tile, DEPTH:SUB, :] = jnp.where(one, far, near)
    for index in range(2):
        part = pl.ds(height - SUB, SUB)
        last_ref[index, part, :] = pack(
            [halo_ref[index, layer, tiles - 1] for layer in range(layers)], LANES - DEPTH
        )
        first_ref[index, part, :] = pack([halo_ref[index, layer, 0] for layer in range(layers)], 0)
    near_ref[...] = jnp.where(two, last_ref[...], first_ref[...])
    far_ref[...] = jnp.where(two, first_ref[...], last_ref[...])


def basis_kernel(
    halo_ref,
    last_ref,
    first_ref,
    near_ref,
    far_ref,
    base_in,
    inverse_in,
    face_x_in,
    face_y_in,
    face_z_in,
    base_ref,
    inverse_ref,
    face_x_ref,
    face_y_ref,
    face_z_ref,
    one_ref,
    two_ref,
    three_ref,
    four_ref,
    rims_ref,
    sums_ref,
    strip_ref,
    strip_inv_ref,
    strip_x_ref,
    strip_y_ref,
    strip_z_ref,
    rim_ref,
):
    del base_in, inverse_in, face_x_in, face_y_in, face_z_in
    layers, tiles, height, _ = base_ref.shape
    rows = height - 3 * SUB
    slots = layers // (LANES // GROUP)
    groups = layers // slots
    blocks = rows // SUB
    ring = LO + rows + SUB
    lanes = lane_ids()
    place = lanes % GROUP
    subs = row_ids()
    here_x, here_y = lax.axis_index("gx"), lax.axis_index("gy")
    past_x, before_x = here_x < lax.axis_size("gx") - 1, here_x > 0
    past_y, before_y = here_y < lax.axis_size("gy") - 1, here_y > 0
    inside_rows = jnp.where(subs < DEPTH, past_x.astype(jnp.int32), before_x.astype(jnp.int32)) > 0
    inside_cols = (
        jnp.where(
            (place >= DEPTH) & (place < 2 * DEPTH),
            past_y.astype(jnp.int32),
            jnp.where((place >= 2 * DEPTH) & (place < 3 * DEPTH), before_y.astype(jnp.int32), 1),
        )
        > 0
    )
    inside_both = inside_rows & inside_cols
    first_lane, last_lane = lanes == 0, lanes == LANES - 1
    first_y = even("gy")

    def at(block, step=0):
        return pl.ds(LO + block * SUB + step, SUB)

    def close_ring(ref, index, block, value):
        if block == 0:
            ref[(*index, pl.ds(ring, 1), slice(None))] = value[0:1]
        if block == blocks:
            ref[(*index, pl.ds(LO - 1, 1), slice(None))] = value[SUB - 1 : SUB]

    def spread(index, block):
        part = pl.ds(block * SUB, SUB)
        near, far = near_ref[index, part, :], far_ref[index, part, :]
        packed = (
            last_ref[index, part, :],
            jnp.where(first_y, near, far),
            jnp.where(first_y, far, near),
            first_ref[index, part, :],
        )
        found = []
        for slot in range(slots):
            moved = [turn(value, (kind - slot) * DEPTH) for kind, value in enumerate(packed)]
            found.append(
                jnp.where(
                    place < 2 * DEPTH,
                    jnp.where(place < DEPTH, moved[0], moved[1]),
                    jnp.where(place < 3 * DEPTH, moved[2], moved[3]),
                )
            )
        return found

    def put_strip(ref, block, values):
        ref[0, at(block), :] = turn(values[-1], GROUP)
        ref[slots + 1, at(block), :] = turn(values[0], -GROUP)
        for slot, value in enumerate(values):
            ref[slot + 1, at(block), :] = value
            close_ring(ref, (slot + 1,), block, value)

    def rim_of(values, group):
        return pltpu.roll(values, LANES - 1 - DEPTH - group * GROUP, 1)

    def x_part(face_ref, index, old, old_index, block, value):
        there = old[(*old_index, at(block, 1), slice(None))]
        back = old[(*old_index, at(block, -1), slice(None))]
        return face_ref[(*index, at(block), slice(None))] * (value - there) - face_ref[
            (*index, at(block, -1), slice(None))
        ] * (back - value)

    for block in range(blocks + 1):
        put_strip(strip_ref.at[0], block, spread(1, block))
        values = [0.5 * jnp.exp(-value) for value in spread(0, block)]
        put_strip(strip_inv_ref, block, values)
        for slot, value in enumerate(values):
            rim_ref[slot, at(block), :] = value
    top, bottom = lanes >= LANES - GROUP, lanes < GROUP
    for block in range(blocks + 1):
        for slot in range(1, slots + 1):
            value = strip_inv_ref[slot, at(block), :]
            face = reciprocal(value + strip_inv_ref[slot, at(block, 1), :])
            strip_x_ref[slot - 1, at(block), :] = face
            close_ring(strip_x_ref, (slot - 1,), block, face)
            strip_y_ref[slot - 1, at(block), :] = reciprocal(value + turn(value, -1))
        for slot in range(slots + 1):
            face = reciprocal(strip_inv_ref[slot, at(block), :] + strip_inv_ref[slot + 1, at(block), :])
            if slot == 0:
                face = jnp.where(bottom, 0.0, face)
            if slot == slots:
                face = jnp.where(top, 0.0, face)
            strip_z_ref[slot, at(block), :] = face

    for power in range(1, DEPTH + 1):
        old = strip_ref.at[power - 1]
        for block in range(blocks + 1):
            levels = [old[slot, at(block), :] for slot in range(slots + 2)]
            ups = [
                strip_z_ref[slot, at(block), :] * (levels[slot] - levels[slot + 1]) for slot in range(slots + 1)
            ]
            values = []
            for slot in range(slots):
                value = levels[slot + 1]
                flux = strip_y_ref[slot, at(block), :] * (value - turn(value, -1))
                rims_ref[power - 1, slot, at(block), :] = jnp.where(
                    place == DEPTH, value, turn(flux, 2 - 2 * DEPTH)
                )
                if power < DEPTH:
                    result = (
                        (flux - turn(flux, 1))
                        + x_part(strip_x_ref, (slot,), old, (slot + 1,), block, value)
                        + (ups[slot + 1] - ups[slot])
                    )
                    values.append(jnp.where(inside_both if block == blocks else inside_cols, result, 0.0))
            if power < DEPTH:
                put_strip(strip_ref.at[power], block, values)

    def fill(layer, _):
        for tile in range(tiles):
            source = halo_ref[1, layer, tile]
            base_ref[layer, tile, at(blocks), :] = source
            close_ring(base_ref, (layer, tile), blocks, source)
            inverse_ref[layer, tile, at(blocks), :] = 0.5 * jnp.exp(-halo_ref[0, layer, tile])
        return 0

    lax.fori_loop(0, layers, fill, 0, unroll=slots)

    def faces(group, _):
        for slot in range(slots):
            layer = group * slots + slot
            for block in range(blocks + 1):
                rim = rim_of(rim_ref[slot, at(block), :], group)
                whole = block == blocks
                values = [inverse_ref[layer, tile, at(block), :] for tile in range(tiles)]
                if whole:
                    moved = [turn(value, -1) for value in values] + [rim]
                    for tile in range(tiles):
                        other = jnp.where(last_lane, moved[tile + 1], moved[tile])
                        face_y_ref[layer, tile, at(block), :] = reciprocal(values[tile] + other)
                else:
                    face_y_ref[layer, tiles - 1, at(block), :] = jnp.where(
                        last_lane, reciprocal(values[-1] + rim), face_y_ref[layer, tiles - 1, at(block), :]
                    )
                if block >= blocks - 1:
                    for tile in range(tiles):
                        face = reciprocal(values[tile] + inverse_ref[layer, tile, at(block, 1), :])
                        face_x_ref[layer, tile, at(block), :] = face
                        close_ring(face_x_ref, (layer, tile), block, face)
        return 0

    lax.fori_loop(0, groups, faces, 0)

    def faces_z(layer, _):
        for tile in range(tiles):
            face_z_ref[layer, tile, at(blocks), :] = reciprocal(
                inverse_ref[layer - 1, tile, at(blocks), :] + inverse_ref[layer, tile, at(blocks), :]
            )
        return 0

    lax.fori_loop(1, layers, faces_z, 0, unroll=slots)

    zero = jnp.zeros((SUB, LANES), F32)

    def power_step(number, old, new):
        last_power = number == DEPTH

        def chunk(group, sums):
            own_sums, next_sums = list(sums[0]), list(sums[1])
            for block in range(blocks if last_power else blocks + 1):
                levels = []
                for slot in range(-1, slots + 1):
                    layer = group * slots + slot
                    if slot < 0:
                        layer = jnp.maximum(layer, 0)
                    if slot == slots:
                        layer = jnp.minimum(layer, layers - 1)
                    levels.append([old[layer, tile, at(block), :] for tile in range(tiles)])
                ups = [
                    [
                        face_z_ref[group * slots + slot, tile, at(block), :]
                        * (levels[slot][tile] - levels[slot + 1][tile])
                        for tile in range(tiles)
                    ]
                    for slot in range(slots + 1)
                ]
                for slot in range(slots):
                    layer = group * slots + slot
                    values = levels[slot + 1]
                    rim = rim_of(rims_ref[number - 1, slot, at(block), :], group)
                    moved = [turn(value, -1) for value in values] + [rim]
                    flux = [
                        face_y_ref[layer, tile, at(block), :]
                        * (values[tile] - jnp.where(last_lane, moved[tile + 1], moved[tile]))
                        for tile in range(tiles)
                    ]
                    moved = [rim] + [turn(value, 1) for value in flux]
                    for tile in range(tiles):
                        value = values[tile]
                        result = (
                            (flux[tile] - jnp.where(first_lane, moved[tile], moved[tile + 1]))
                            + x_part(face_x_ref, (layer, tile), old, (layer, tile), block, value)
                            + (ups[slot + 1][tile] - ups[slot][tile])
                        )
                        if block == blocks:
                            result = jnp.where(inside_rows, result, 0.0)
                        else:
                            own_sums[tile] = own_sums[tile] + value * value
                            next_sums[tile] = next_sums[tile] + value * result
                        new[layer, tile, at(block), :] = result
                        if not last_power:
                            close_ring(new, (layer, tile), block, result)
            return tuple(own_sums), tuple(next_sums)

        start = (zero,) * tiles
        own_sums, next_sums = lax.fori_loop(0, groups, chunk, (start, start), unroll=1)
        found = []
        for parts in (own_sums, next_sums):
            total = functools.reduce(jnp.add, parts)
            found.append(jnp.sum(total, axis=0, keepdims=True))
        return found

    fields = (base_ref, one_ref, two_ref, three_ref, four_ref)
    found = []
    for number in range(1, DEPTH + 1):
        found += power_step(number, fields[number - 1], fields[number])
    total = jnp.concatenate(found, axis=0)
    for peer in range(sums_ref.shape[0]):
        sums_ref[peer] = total


def two_sum(first, second):
    total = first + second
    part = total - first
    return total, (first - (total - part)) + (second - part)


def quick_sum(first, second):
    total = first + second
    return total, second - (total - first)


def halves(value):
    scaled = 4097.0 * value
    high = scaled - (scaled - value)
    return high, value - high


def two_product(first, second):
    total = first * second
    first_high, first_low = halves(first)
    second_high, second_low = halves(second)
    rest = ((first_high * second_high - total) + first_high * second_low + first_low * second_high) + (
        first_low * second_low
    )
    return total, rest


def pair_add(first, second):
    total, rest = two_sum(first[0], second[0])
    return quick_sum(total, rest + (first[1] + second[1]))


def pair_sub(first, second):
    return pair_add(first, (-second[0], -second[1]))


def pair_mul(first, second):
    total, rest = two_product(first[0], second[0])
    return quick_sum(total, rest + (first[0] * second[1] + first[1] * second[0]))


def pair_div(first, second):
    guess = first[0] / second[0]
    total, rest = two_product(guess, second[0])
    left = ((first[0] - total) - rest) + (first[1] - guess * second[1])
    return quick_sum(guess, left / second[0])


def galerkin(moments):
    count = DEPTH
    matrix = {(i, j): moments[i + j + 1] for i in range(count) for j in range(i + 1)}
    right = [moments[i] for i in range(count)]
    for pivot in range(count):
        for i in range(pivot + 1, count):
            ratio = pair_div(matrix[i, pivot], matrix[pivot, pivot])
            for j in range(pivot + 1, i + 1):
                matrix[i, j] = pair_sub(matrix[i, j], pair_mul(ratio, matrix[j, pivot]))
            right[i] = pair_sub(right[i], pair_mul(ratio, right[pivot]))
    found = [None] * count
    for i in reversed(range(count)):
        value = right[i]
        for j in range(i + 1, count):
            value = pair_sub(value, pair_mul(matrix[j, i], found[j]))
        found[i] = pair_div(value, matrix[i, i])
    return [value[0] for value in found]


def finish_kernel(
    sums_ref,
    base_ref,
    one_ref,
    two_ref,
    three_ref,
    four_ref,
    face_x_ref,
    face_y_ref,
    rims_ref,
    pressure_hbm,
    residual_hbm,
    east_hbm,
    north_hbm,
    pressure_ref,
    residual_ref,
    east_ref,
    north_ref,
    field_ref,
    sems,
):
    layers, tiles, height, _ = base_ref.shape
    rows = height - 3 * SUB
    slots = layers // (LANES // GROUP)
    blocks = rows // SUB
    last_lane = lane_ids() == LANES - 1
    fields = (base_ref, one_ref, two_ref, three_ref, four_ref)

    total = functools.reduce(jnp.add, [sums_ref[peer] for peer in range(sums_ref.shape[0])])
    rest = jnp.zeros((SUB, LANES), F32)
    step = 1
    while step < LANES:
        total, lost = two_sum(total, turn(total, step))
        rest = rest + turn(rest, step) + lost
        step *= 2
    total, rest = quick_sum(total, rest)
    coefs = galerkin([(total[k : k + 1], rest[k : k + 1]) for k in range(2 * DEPTH)])
    coefs = [jnp.broadcast_to(value, (SUB, LANES)) for value in coefs]

    def at(block, step=0):
        return pl.ds(LO + block * SUB + step, SUB)

    def mix(values):
        return functools.reduce(jnp.add, [coef * value for coef, value in zip(coefs, values, strict=True)])

    outs = (
        (pressure_ref, pressure_hbm),
        (residual_ref, residual_hbm),
        (east_ref, east_hbm),
        (north_ref, north_hbm),
    )

    def copies(group):
        part = pl.ds(group * slots, slots)
        return [
            pltpu.make_async_copy(ref.at[part], hbm.at[0, part], sems.at[index, group])
            for index, (ref, hbm) in enumerate(outs)
        ]

    def chunk(group, _):
        for slot in range(slots):
            layer = group * slots + slot
            for block in range(blocks + 1):
                values = []
                for tile in range(tiles):
                    found = [ref[layer, tile, at(block), :] for ref in fields[: DEPTH + (block < blocks)]]
                    value = mix(found[:DEPTH])
                    values.append(value)
                    field_ref[tile, at(block), :] = value
                    if block < blocks:
                        spot = (layer, pl.ds(block * SUB, SUB), pl.ds(tile * LANES, LANES))
                        pressure_ref[spot] = value
                        residual_ref[spot] = found[0] - mix(found[1:])
                if block < blocks:
                    rim = mix([rims_ref[power, slot, at(block), :] for power in range(DEPTH)])
                    rim = pltpu.roll(rim, LANES - 1 - DEPTH - group * GROUP, 1)
                    moved = [turn(value, -1) for value in values] + [rim]
                    for tile in range(tiles):
                        other = jnp.where(last_lane, moved[tile + 1], moved[tile])
                        spot = (layer, pl.ds(block * SUB, SUB), pl.ds(tile * LANES, LANES))
                        north_ref[spot] = face_y_ref[layer, tile, at(block), :] * (values[tile] - other)
            for block in range(blocks):
                for tile in range(tiles):
                    spot = (layer, pl.ds(block * SUB, SUB), pl.ds(tile * LANES, LANES))
                    east_ref[spot] = face_x_ref[layer, tile, at(block), :] * (
                        field_ref[tile, at(block), :] - field_ref[tile, at(block, 1), :]
                    )
        for copy in copies(group):
            copy.start()
        return 0

    lax.fori_loop(0, layers // slots, chunk, 0)

    def drain(group, _):
        for copy in copies(group):
            copy.wait()
        return 0

    lax.fori_loop(0, layers // slots, drain, 0)


def exchange(value, axis, near):
    count = lax.axis_size(axis)
    pairs = []
    for i in range(count):
        other = i + 1 if (i % 2 == 0) == near else i - 1
        if 0 <= other < count:
            pairs.append((i, other))
    return lax.ppermute(value, axis, pairs)


def on_device(log_perm, source):
    _, layers, rows, cols = log_perm.shape
    tiles, slots = cols // LANES, layers // (LANES // GROUP)
    height = rows + 3 * SUB
    full = (layers, tiles, height, LANES)
    deep = (layers + 1, tiles, height, LANES)
    ends = (2, layers, tiles * DEPTH, LANES)
    edges = (2, rows + SUB, LANES)
    strip = (slots + 2, height, LANES)
    inner = (slots, height, LANES)
    peers = lax.axis_size("gx") * lax.axis_size("gy")
    cells = layers * rows * cols

    near, far = pl.pallas_call(
        ends_kernel,
        out_shape=(in_vmem(*ends),) * 2,
        in_specs=[HBM_SPEC] * 2,
        out_specs=[VMEM_SPEC] * 2,
        scratch_shapes=[in_vmem(2, 2, tiles, layers, SUB, LANES), pltpu.SemaphoreType.DMA((2, 2, tiles))],
        compiler_params=params(16),
        name="ends",
    )(log_perm, source)
    far = exchange(far, "gx", False)
    near = exchange(near, "gx", True)
    *fields, last, first = pl.pallas_call(
        own_kernel,
        out_shape=(in_vmem(*full),) * 4 + (in_vmem(*deep),) + (in_vmem(*edges),) * 2,
        in_specs=[HBM_SPEC] * 2,
        out_specs=[VMEM_SPEC] * 7,
        scratch_shapes=[in_vmem(*full), pltpu.SemaphoreType.DMA((2, tiles))],
        compiler_params=params(16),
        cost_estimate=pl.CostEstimate(flops=60 * cells, bytes_accessed=8 * cells, transcendentals=4 * cells),
        name="own",
    )(log_perm, source)
    last, first, near, far, halo = pl.pallas_call(
        edge_kernel,
        out_shape=(in_vmem(*edges),) * 4 + (in_vmem(2, layers, tiles, SUB, LANES),),
        in_specs=[VMEM_SPEC] * 4,
        out_specs=[VMEM_SPEC] * 5,
        input_output_aliases={2: 0, 3: 1},
        compiler_params=params(16),
        name="edges",
    )(near, far, last, first)
    far = exchange(far, "gy", False)
    near = exchange(near, "gy", True)
    results = pl.pallas_call(
        basis_kernel,
        out_shape=(in_vmem(*full),) * 4
        + (in_vmem(*deep),)
        + (in_vmem(*full),) * 4
        + (in_vmem(DEPTH, *inner), in_vmem(peers, SUB, LANES)),
        in_specs=[VMEM_SPEC] * 10,
        out_specs=[VMEM_SPEC] * 11,
        input_output_aliases={5: 0, 6: 1, 7: 2, 8: 3, 9: 4},
        scratch_shapes=[
            in_vmem(DEPTH, *strip),
            in_vmem(*strip),
            in_vmem(*inner),
            in_vmem(*inner),
            in_vmem(slots + 1, height, LANES),
            in_vmem(*inner),
        ],
        compiler_params=params(16),
        name="basis",
    )(halo, last, first, near, far, *fields)
    base, _, face_x, face_y, _, *powers, rims, sums = results
    sums = lax.all_to_all(sums, ("gx", "gy"), 0, 0)
    block = (layers, rows, cols)
    return pl.pallas_call(
        finish_kernel,
        out_shape=(jax.ShapeDtypeStruct((1, *block), F32),) * 4,
        in_specs=[VMEM_SPEC] * 9,
        out_specs=[ANY_SPEC] * 4,
        scratch_shapes=[in_vmem(*block)] * 4
        + [in_vmem(tiles, height, LANES), pltpu.SemaphoreType.DMA((4, layers // slots))],
        compiler_params=params(16),
        name="finish",
    )(sums, base, *powers, face_x, face_y, rims)


def solution(mesh):
    spec = P(None, None, "gx", "gy")
    return jax.shard_map(on_device, mesh=mesh, in_specs=(spec,) * 2, out_specs=(spec,) * 4, check_vma=False)
```

```python
import functools

import jax
import jax.numpy as jnp
from jax import lax
from jax.experimental import pallas as pl
from jax.experimental.pallas import tpu as pltpu
from jax.sharding import PartitionSpec as P

DEPTH = 4
LANES = 128
SUB = 8
LO = 8
GROUP = 4 * DEPTH
HALO_LAYERS = 16
F32 = jnp.float32
HBM_SPEC = pl.BlockSpec(memory_space=pltpu.HBM)
VMEM_SPEC = pl.BlockSpec(memory_space=pltpu.VMEM)
ANY_SPEC = pl.BlockSpec(memory_space=pl.ANY)


def in_vmem(*shape):
    return pltpu.VMEM(shape, F32)


def params(limit):
    return pltpu.CompilerParams(vmem_limit_bytes=limit * 1024 * 1024)


def lane_ids():
    return lax.broadcasted_iota(jnp.int32, (SUB, LANES), 1)


def row_ids():
    return lax.broadcasted_iota(jnp.int32, (SUB, LANES), 0)


def turn(value, shift):
    return pltpu.roll(value, shift % LANES, 1)


def reciprocal(value):
    return 1.0 / value


def even(axis):
    return lax.rem(lax.axis_index(axis), 2) == 0


def ends_kernel(log_hbm, src_hbm, near_ref, far_ref, rows_ref, sems):
    _, _, rows, cols = log_hbm.shape
    copies = []
    for index, hbm in enumerate((log_hbm, src_hbm)):
        for end, start in enumerate((0, rows - SUB)):
            for tile in range(cols // LANES):
                copies.append(
                    pltpu.make_async_copy(
                        hbm.at[0, :, pl.ds(start, SUB), pl.ds(tile * LANES, LANES)],
                        rows_ref.at[index, end, tile],
                        sems.at[index, end, tile],
                    )
                )
                copies[-1].start()
    for copy in copies:
        copy.wait()
    first = even("gx")
    for tile in range(cols // LANES):
        head = rows_ref[:, 0, tile, :, 0:DEPTH, :]
        tail = rows_ref[:, 1, tile, :, SUB - DEPTH : SUB, :]
        part = pl.ds(tile * DEPTH, DEPTH)
        near_ref[:, :, part, :] = jnp.where(first, tail, head)
        far_ref[:, :, part, :] = jnp.where(first, head, tail)


def pack(blocks_of, lane):
    lanes = lane_ids()
    total = None
    for layer, value in enumerate(blocks_of):
        moved = turn(value, layer * DEPTH - lane)
        total = moved if total is None else jnp.where(lanes // DEPTH == layer, moved, total)
    return total


def own_kernel(
    log_hbm,
    src_hbm,
    fields_ref,
    inverse_ref,
    face_x_ref,
    face_y_ref,
    face_z_ref,
    last_ref,
    first_ref,
    log_ref,
    sems,
):
    _, layers, rows, cols = log_hbm.shape
    tiles, blocks = cols // LANES, rows // SUB
    slots = layers // (LANES // GROUP)
    ring = LO + rows + SUB
    last_lane = lane_ids() == LANES - 1
    base_ref = fields_ref.at[0]
    copies = []
    for index, (hbm, ref) in enumerate(((log_hbm, log_ref), (src_hbm, base_ref))):
        for tile in range(tiles):
            copies.append(
                pltpu.make_async_copy(
                    hbm.at[0, :, :, pl.ds(tile * LANES, LANES)],
                    ref.at[:, tile, pl.ds(LO, rows), :],
                    sems.at[index, tile],
                )
            )
            copies[-1].start()
    for copy in copies[:tiles]:
        copy.wait()

    def at(block, step=0):
        return pl.ds(LO + block * SUB + step, SUB)

    def fill(layer, _):
        for tile in range(tiles):
            for block in range(blocks):
                value = 0.5 * jnp.exp(-log_ref[layer, tile, at(block), :])
                inverse_ref[layer, tile, at(block), :] = value
                if block == 0:
                    inverse_ref[layer, tile, pl.ds(ring, 1), :] = value[0:1]
        return 0

    lax.fori_loop(0, layers, fill, 0, unroll=slots)

    zero = jnp.zeros((SUB, LANES), F32)
    for tile in range(tiles):
        for block in range(blocks + 1):
            face_z_ref[0, tile, at(block), :] = zero
            face_z_ref[layers, tile, at(block), :] = zero

    def faces(layer, _):
        for block in range(blocks):
            values = [inverse_ref[layer, tile, at(block), :] for tile in range(tiles)]
            moved = [turn(value, -1) for value in values]
            for tile in range(tiles):
                other = moved[tile]
                if tile < tiles - 1:
                    other = jnp.where(last_lane, moved[tile + 1], other)
                face = reciprocal(values[tile] + other)
                face_y_ref[layer, tile, at(block), :] = face if tile < tiles - 1 else jnp.where(last_lane, 0.0, face)
                face_x_ref[layer, tile, at(block), :] = reciprocal(
                    values[tile] + inverse_ref[layer, tile, at(block, 1), :]
                )
        return 0

    lax.fori_loop(0, layers, faces, 0, unroll=slots)

    def faces_z(layer, _):
        for tile in range(tiles):
            for block in range(blocks):
                face_z_ref[layer, tile, at(block), :] = reciprocal(
                    inverse_ref[layer - 1, tile, at(block), :] + inverse_ref[layer, tile, at(block), :]
                )
        return 0

    lax.fori_loop(1, layers, faces_z, 0, unroll=slots)

    for copy in copies[tiles:]:
        copy.wait()

    base_ref[:, :, pl.ds(ring, 1), :] = base_ref[:, :, pl.ds(LO, 1), :]
    for index, ref in enumerate((log_ref, base_ref)):
        for block in range(blocks):
            part = pl.ds(block * SUB, SUB)
            last_ref[index, part, :] = pack(
                [ref[layer, tiles - 1, at(block), :] for layer in range(layers)], LANES - DEPTH
            )
            first_ref[index, part, :] = pack([ref[layer, 0, at(block), :] for layer in range(layers)], 0)


def edge_kernel(near_in, far_in, last_in, first_in, last_ref, first_ref, near_ref, far_ref, halo_ref):
    del last_in, first_in
    _, layers, tiles, _, _ = halo_ref.shape
    height = last_ref.shape[1]
    one, two = even("gx"), even("gy")
    for tile in range(tiles):
        part = pl.ds(tile * DEPTH, DEPTH)
        near, far = near_in[:, :, part, :], far_in[:, :, part, :]
        halo_ref[:, :, tile, 0:DEPTH, :] = jnp.where(one, near, far)
        halo_ref[:, :, tile, DEPTH:SUB, :] = jnp.where(one, far, near)
    for index in range(2):
        part = pl.ds(height - SUB, SUB)
        last_ref[index, part, :] = pack(
            [halo_ref[index, layer, tiles - 1] for layer in range(layers)], LANES - DEPTH
        )
        first_ref[index, part, :] = pack([halo_ref[index, layer, 0] for layer in range(layers)], 0)
    near_ref[...] = jnp.where(two, last_ref[...], first_ref[...])
    far_ref[...] = jnp.where(two, first_ref[...], last_ref[...])


def place_of(block, step=0):
    return pl.ds(LO + block * SUB + step, SUB)


def close_ring(ref, index, block, blocks, value):
    ring = LO + (blocks + 1) * SUB
    if block == 0:
        ref[(*index, pl.ds(ring, 1), slice(None))] = value[0:1]
    if block == blocks:
        ref[(*index, pl.ds(LO - 1, 1), slice(None))] = value[SUB - 1 : SUB]


def rim_of(values, group):
    return pltpu.roll(values, LANES - 1 - DEPTH - group * GROUP, 1)


def x_part(face_ref, index, old, old_index, block, value):
    there = old[(*old_index, place_of(block, 1), slice(None))]
    back = old[(*old_index, place_of(block, -1), slice(None))]
    return face_ref[(*index, place_of(block), slice(None))] * (value - there) - face_ref[
        (*index, place_of(block, -1), slice(None))
    ] * (back - value)


def inside_masks():
    here_x, here_y = lax.axis_index("gx"), lax.axis_index("gy")
    past_x, before_x = here_x < lax.axis_size("gx") - 1, here_x > 0
    past_y, before_y = here_y < lax.axis_size("gy") - 1, here_y > 0
    place = lane_ids() % GROUP
    inside_rows = jnp.where(row_ids() < DEPTH, past_x.astype(jnp.int32), before_x.astype(jnp.int32)) > 0
    inside_cols = (
        jnp.where(
            (place >= DEPTH) & (place < 2 * DEPTH),
            past_y.astype(jnp.int32),
            jnp.where((place >= 2 * DEPTH) & (place < 3 * DEPTH), before_y.astype(jnp.int32), 1),
        )
        > 0
    )
    return inside_rows, inside_cols


def apply_power(number, fields_ref, face_x_ref, face_y_ref, face_z_ref, rims_ref):
    _, layers, tiles, height, _ = fields_ref.shape
    blocks = (height - 3 * SUB) // SUB
    slots = layers // (LANES // GROUP)
    groups = layers // slots
    old, new = fields_ref.at[number - 1], fields_ref.at[number]
    lanes = lane_ids()
    first_lane, last_lane = lanes == 0, lanes == LANES - 1
    inside_rows, _ = inside_masks()
    at = place_of

    def layer_range(start, count, block):
        levels = []
        for step in range(-1, count + 1):
            layer = start + step
            if step < 0:
                layer = jnp.maximum(layer, 0)
            if step == count:
                layer = jnp.minimum(layer, layers - 1)
            levels.append([old[layer, tile, at(block), :] for tile in range(tiles)])
        ups = [
            [
                face_z_ref[start + step, tile, at(block), :] * (levels[step][tile] - levels[step + 1][tile])
                for tile in range(tiles)
            ]
            for step in range(count + 1)
        ]
        for step in range(count):
            layer = start + step
            values = levels[step + 1]
            moved = [turn(value, -1) for value in values]
            flux = []
            for tile in range(tiles):
                other = moved[tile]
                if tile < tiles - 1:
                    other = jnp.where(last_lane, moved[tile + 1], other)
                flux.append(face_y_ref[layer, tile, at(block), :] * (values[tile] - other))
            rim = None
            if rims_ref is not None:
                rim = rim_of(rims_ref[number - 1, step % slots, at(block), :], start // slots + step // slots)
            moved = [turn(value, 1) for value in flux]
            moved = [moved[-1] if rim is None else rim] + moved
            if rim is not None:
                flux[-1] = jnp.where(last_lane, rim, flux[-1])
            for tile in range(tiles):
                value = values[tile]
                result = (
                    (flux[tile] - jnp.where(first_lane, moved[tile], moved[tile + 1]))
                    + x_part(face_x_ref, (layer, tile), old, (layer, tile), block, value)
                    + (ups[step + 1][tile] - ups[step][tile])
                )
                if block == blocks:
                    result = jnp.where(inside_rows, result, 0.0)
                new[layer, tile, at(block), :] = result
                if number < DEPTH:
                    close_ring(new, (layer, tile), block, blocks, result)
                yield tile, value, result

    def chunk(group, sums):
        own_sums, next_sums = list(sums[0]), list(sums[1])
        for block in range(blocks):
            for tile, value, result in layer_range(group * slots, slots, block):
                own_sums[tile] = own_sums[tile] + value * value
                next_sums[tile] = next_sums[tile] + value * result
        return tuple(own_sums), tuple(next_sums)

    def halo_chunk(part, _):
        for _ in layer_range(part * HALO_LAYERS, HALO_LAYERS, blocks):
            pass
        return 0

    start = (jnp.zeros((SUB, LANES), F32),) * tiles
    sums = lax.fori_loop(0, groups, chunk, (start, start), unroll=2)
    if number < DEPTH:
        lax.fori_loop(0, layers // HALO_LAYERS, halo_chunk, 0)
    return [functools.reduce(jnp.add, parts) for parts in sums]


def first_kernel(
    halo_ref,
    fields_in,
    inverse_in,
    face_x_in,
    face_y_in,
    face_z_in,
    fields_ref,
    inverse_ref,
    face_x_ref,
    face_y_ref,
    face_z_ref,
    parts_ref,
):
    del fields_in, inverse_in, face_x_in, face_y_in, face_z_in
    _, layers, tiles, height, _ = fields_ref.shape
    blocks = (height - 3 * SUB) // SUB
    slots = layers // (LANES // GROUP)
    last_lane = lane_ids() == LANES - 1
    at = place_of

    def fill(layer, _):
        for tile in range(tiles):
            source = halo_ref[1, layer, tile]
            fields_ref[0, layer, tile, at(blocks), :] = source
            close_ring(fields_ref, (0, layer, tile), blocks, blocks, source)
            inverse_ref[layer, tile, at(blocks), :] = 0.5 * jnp.exp(-halo_ref[0, layer, tile])
        return 0

    lax.fori_loop(0, layers, fill, 0, unroll=2 * slots)

    def faces(layer, _):
        values = [inverse_ref[layer, tile, at(blocks), :] for tile in range(tiles)]
        moved = [turn(value, -1) for value in values]
        for tile in range(tiles):
            other = moved[tile]
            if tile < tiles - 1:
                other = jnp.where(last_lane, moved[tile + 1], other)
            face = reciprocal(values[tile] + other)
            face_y_ref[layer, tile, at(blocks), :] = face if tile < tiles - 1 else jnp.where(last_lane, 0.0, face)
            for block in (blocks - 1, blocks):
                face = reciprocal(
                    inverse_ref[layer, tile, at(block), :] + inverse_ref[layer, tile, at(block, 1), :]
                )
                face_x_ref[layer, tile, at(block), :] = face
                close_ring(face_x_ref, (layer, tile), block, blocks, face)
            before = inverse_ref[jnp.maximum(layer - 1, 0), tile, at(blocks), :]
            face_z_ref[layer, tile, at(blocks), :] = jnp.where(layer > 0, reciprocal(before + values[tile]), 0.0)
        return 0

    lax.fori_loop(0, layers, faces, 0, unroll=2 * slots)
    found = apply_power(1, fields_ref, face_x_ref, face_y_ref, face_z_ref, None)
    for which, part in enumerate(found):
        parts_ref[which] = part


def basis_kernel(
    last_ref,
    first_ref,
    far_ref,
    near_ref,
    parts_ref,
    face_x_ref,
    face_y_ref,
    face_z_ref,
    fields_in,
    fields_ref,
    rims_ref,
    sums_ref,
    strip_ref,
    strip_inv_ref,
    strip_x_ref,
    strip_y_ref,
    strip_z_ref,
):
    del fields_in
    _, layers, tiles, height, _ = fields_ref.shape
    rows = height - 3 * SUB
    slots = layers // (LANES // GROUP)
    groups = layers // slots
    blocks = rows // SUB
    lanes = lane_ids()
    place = lanes % GROUP
    inside_rows, inside_cols = inside_masks()
    inside_both = inside_rows & inside_cols
    first_lane, last_lane = lanes == 0, lanes == LANES - 1
    first_y = even("gy")
    at = place_of

    def spread(index, block):
        part = pl.ds(block * SUB, SUB)
        near, far = near_ref[index, part, :], far_ref[index, part, :]
        packed = (
            last_ref[index, part, :],
            jnp.where(first_y, near, far),
            jnp.where(first_y, far, near),
            first_ref[index, part, :],
        )
        found = []
        for slot in range(slots):
            moved = [turn(value, (kind - slot) * DEPTH) for kind, value in enumerate(packed)]
            found.append(
                jnp.where(
                    place < 2 * DEPTH,
                    jnp.where(place < DEPTH, moved[0], moved[1]),
                    jnp.where(place < 3 * DEPTH, moved[2], moved[3]),
                )
            )
        return found

    def put_strip(ref, block, values):
        ref[0, at(block), :] = turn(values[-1], GROUP)
        ref[slots + 1, at(block), :] = turn(values[0], -GROUP)
        for slot, value in enumerate(values):
            ref[slot + 1, at(block), :] = value
            close_ring(ref, (slot + 1,), block, blocks, value)

    for block in range(blocks + 1):
        put_strip(strip_ref.at[0], block, spread(1, block))
        values = [0.5 * jnp.exp(-value) for value in spread(0, block)]
        put_strip(strip_inv_ref, block, values)
    top, bottom = lanes >= LANES - GROUP, lanes < GROUP
    for block in range(blocks + 1):
        for slot in range(1, slots + 1):
            value = strip_inv_ref[slot, at(block), :]
            face = reciprocal(value + strip_inv_ref[slot, at(block, 1), :])
            strip_x_ref[slot - 1, at(block), :] = face
            close_ring(strip_x_ref, (slot - 1,), block, blocks, face)
            strip_y_ref[slot - 1, at(block), :] = reciprocal(value + turn(value, -1))
        for slot in range(slots + 1):
            face = reciprocal(strip_inv_ref[slot, at(block), :] + strip_inv_ref[slot + 1, at(block), :])
            if slot == 0:
                face = jnp.where(bottom, 0.0, face)
            if slot == slots:
                face = jnp.where(top, 0.0, face)
            strip_z_ref[slot, at(block), :] = face

    for power in range(1, DEPTH + 1):
        old = strip_ref.at[power - 1]
        for block in range(blocks + 1):
            levels = [old[slot, at(block), :] for slot in range(slots + 2)]
            ups = [
                strip_z_ref[slot, at(block), :] * (levels[slot] - levels[slot + 1]) for slot in range(slots + 1)
            ]
            values = []
            for slot in range(slots):
                value = levels[slot + 1]
                flux = strip_y_ref[slot, at(block), :] * (value - turn(value, -1))
                after = turn(flux, 1)
                rims_ref[power - 1, slot, at(block), :] = jnp.where(
                    place == DEPTH, after, turn(flux, 2 - 2 * DEPTH)
                )
                if power < DEPTH:
                    result = (
                        (flux - after)
                        + x_part(strip_x_ref, (slot,), old, (slot + 1,), block, value)
                        + (ups[slot + 1] - ups[slot])
                    )
                    values.append(jnp.where(inside_both if block == blocks else inside_cols, result, 0.0))
            if power < DEPTH:
                put_strip(strip_ref.at[power], block, values)

    zero = jnp.zeros((SUB, LANES), F32)

    def complete(group, lost):
        for slot in range(slots):
            layer = group * slots + slot
            for block in range(blocks + 1):
                rim = rim_of(rims_ref[0, slot, at(block), :], group)
                for tile, part in ((0, jnp.where(first_lane, -rim, 0.0)), (tiles - 1, jnp.where(last_lane, rim, 0.0))):
                    value = fields_ref[1, layer, tile, at(block), :] + part
                    fields_ref[1, layer, tile, at(block), :] = value
                    close_ring(fields_ref, (1, layer, tile), block, blocks, value)
                    if block < blocks:
                        lost = lost + part * fields_ref[0, layer, tile, at(block), :]
        return lost

    lost = lax.fori_loop(0, groups, complete, zero)

    found = [parts_ref[0], parts_ref[1] + lost]
    for number in range(2, DEPTH + 1):
        found += apply_power(number, fields_ref, face_x_ref, face_y_ref, face_z_ref, rims_ref)
    total = jnp.concatenate([jnp.sum(part, axis=0, keepdims=True) for part in found], axis=0)
    share = LANES // SUB
    step = LANES // 2
    while step >= share:
        total = total + turn(total, step)
        step //= 2
    total = jnp.sum(jnp.where(lanes // share == row_ids(), total, 0.0), axis=0, keepdims=True)
    sums_ref[...] = jnp.broadcast_to(total, sums_ref.shape)


def two_sum(first, second):
    total = first + second
    part = total - first
    return total, (first - (total - part)) + (second - part)


def quick_sum(first, second):
    total = first + second
    return total, second - (total - first)


def halves(value):
    scaled = 4097.0 * value
    high = scaled - (scaled - value)
    return high, value - high


def two_product(first, second):
    total = first * second
    first_high, first_low = halves(first)
    second_high, second_low = halves(second)
    rest = ((first_high * second_high - total) + first_high * second_low + first_low * second_high) + (
        first_low * second_low
    )
    return total, rest


def pair_add(first, second):
    total, rest = two_sum(first[0], second[0])
    return quick_sum(total, rest + (first[1] + second[1]))


def pair_sub(first, second):
    return pair_add(first, (-second[0], -second[1]))


def pair_mul(first, second):
    total, rest = two_product(first[0], second[0])
    return quick_sum(total, rest + (first[0] * second[1] + first[1] * second[0]))


def pair_div(first, second):
    guess = first[0] / second[0]
    total, rest = two_product(guess, second[0])
    left = ((first[0] - total) - rest) + (first[1] - guess * second[1])
    return quick_sum(guess, left / second[0])


def galerkin(moments):
    count = DEPTH
    matrix = {(i, j): moments[i + j + 1] for i in range(count) for j in range(i + 1)}
    right = [moments[i] for i in range(count)]
    for pivot in range(count):
        for i in range(pivot + 1, count):
            ratio = pair_div(matrix[i, pivot], matrix[pivot, pivot])
            for j in range(pivot + 1, i + 1):
                matrix[i, j] = pair_sub(matrix[i, j], pair_mul(ratio, matrix[j, pivot]))
            right[i] = pair_sub(right[i], pair_mul(ratio, right[pivot]))
    found = [None] * count
    for i in reversed(range(count)):
        value = right[i]
        for j in range(i + 1, count):
            value = pair_sub(value, pair_mul(matrix[j, i], found[j]))
        found[i] = pair_div(value, matrix[i, i])
    return [value[0] for value in found]


def finish_kernel(
    sums_ref,
    fields_ref,
    face_x_ref,
    face_y_ref,
    rims_ref,
    pressure_hbm,
    residual_hbm,
    east_hbm,
    north_hbm,
    pressure_ref,
    residual_ref,
    east_ref,
    north_ref,
    field_ref,
    sems,
):
    _, layers, tiles, height, _ = fields_ref.shape
    rows = height - 3 * SUB
    slots = layers // (LANES // GROUP)
    blocks = rows // SUB
    last_lane = lane_ids() == LANES - 1

    total = jnp.sum(sums_ref[...], axis=0, keepdims=True)
    total = jnp.where(lane_ids() // (LANES // SUB) == row_ids(), total, 0.0)
    rest = jnp.zeros((SUB, LANES), F32)
    step = 1
    while step < LANES:
        total, lost = two_sum(total, turn(total, step))
        rest = rest + turn(rest, step) + lost
        step *= 2
    total, rest = quick_sum(total, rest)
    coefs = galerkin([(total[k : k + 1], rest[k : k + 1]) for k in range(2 * DEPTH)])
    coefs = [jnp.broadcast_to(value, (SUB, LANES)) for value in coefs]

    def at(block, step=0):
        return pl.ds(LO + block * SUB + step, SUB)

    def mix(values):
        return functools.reduce(jnp.add, [coef * value for coef, value in zip(coefs, values, strict=True)])

    outs = (
        (pressure_ref, pressure_hbm),
        (residual_ref, residual_hbm),
        (east_ref, east_hbm),
        (north_ref, north_hbm),
    )

    def copies(group):
        part = pl.ds(group * slots, slots)
        return [
            pltpu.make_async_copy(ref.at[part], hbm.at[0, part], sems.at[index, group])
            for index, (ref, hbm) in enumerate(outs)
        ]

    def chunk(group, _):
        for slot in range(slots):
            layer = group * slots + slot
            for block in range(blocks + 1):
                values = []
                for tile in range(tiles):
                    found = [
                        fields_ref[power, layer, tile, at(block), :] for power in range(DEPTH + (block < blocks))
                    ]
                    value = mix(found[:DEPTH])
                    values.append(value)
                    field_ref[tile, at(block), :] = value
                    if block < blocks:
                        spot = (layer, pl.ds(block * SUB, SUB), pl.ds(tile * LANES, LANES))
                        pressure_ref[spot] = value
                        residual_ref[spot] = found[0] - mix(found[1:])
                if block < blocks:
                    rim = mix([rims_ref[power, slot, at(block), :] for power in range(DEPTH)])
                    rim = rim_of(rim, group)
                    moved = [turn(value, -1) for value in values]
                    for tile in range(tiles):
                        other = moved[tile]
                        if tile < tiles - 1:
                            other = jnp.where(last_lane, moved[tile + 1], other)
                        flux = face_y_ref[layer, tile, at(block), :] * (values[tile] - other)
                        if tile == tiles - 1:
                            flux = jnp.where(last_lane, rim, flux)
                        spot = (layer, pl.ds(block * SUB, SUB), pl.ds(tile * LANES, LANES))
                        north_ref[spot] = flux
            for block in range(blocks):
                for tile in range(tiles):
                    spot = (layer, pl.ds(block * SUB, SUB), pl.ds(tile * LANES, LANES))
                    east_ref[spot] = face_x_ref[layer, tile, at(block), :] * (
                        field_ref[tile, at(block), :] - field_ref[tile, at(block, 1), :]
                    )
        for copy in copies(group):
            copy.start()
        return 0

    lax.fori_loop(0, layers // slots, chunk, 0)

    def drain(group, _):
        for copy in copies(group):
            copy.wait()
        return 0

    lax.fori_loop(0, layers // slots, drain, 0)


def exchange(value, axis, near):
    count = lax.axis_size(axis)
    pairs = []
    for i in range(count):
        other = i + 1 if (i % 2 == 0) == near else i - 1
        if 0 <= other < count:
            pairs.append((i, other))
    return lax.ppermute(value, axis, pairs)


def on_device(log_perm, source):
    _, layers, rows, cols = log_perm.shape
    tiles, slots = cols // LANES, layers // (LANES // GROUP)
    height = rows + 3 * SUB
    full = (layers, tiles, height, LANES)
    deep = (layers + 1, tiles, height, LANES)
    ends = (2, layers, tiles * DEPTH, LANES)
    edges = (2, rows + SUB, LANES)
    strip = (slots + 2, height, LANES)
    inner = (slots, height, LANES)
    peers = lax.axis_size("gx") * lax.axis_size("gy")
    cells = layers * rows * cols

    log_perm, source = (pltpu.with_memory_space_constraint(value, pltpu.HBM) for value in (log_perm, source))
    powers = (in_vmem(DEPTH + 1, *full),) + (in_vmem(*full),) * 3 + (in_vmem(*deep),)
    near, far = pl.pallas_call(
        ends_kernel,
        out_shape=(in_vmem(*ends),) * 2,
        in_specs=[HBM_SPEC] * 2,
        out_specs=[VMEM_SPEC] * 2,
        scratch_shapes=[in_vmem(2, 2, tiles, layers, SUB, LANES), pltpu.SemaphoreType.DMA((2, 2, tiles))],
        compiler_params=params(16),
        name="ends",
    )(log_perm, source)
    far = exchange(far, "gx", False)
    near = exchange(near, "gx", True)
    *fields, last, first = pl.pallas_call(
        own_kernel,
        out_shape=powers + (in_vmem(*edges),) * 2,
        in_specs=[HBM_SPEC] * 2,
        out_specs=[VMEM_SPEC] * 7,
        scratch_shapes=[in_vmem(*full), pltpu.SemaphoreType.DMA((2, tiles))],
        compiler_params=params(16),
        cost_estimate=pl.CostEstimate(flops=60 * cells, bytes_accessed=8 * cells, transcendentals=4 * cells),
        name="own",
    )(log_perm, source)
    last, first, near, far, halo = pl.pallas_call(
        edge_kernel,
        out_shape=(in_vmem(*edges),) * 4 + (in_vmem(2, layers, tiles, SUB, LANES),),
        in_specs=[VMEM_SPEC] * 4,
        out_specs=[VMEM_SPEC] * 5,
        input_output_aliases={2: 0, 3: 1},
        compiler_params=params(16),
        name="edges",
    )(near, far, last, first)
    far = exchange(far, "gy", False)
    near = exchange(near, "gy", True)
    fields, _, face_x, face_y, face_z, parts = pl.pallas_call(
        first_kernel,
        out_shape=powers + (in_vmem(2, SUB, LANES),),
        in_specs=[VMEM_SPEC] * 6,
        out_specs=[VMEM_SPEC] * 6,
        input_output_aliases={1: 0, 2: 1, 3: 2, 4: 3, 5: 4},
        compiler_params=params(16),
        cost_estimate=pl.CostEstimate(flops=40 * cells, bytes_accessed=8 * cells, transcendentals=cells),
        name="first",
    )(halo, *fields)
    fields, rims, sums = pl.pallas_call(
        basis_kernel,
        out_shape=(powers[0], in_vmem(DEPTH, *inner), in_vmem(peers, LANES)),
        in_specs=[VMEM_SPEC] * 9,
        out_specs=[VMEM_SPEC] * 3,
        input_output_aliases={8: 0},
        scratch_shapes=[
            in_vmem(DEPTH, *strip),
            in_vmem(*strip),
            in_vmem(*inner),
            in_vmem(*inner),
            in_vmem(slots + 1, height, LANES),
        ],
        compiler_params=params(16),
        name="basis",
    )(last, first, far, near, parts, face_x, face_y, face_z, fields)
    sums = lax.all_to_all(sums, ("gx", "gy"), 0, 0, tiled=True)
    block = (layers, rows, cols)
    return pl.pallas_call(
        finish_kernel,
        out_shape=(jax.ShapeDtypeStruct((1, *block), F32),) * 4,
        in_specs=[VMEM_SPEC] * 5,
        out_specs=[ANY_SPEC] * 4,
        scratch_shapes=[in_vmem(*block)] * 4
        + [in_vmem(tiles, height, LANES), pltpu.SemaphoreType.DMA((4, layers // slots))],
        compiler_params=params(16),
        name="finish",
    )(sums, fields, face_x, face_y, rims)


def solution(mesh):
    spec = P(None, None, "gx", "gy")
    return jax.shard_map(on_device, mesh=mesh, in_specs=(spec,) * 2, out_specs=(spec,) * 4, check_vma=False)
```

```python
import functools

import jax
import jax.numpy as jnp
from jax import lax
from jax.experimental import pallas as pl
from jax.experimental.pallas import tpu as pltpu
from jax.sharding import PartitionSpec as P

DEPTH = 4
LANES = 128
SUB = 8
LO = 8
GROUP = 4 * DEPTH
HALO_LAYERS = 16
F32 = jnp.float32
HBM_SPEC = pl.BlockSpec(memory_space=pltpu.HBM)
VMEM_SPEC = pl.BlockSpec(memory_space=pltpu.VMEM)
ANY_SPEC = pl.BlockSpec(memory_space=pl.ANY)


def in_vmem(*shape):
    return pltpu.VMEM(shape, F32)


def params(limit):
    return pltpu.CompilerParams(vmem_limit_bytes=limit * 1024 * 1024)


def lane_ids():
    return lax.broadcasted_iota(jnp.int32, (SUB, LANES), 1)


def row_ids():
    return lax.broadcasted_iota(jnp.int32, (SUB, LANES), 0)


def turn(value, shift):
    return pltpu.roll(value, shift % LANES, 1)


def reciprocal(value):
    return 1.0 / value


def even(axis):
    return lax.rem(lax.axis_index(axis), 2) == 0


def far_kernel(log_hbm, src_hbm, far_ref, rows_ref, sems):
    _, _, rows, cols = log_hbm.shape
    first = even("gx")
    start = pl.multiple_of(jnp.where(first, 0, rows - SUB), SUB)
    copies = []
    for index, hbm in enumerate((log_hbm, src_hbm)):
        for tile in range(cols // LANES):
            copies.append(
                pltpu.make_async_copy(
                    hbm.at[0, :, pl.ds(start, SUB), pl.ds(tile * LANES, LANES)],
                    rows_ref.at[index, tile],
                    sems.at[index, tile],
                )
            )
            copies[-1].start()
    for copy in copies:
        copy.wait()
    for tile in range(cols // LANES):
        head = rows_ref[:, tile, :, 0:DEPTH, :]
        tail = rows_ref[:, tile, :, SUB - DEPTH : SUB, :]
        far_ref[:, :, pl.ds(tile * DEPTH, DEPTH), :] = jnp.where(first, head, tail)


def load_kernel(log_hbm, src_hbm, log_ref, fields_ref, near_ref, sems):
    _, _, rows, cols = log_hbm.shape
    tiles = cols // LANES
    first = even("gx")
    copies = []
    refs = (log_ref, fields_ref.at[0])
    for index, (hbm, ref) in enumerate(zip((log_hbm, src_hbm), refs, strict=True)):
        for tile in range(tiles):
            copies.append(
                pltpu.make_async_copy(
                    hbm.at[0, :, :, pl.ds(tile * LANES, LANES)],
                    ref.at[:, tile, pl.ds(LO, rows), :],
                    sems.at[index, tile],
                )
            )
            copies[-1].start()
    for copy in copies:
        copy.wait()
    for index, ref in enumerate(refs):
        for tile in range(tiles):
            head = ref[:, tile, LO : LO + DEPTH, :]
            tail = ref[:, tile, LO + rows - DEPTH : LO + rows, :]
            near_ref[index, :, pl.ds(tile * DEPTH, DEPTH), :] = jnp.where(first, tail, head)


def pack(blocks_of, lane):
    lanes = lane_ids()
    total = None
    for layer, value in enumerate(blocks_of):
        moved = turn(value, layer * DEPTH - lane)
        total = moved if total is None else jnp.where(lanes // DEPTH == layer, moved, total)
    return total


def own_kernel(
    log_ref,
    fields_in,
    fields_ref,
    inverse_ref,
    face_x_ref,
    face_y_ref,
    face_z_ref,
    last_ref,
    first_ref,
):
    del fields_in
    layers, tiles, height, _ = log_ref.shape
    rows = height - 3 * SUB
    blocks = rows // SUB
    slots = layers // (LANES // GROUP)
    ring = LO + rows + SUB
    last_lane = lane_ids() == LANES - 1
    base_ref = fields_ref.at[0]

    def at(block, step=0):
        return pl.ds(LO + block * SUB + step, SUB)

    def fill(layer, _):
        for tile in range(tiles):
            for block in range(blocks):
                value = 0.5 * jnp.exp(-log_ref[layer, tile, at(block), :])
                inverse_ref[layer, tile, at(block), :] = value
                if block == 0:
                    inverse_ref[layer, tile, pl.ds(ring, 1), :] = value[0:1]
        return 0

    lax.fori_loop(0, layers, fill, 0, unroll=slots)

    zero = jnp.zeros((SUB, LANES), F32)
    for tile in range(tiles):
        for block in range(blocks + 1):
            face_z_ref[0, tile, at(block), :] = zero
            face_z_ref[layers, tile, at(block), :] = zero

    def faces(layer, _):
        for block in range(blocks):
            values = [inverse_ref[layer, tile, at(block), :] for tile in range(tiles)]
            moved = [turn(value, -1) for value in values]
            for tile in range(tiles):
                other = moved[tile]
                if tile < tiles - 1:
                    other = jnp.where(last_lane, moved[tile + 1], other)
                face = reciprocal(values[tile] + other)
                face_y_ref[layer, tile, at(block), :] = face if tile < tiles - 1 else jnp.where(last_lane, 0.0, face)
                face_x_ref[layer, tile, at(block), :] = reciprocal(
                    values[tile] + inverse_ref[layer, tile, at(block, 1), :]
                )
        return 0

    lax.fori_loop(0, layers, faces, 0, unroll=slots)

    def faces_z(layer, _):
        for tile in range(tiles):
            for block in range(blocks):
                face_z_ref[layer, tile, at(block), :] = reciprocal(
                    inverse_ref[layer - 1, tile, at(block), :] + inverse_ref[layer, tile, at(block), :]
                )
        return 0

    lax.fori_loop(1, layers, faces_z, 0, unroll=slots)

    base_ref[:, :, pl.ds(ring, 1), :] = base_ref[:, :, pl.ds(LO, 1), :]
    for index, ref in enumerate((log_ref, base_ref)):
        for block in range(blocks):
            part = pl.ds(block * SUB, SUB)
            last_ref[index, part, :] = pack(
                [ref[layer, tiles - 1, at(block), :] for layer in range(layers)], LANES - DEPTH
            )
            first_ref[index, part, :] = pack([ref[layer, 0, at(block), :] for layer in range(layers)], 0)


def edge_kernel(far_in, near_in, last_in, first_in, last_ref, first_ref, near_ref, far_ref, halo_ref):
    del last_in, first_in
    _, layers, tiles, _, _ = halo_ref.shape
    height = last_ref.shape[1]
    one, two = even("gx"), even("gy")
    for tile in range(tiles):
        part = pl.ds(tile * DEPTH, DEPTH)
        near, far = near_in[:, :, part, :], far_in[:, :, part, :]
        halo_ref[:, :, tile, 0:DEPTH, :] = jnp.where(one, near, far)
        halo_ref[:, :, tile, DEPTH:SUB, :] = jnp.where(one, far, near)
    for index in range(2):
        part = pl.ds(height - SUB, SUB)
        last_ref[index, part, :] = pack(
            [halo_ref[index, layer, tiles - 1] for layer in range(layers)], LANES - DEPTH
        )
        first_ref[index, part, :] = pack([halo_ref[index, layer, 0] for layer in range(layers)], 0)
    near_ref[...] = jnp.where(two, last_ref[...], first_ref[...])
    far_ref[...] = jnp.where(two, first_ref[...], last_ref[...])


def place_of(block, step=0):
    return pl.ds(LO + block * SUB + step, SUB)


def close_ring(ref, index, block, blocks, value):
    ring = LO + (blocks + 1) * SUB
    if block == 0:
        ref[(*index, pl.ds(ring, 1), slice(None))] = value[0:1]
    if block == blocks:
        ref[(*index, pl.ds(LO - 1, 1), slice(None))] = value[SUB - 1 : SUB]


def rim_of(values, group):
    return pltpu.roll(values, LANES - 1 - DEPTH - group * GROUP, 1)


def x_part(face_ref, index, old, old_index, block, value):
    there = old[(*old_index, place_of(block, 1), slice(None))]
    back = old[(*old_index, place_of(block, -1), slice(None))]
    return face_ref[(*index, place_of(block), slice(None))] * (value - there) - face_ref[
        (*index, place_of(block, -1), slice(None))
    ] * (back - value)


def inside_masks():
    here_x, here_y = lax.axis_index("gx"), lax.axis_index("gy")
    past_x, before_x = here_x < lax.axis_size("gx") - 1, here_x > 0
    past_y, before_y = here_y < lax.axis_size("gy") - 1, here_y > 0
    place = lane_ids() % GROUP
    inside_rows = jnp.where(row_ids() < DEPTH, past_x.astype(jnp.int32), before_x.astype(jnp.int32)) > 0
    inside_cols = (
        jnp.where(
            (place >= DEPTH) & (place < 2 * DEPTH),
            past_y.astype(jnp.int32),
            jnp.where((place >= 2 * DEPTH) & (place < 3 * DEPTH), before_y.astype(jnp.int32), 1),
        )
        > 0
    )
    return inside_rows, inside_cols


def apply_power(number, fields_ref, face_x_ref, face_y_ref, face_z_ref, rims_ref):
    _, layers, tiles, height, _ = fields_ref.shape
    blocks = (height - 3 * SUB) // SUB
    slots = layers // (LANES // GROUP)
    groups = layers // slots
    old, new = fields_ref.at[number - 1], fields_ref.at[number]
    lanes = lane_ids()
    first_lane, last_lane = lanes == 0, lanes == LANES - 1
    inside_rows, _ = inside_masks()
    at = place_of

    def layer_range(start, count, block):
        levels = []
        for step in range(-1, count + 1):
            layer = start + step
            if step < 0:
                layer = jnp.maximum(layer, 0)
            if step == count:
                layer = jnp.minimum(layer, layers - 1)
            levels.append([old[layer, tile, at(block), :] for tile in range(tiles)])
        ups = [
            [
                face_z_ref[start + step, tile, at(block), :] * (levels[step][tile] - levels[step + 1][tile])
                for tile in range(tiles)
            ]
            for step in range(count + 1)
        ]
        for step in range(count):
            layer = start + step
            values = levels[step + 1]
            moved = [turn(value, -1) for value in values]
            flux = []
            for tile in range(tiles):
                other = moved[tile]
                if tile < tiles - 1:
                    other = jnp.where(last_lane, moved[tile + 1], other)
                flux.append(face_y_ref[layer, tile, at(block), :] * (values[tile] - other))
            rim = None
            if rims_ref is not None:
                rim = rim_of(rims_ref[number - 1, step % slots, at(block), :], start // slots + step // slots)
            moved = [turn(value, 1) for value in flux]
            moved = [moved[-1] if rim is None else rim] + moved
            if rim is not None:
                flux[-1] = jnp.where(last_lane, rim, flux[-1])
            for tile in range(tiles):
                value = values[tile]
                result = (
                    (flux[tile] - jnp.where(first_lane, moved[tile], moved[tile + 1]))
                    + x_part(face_x_ref, (layer, tile), old, (layer, tile), block, value)
                    + (ups[step + 1][tile] - ups[step][tile])
                )
                if block == blocks:
                    result = jnp.where(inside_rows, result, 0.0)
                new[layer, tile, at(block), :] = result
                if number < DEPTH:
                    close_ring(new, (layer, tile), block, blocks, result)
                yield tile, value, result

    def chunk(group, sums):
        own_sums, next_sums = list(sums[0]), list(sums[1])
        for block in range(blocks):
            for tile, value, result in layer_range(group * slots, slots, block):
                own_sums[tile] = own_sums[tile] + value * value
                next_sums[tile] = next_sums[tile] + value * result
        return tuple(own_sums), tuple(next_sums)

    def halo_chunk(part, _):
        for _ in layer_range(part * HALO_LAYERS, HALO_LAYERS, blocks):
            pass
        return 0

    start = (jnp.zeros((SUB, LANES), F32),) * tiles
    sums = lax.fori_loop(0, groups, chunk, (start, start), unroll=2)
    if number < DEPTH:
        lax.fori_loop(0, layers // HALO_LAYERS, halo_chunk, 0)
    return [functools.reduce(jnp.add, parts) for parts in sums]


def first_kernel(
    halo_ref,
    fields_in,
    inverse_in,
    face_x_in,
    face_y_in,
    face_z_in,
    fields_ref,
    inverse_ref,
    face_x_ref,
    face_y_ref,
    face_z_ref,
    parts_ref,
):
    del fields_in, inverse_in, face_x_in, face_y_in, face_z_in
    _, layers, tiles, height, _ = fields_ref.shape
    blocks = (height - 3 * SUB) // SUB
    slots = layers // (LANES // GROUP)
    last_lane = lane_ids() == LANES - 1
    at = place_of

    def fill(layer, _):
        for tile in range(tiles):
            source = halo_ref[1, layer, tile]
            fields_ref[0, layer, tile, at(blocks), :] = source
            close_ring(fields_ref, (0, layer, tile), blocks, blocks, source)
            inverse_ref[layer, tile, at(blocks), :] = 0.5 * jnp.exp(-halo_ref[0, layer, tile])
        return 0

    lax.fori_loop(0, layers, fill, 0, unroll=2 * slots)

    def faces(layer, _):
        values = [inverse_ref[layer, tile, at(blocks), :] for tile in range(tiles)]
        moved = [turn(value, -1) for value in values]
        for tile in range(tiles):
            other = moved[tile]
            if tile < tiles - 1:
                other = jnp.where(last_lane, moved[tile + 1], other)
            face = reciprocal(values[tile] + other)
            face_y_ref[layer, tile, at(blocks), :] = face if tile < tiles - 1 else jnp.where(last_lane, 0.0, face)
            for block in (blocks - 1, blocks):
                face = reciprocal(
                    inverse_ref[layer, tile, at(block), :] + inverse_ref[layer, tile, at(block, 1), :]
                )
                face_x_ref[layer, tile, at(block), :] = face
                close_ring(face_x_ref, (layer, tile), block, blocks, face)
            before = inverse_ref[jnp.maximum(layer - 1, 0), tile, at(blocks), :]
            face_z_ref[layer, tile, at(blocks), :] = jnp.where(layer > 0, reciprocal(before + values[tile]), 0.0)
        return 0

    lax.fori_loop(0, layers, faces, 0, unroll=2 * slots)
    found = apply_power(1, fields_ref, face_x_ref, face_y_ref, face_z_ref, None)
    for which, part in enumerate(found):
        parts_ref[which] = part


def basis_kernel(
    last_ref,
    first_ref,
    far_ref,
    near_ref,
    parts_ref,
    face_x_ref,
    face_y_ref,
    face_z_ref,
    fields_in,
    fields_ref,
    rims_ref,
    sums_ref,
    strip_ref,
    strip_inv_ref,
    strip_x_ref,
    strip_y_ref,
    strip_z_ref,
):
    del fields_in
    _, layers, tiles, height, _ = fields_ref.shape
    rows = height - 3 * SUB
    slots = layers // (LANES // GROUP)
    groups = layers // slots
    blocks = rows // SUB
    lanes = lane_ids()
    place = lanes % GROUP
    inside_rows, inside_cols = inside_masks()
    inside_both = inside_rows & inside_cols
    first_lane, last_lane = lanes == 0, lanes == LANES - 1
    first_y = even("gy")
    at = place_of

    def spread(index, block):
        part = pl.ds(block * SUB, SUB)
        near, far = near_ref[index, part, :], far_ref[index, part, :]
        packed = (
            last_ref[index, part, :],
            jnp.where(first_y, near, far),
            jnp.where(first_y, far, near),
            first_ref[index, part, :],
        )
        found = []
        for slot in range(slots):
            moved = [turn(value, (kind - slot) * DEPTH) for kind, value in enumerate(packed)]
            found.append(
                jnp.where(
                    place < 2 * DEPTH,
                    jnp.where(place < DEPTH, moved[0], moved[1]),
                    jnp.where(place < 3 * DEPTH, moved[2], moved[3]),
                )
            )
        return found

    def put_strip(ref, block, values):
        ref[0, at(block), :] = turn(values[-1], GROUP)
        ref[slots + 1, at(block), :] = turn(values[0], -GROUP)
        for slot, value in enumerate(values):
            ref[slot + 1, at(block), :] = value
            close_ring(ref, (slot + 1,), block, blocks, value)

    for block in range(blocks + 1):
        put_strip(strip_ref.at[0], block, spread(1, block))
        values = [0.5 * jnp.exp(-value) for value in spread(0, block)]
        put_strip(strip_inv_ref, block, values)
    top, bottom = lanes >= LANES - GROUP, lanes < GROUP
    for block in range(blocks + 1):
        for slot in range(1, slots + 1):
            value = strip_inv_ref[slot, at(block), :]
            face = reciprocal(value + strip_inv_ref[slot, at(block, 1), :])
            strip_x_ref[slot - 1, at(block), :] = face
            close_ring(strip_x_ref, (slot - 1,), block, blocks, face)
            strip_y_ref[slot - 1, at(block), :] = reciprocal(value + turn(value, -1))
        for slot in range(slots + 1):
            face = reciprocal(strip_inv_ref[slot, at(block), :] + strip_inv_ref[slot + 1, at(block), :])
            if slot == 0:
                face = jnp.where(bottom, 0.0, face)
            if slot == slots:
                face = jnp.where(top, 0.0, face)
            strip_z_ref[slot, at(block), :] = face

    for power in range(1, DEPTH + 1):
        old = strip_ref.at[power - 1]
        for block in range(blocks + 1):
            levels = [old[slot, at(block), :] for slot in range(slots + 2)]
            ups = [
                strip_z_ref[slot, at(block), :] * (levels[slot] - levels[slot + 1]) for slot in range(slots + 1)
            ]
            values = []
            for slot in range(slots):
                value = levels[slot + 1]
                flux = strip_y_ref[slot, at(block), :] * (value - turn(value, -1))
                after = turn(flux, 1)
                rims_ref[power - 1, slot, at(block), :] = jnp.where(
                    place == DEPTH, after, turn(flux, 2 - 2 * DEPTH)
                )
                if power < DEPTH:
                    result = (
                        (flux - after)
                        + x_part(strip_x_ref, (slot,), old, (slot + 1,), block, value)
                        + (ups[slot + 1] - ups[slot])
                    )
                    values.append(jnp.where(inside_both if block == blocks else inside_cols, result, 0.0))
            if power < DEPTH:
                put_strip(strip_ref.at[power], block, values)

    zero = jnp.zeros((SUB, LANES), F32)

    def complete(group, lost):
        for slot in range(slots):
            layer = group * slots + slot
            for block in range(blocks + 1):
                rim = rim_of(rims_ref[0, slot, at(block), :], group)
                for tile, part in ((0, jnp.where(first_lane, -rim, 0.0)), (tiles - 1, jnp.where(last_lane, rim, 0.0))):
                    value = fields_ref[1, layer, tile, at(block), :] + part
                    fields_ref[1, layer, tile, at(block), :] = value
                    close_ring(fields_ref, (1, layer, tile), block, blocks, value)
                    if block < blocks:
                        lost = lost + part * fields_ref[0, layer, tile, at(block), :]
        return lost

    lost = lax.fori_loop(0, groups, complete, zero, unroll=4)

    found = [parts_ref[0], parts_ref[1] + lost]
    for number in range(2, DEPTH + 1):
        found += apply_power(number, fields_ref, face_x_ref, face_y_ref, face_z_ref, rims_ref)
    total = jnp.concatenate([jnp.sum(part, axis=0, keepdims=True) for part in found], axis=0)
    share = LANES // SUB
    step = LANES // 2
    while step >= share:
        total = total + turn(total, step)
        step //= 2
    total = jnp.sum(jnp.where(lanes // share == row_ids(), total, 0.0), axis=0, keepdims=True)
    sums_ref[...] = jnp.broadcast_to(total, sums_ref.shape)


def two_sum(first, second):
    total = first + second
    part = total - first
    return total, (first - (total - part)) + (second - part)


def quick_sum(first, second):
    total = first + second
    return total, second - (total - first)


def halves(value):
    scaled = 4097.0 * value
    high = scaled - (scaled - value)
    return high, value - high


def two_product(first, second):
    total = first * second
    first_high, first_low = halves(first)
    second_high, second_low = halves(second)
    rest = ((first_high * second_high - total) + first_high * second_low + first_low * second_high) + (
        first_low * second_low
    )
    return total, rest


def pair_add(first, second):
    total, rest = two_sum(first[0], second[0])
    return quick_sum(total, rest + (first[1] + second[1]))


def pair_sub(first, second):
    return pair_add(first, (-second[0], -second[1]))


def pair_mul(first, second):
    total, rest = two_product(first[0], second[0])
    return quick_sum(total, rest + (first[0] * second[1] + first[1] * second[0]))


def pair_div(first, second):
    guess = first[0] / second[0]
    total, rest = two_product(guess, second[0])
    left = ((first[0] - total) - rest) + (first[1] - guess * second[1])
    return quick_sum(guess, left / second[0])


def galerkin(moments):
    count = DEPTH
    matrix = {(i, j): moments[i + j + 1] for i in range(count) for j in range(i + 1)}
    right = [moments[i] for i in range(count)]
    for pivot in range(count):
        for i in range(pivot + 1, count):
            ratio = pair_div(matrix[i, pivot], matrix[pivot, pivot])
            for j in range(pivot + 1, i + 1):
                matrix[i, j] = pair_sub(matrix[i, j], pair_mul(ratio, matrix[j, pivot]))
            right[i] = pair_sub(right[i], pair_mul(ratio, right[pivot]))
    found = [None] * count
    for i in reversed(range(count)):
        value = right[i]
        for j in range(i + 1, count):
            value = pair_sub(value, pair_mul(matrix[j, i], found[j]))
        found[i] = pair_div(value, matrix[i, i])
    return [value[0] for value in found]


def finish_kernel(
    sums_ref,
    fields_ref,
    face_x_ref,
    face_y_ref,
    rims_ref,
    pressure_hbm,
    residual_hbm,
    east_hbm,
    north_hbm,
    pressure_ref,
    residual_ref,
    east_ref,
    north_ref,
    field_ref,
    sems,
):
    _, layers, tiles, height, _ = fields_ref.shape
    rows = height - 3 * SUB
    slots = layers // (LANES // GROUP)
    blocks = rows // SUB
    last_lane = lane_ids() == LANES - 1

    total = jnp.sum(sums_ref[...], axis=0, keepdims=True)
    total = jnp.where(lane_ids() // (LANES // SUB) == row_ids(), total, 0.0)
    rest = jnp.zeros((SUB, LANES), F32)
    step = 1
    while step < LANES:
        total, lost = two_sum(total, turn(total, step))
        rest = rest + turn(rest, step) + lost
        step *= 2
    total, rest = quick_sum(total, rest)
    coefs = galerkin([(total[k : k + 1], rest[k : k + 1]) for k in range(2 * DEPTH)])
    coefs = [jnp.broadcast_to(value, (SUB, LANES)) for value in coefs]

    def at(block, step=0):
        return pl.ds(LO + block * SUB + step, SUB)

    def mix(values):
        return functools.reduce(jnp.add, [coef * value for coef, value in zip(coefs, values, strict=True)])

    outs = (
        (pressure_ref, pressure_hbm),
        (residual_ref, residual_hbm),
        (east_ref, east_hbm),
        (north_ref, north_hbm),
    )

    def copies(group):
        part = pl.ds(group * slots, slots)
        return [
            pltpu.make_async_copy(ref.at[part], hbm.at[0, part], sems.at[index, group])
            for index, (ref, hbm) in enumerate(outs)
        ]

    def chunk(group, _):
        for slot in range(slots):
            layer = group * slots + slot
            for block in range(blocks + 1):
                values = []
                for tile in range(tiles):
                    found = [
                        fields_ref[power, layer, tile, at(block), :] for power in range(DEPTH + (block < blocks))
                    ]
                    value = mix(found[:DEPTH])
                    values.append(value)
                    field_ref[tile, at(block), :] = value
                    if block < blocks:
                        spot = (layer, pl.ds(block * SUB, SUB), pl.ds(tile * LANES, LANES))
                        pressure_ref[spot] = value
                        residual_ref[spot] = found[0] - mix(found[1:])
                if block < blocks:
                    rim = mix([rims_ref[power, slot, at(block), :] for power in range(DEPTH)])
                    rim = rim_of(rim, group)
                    moved = [turn(value, -1) for value in values]
                    for tile in range(tiles):
                        other = moved[tile]
                        if tile < tiles - 1:
                            other = jnp.where(last_lane, moved[tile + 1], other)
                        flux = face_y_ref[layer, tile, at(block), :] * (values[tile] - other)
                        if tile == tiles - 1:
                            flux = jnp.where(last_lane, rim, flux)
                        spot = (layer, pl.ds(block * SUB, SUB), pl.ds(tile * LANES, LANES))
                        north_ref[spot] = flux
            for block in range(blocks):
                for tile in range(tiles):
                    spot = (layer, pl.ds(block * SUB, SUB), pl.ds(tile * LANES, LANES))
                    east_ref[spot] = face_x_ref[layer, tile, at(block), :] * (
                        field_ref[tile, at(block), :] - field_ref[tile, at(block, 1), :]
                    )
        for copy in copies(group):
            copy.start()
        return 0

    lax.fori_loop(0, layers // slots, chunk, 0)

    def drain(group, _):
        for copy in copies(group):
            copy.wait()
        return 0

    lax.fori_loop(0, layers // slots, drain, 0)


def exchange(value, axis, near):
    count = lax.axis_size(axis)
    pairs = []
    for i in range(count):
        other = i + 1 if (i % 2 == 0) == near else i - 1
        if 0 <= other < count:
            pairs.append((i, other))
    return lax.ppermute(value, axis, pairs)


def on_device(log_perm, source):
    _, layers, rows, cols = log_perm.shape
    tiles, slots = cols // LANES, layers // (LANES // GROUP)
    height = rows + 3 * SUB
    full = (layers, tiles, height, LANES)
    deep = (layers + 1, tiles, height, LANES)
    ends = (2, layers, tiles * DEPTH, LANES)
    edges = (2, rows + SUB, LANES)
    strip = (slots + 2, height, LANES)
    inner = (slots, height, LANES)
    peers = lax.axis_size("gx") * lax.axis_size("gy")
    cells = layers * rows * cols

    log_perm, source = (pltpu.with_memory_space_constraint(value, pltpu.HBM) for value in (log_perm, source))
    powers = (in_vmem(DEPTH + 1, *full), in_vmem(*deep)) + (in_vmem(*full),) * 2 + (in_vmem(*deep),)
    far = pl.pallas_call(
        far_kernel,
        out_shape=in_vmem(*ends),
        in_specs=[HBM_SPEC] * 2,
        out_specs=VMEM_SPEC,
        scratch_shapes=[in_vmem(2, tiles, layers, SUB, LANES), pltpu.SemaphoreType.DMA((2, tiles))],
        compiler_params=params(16),
        name="far",
    )(log_perm, source)
    far = exchange(far, "gx", False)
    log_own, fields, near = pl.pallas_call(
        load_kernel,
        out_shape=(in_vmem(*full), powers[0], in_vmem(*ends)),
        in_specs=[HBM_SPEC] * 2,
        out_specs=[VMEM_SPEC] * 3,
        scratch_shapes=[pltpu.SemaphoreType.DMA((2, tiles))],
        compiler_params=params(16),
        cost_estimate=pl.CostEstimate(flops=cells, bytes_accessed=8 * cells, transcendentals=0),
        name="load",
    )(log_perm, source)
    near = exchange(near, "gx", True)
    *fields, last, first = pl.pallas_call(
        own_kernel,
        out_shape=powers + (in_vmem(*edges),) * 2,
        in_specs=[VMEM_SPEC] * 2,
        out_specs=[VMEM_SPEC] * 7,
        input_output_aliases={1: 0},
        compiler_params=params(16),
        cost_estimate=pl.CostEstimate(flops=60 * cells, bytes_accessed=8 * cells, transcendentals=4 * cells),
        name="own",
    )(log_own, fields)
    last, first, near, far, halo = pl.pallas_call(
        edge_kernel,
        out_shape=(in_vmem(*edges),) * 4 + (in_vmem(2, layers, tiles, SUB, LANES),),
        in_specs=[VMEM_SPEC] * 4,
        out_specs=[VMEM_SPEC] * 5,
        input_output_aliases={2: 0, 3: 1},
        compiler_params=params(16),
        name="edges",
    )(far, near, last, first)
    far = exchange(far, "gy", False)
    near = exchange(near, "gy", True)
    fields, _, face_x, face_y, face_z, parts = pl.pallas_call(
        first_kernel,
        out_shape=powers + (in_vmem(2, SUB, LANES),),
        in_specs=[VMEM_SPEC] * 6,
        out_specs=[VMEM_SPEC] * 6,
        input_output_aliases={1: 0, 2: 1, 3: 2, 4: 3, 5: 4},
        compiler_params=params(16),
        cost_estimate=pl.CostEstimate(flops=40 * cells, bytes_accessed=8 * cells, transcendentals=cells),
        name="first",
    )(halo, *fields)
    fields, rims, sums = pl.pallas_call(
        basis_kernel,
        out_shape=(powers[0], in_vmem(DEPTH, *inner), in_vmem(peers, LANES)),
        in_specs=[VMEM_SPEC] * 9,
        out_specs=[VMEM_SPEC] * 3,
        input_output_aliases={8: 0},
        scratch_shapes=[
            in_vmem(DEPTH, *strip),
            in_vmem(*strip),
            in_vmem(*inner),
            in_vmem(*inner),
            in_vmem(slots + 1, height, LANES),
        ],
        compiler_params=params(16),
        name="basis",
    )(last, first, far, near, parts, face_x, face_y, face_z, fields)
    sums = lax.all_to_all(sums, ("gx", "gy"), 0, 0, tiled=True)
    block = (layers, rows, cols)
    return pl.pallas_call(
        finish_kernel,
        out_shape=(jax.ShapeDtypeStruct((1, *block), F32),) * 4,
        in_specs=[VMEM_SPEC] * 5,
        out_specs=[ANY_SPEC] * 4,
        scratch_shapes=[in_vmem(*block)] * 4
        + [in_vmem(tiles, height, LANES), pltpu.SemaphoreType.DMA((4, layers // slots))],
        compiler_params=params(16),
        name="finish",
    )(sums, fields, face_x, face_y, rims)


def solution(mesh):
    spec = P(None, None, "gx", "gy")
    return jax.shard_map(on_device, mesh=mesh, in_specs=(spec,) * 2, out_specs=(spec,) * 4, check_vma=False)
```

```python
import functools

import jax
import jax.numpy as jnp
from jax import lax
from jax.experimental import pallas as pl
from jax.experimental.pallas import tpu as pltpu
from jax.sharding import PartitionSpec as P

DEPTH = 4
LANES = 128
SUB = 8
LO = 8
GROUP = 4 * DEPTH
HALO_LAYERS = 16
F32 = jnp.float32
HBM_SPEC = pl.BlockSpec(memory_space=pltpu.HBM)
VMEM_SPEC = pl.BlockSpec(memory_space=pltpu.VMEM)
ANY_SPEC = pl.BlockSpec(memory_space=pl.ANY)


def in_vmem(*shape):
    return pltpu.VMEM(shape, F32)


def params(limit):
    return pltpu.CompilerParams(vmem_limit_bytes=limit * 1024 * 1024)


def lane_ids():
    return lax.broadcasted_iota(jnp.int32, (SUB, LANES), 1)


def row_ids():
    return lax.broadcasted_iota(jnp.int32, (SUB, LANES), 0)


def turn(value, shift):
    return pltpu.roll(value, shift % LANES, 1) if shift % LANES else value


def reciprocal(value):
    return 1.0 / value


def even(axis):
    return lax.rem(lax.axis_index(axis), 2) == 0


def far_kernel(log_hbm, src_hbm, far_ref, rows_ref, sems):
    _, _, rows, cols = log_hbm.shape
    first = even("gx")
    start = pl.multiple_of(jnp.where(first, 0, rows - SUB), SUB)
    copies = []
    for index, hbm in enumerate((log_hbm, src_hbm)):
        for tile in range(cols // LANES):
            copies.append(
                pltpu.make_async_copy(
                    hbm.at[0, :, pl.ds(start, SUB), pl.ds(tile * LANES, LANES)],
                    rows_ref.at[index, tile],
                    sems.at[index, tile],
                )
            )
            copies[-1].start()
    for copy in copies:
        copy.wait()
    for tile in range(cols // LANES):
        head = rows_ref[:, tile, :, 0:DEPTH, :]
        tail = rows_ref[:, tile, :, SUB - DEPTH : SUB, :]
        far_ref[:, :, pl.ds(tile * DEPTH, DEPTH), :] = jnp.where(first, head, tail)


def load_kernel(log_hbm, src_hbm, log_ref, fields_ref, near_ref, sems):
    _, _, rows, cols = log_hbm.shape
    tiles = cols // LANES
    first = even("gx")
    copies = []
    refs = (log_ref, fields_ref.at[0])
    for index, (hbm, ref) in enumerate(zip((log_hbm, src_hbm), refs, strict=True)):
        for tile in range(tiles):
            copies.append(
                pltpu.make_async_copy(
                    hbm.at[0, :, :, pl.ds(tile * LANES, LANES)],
                    ref.at[:, tile, pl.ds(LO, rows), :],
                    sems.at[index, tile],
                )
            )
            copies[-1].start()
    for copy in copies:
        copy.wait()
    for index, ref in enumerate(refs):
        for tile in range(tiles):
            head = ref[:, tile, LO : LO + DEPTH, :]
            tail = ref[:, tile, LO + rows - DEPTH : LO + rows, :]
            near_ref[index, :, pl.ds(tile * DEPTH, DEPTH), :] = jnp.where(first, tail, head)


def pack(blocks_of, lane):
    lanes = lane_ids()
    total = None
    for layer, value in enumerate(blocks_of):
        moved = turn(value, layer * DEPTH - lane)
        total = moved if total is None else jnp.where(lanes // DEPTH == layer, moved, total)
    return total


def own_kernel(
    log_ref,
    fields_in,
    fields_ref,
    inverse_ref,
    face_x_ref,
    face_y_ref,
    face_z_ref,
    last_ref,
    first_ref,
):
    del fields_in
    layers, tiles, height, _ = log_ref.shape
    rows = height - 3 * SUB
    blocks = rows // SUB
    slots = layers // (LANES // GROUP)
    ring = LO + rows + SUB
    last_lane = lane_ids() == LANES - 1
    base_ref = fields_ref.at[0]

    def at(block, step=0):
        return pl.ds(LO + block * SUB + step, SUB)

    def fill(layer, _):
        for tile in range(tiles):
            for block in range(blocks):
                value = 0.5 * jnp.exp(-log_ref[layer, tile, at(block), :])
                inverse_ref[layer, tile, at(block), :] = value
                if block == 0:
                    inverse_ref[layer, tile, pl.ds(ring, 1), :] = value[0:1]
        return 0

    lax.fori_loop(0, layers, fill, 0, unroll=slots)

    zero = jnp.zeros((SUB, LANES), F32)
    for tile in range(tiles):
        for block in range(blocks + 1):
            face_z_ref[0, tile, at(block), :] = zero
            face_z_ref[layers, tile, at(block), :] = zero

    def faces(layer, _):
        for block in range(blocks):
            values = [inverse_ref[layer, tile, at(block), :] for tile in range(tiles)]
            moved = [turn(value, -1) for value in values]
            for tile in range(tiles):
                other = moved[tile]
                if tile < tiles - 1:
                    other = jnp.where(last_lane, moved[tile + 1], other)
                face = reciprocal(values[tile] + other)
                face_y_ref[layer, tile, at(block), :] = face if tile < tiles - 1 else jnp.where(last_lane, 0.0, face)
                face_x_ref[layer, tile, at(block), :] = reciprocal(
                    values[tile] + inverse_ref[layer, tile, at(block, 1), :]
                )
        return 0

    lax.fori_loop(0, layers, faces, 0, unroll=slots)

    def faces_z(layer, _):
        for tile in range(tiles):
            for block in range(blocks):
                face_z_ref[layer, tile, at(block), :] = reciprocal(
                    inverse_ref[layer - 1, tile, at(block), :] + inverse_ref[layer, tile, at(block), :]
                )
        return 0

    lax.fori_loop(1, layers, faces_z, 0, unroll=slots)

    base_ref[:, :, pl.ds(ring, 1), :] = base_ref[:, :, pl.ds(LO, 1), :]
    for index, ref in enumerate((log_ref, base_ref)):
        for block in range(blocks):
            part = pl.ds(block * SUB, SUB)
            last_ref[index, part, :] = pack(
                [ref[layer, tiles - 1, at(block), :] for layer in range(layers)], LANES - DEPTH
            )
            first_ref[index, part, :] = pack([ref[layer, 0, at(block), :] for layer in range(layers)], 0)


def edge_kernel(far_in, near_in, last_in, first_in, last_ref, first_ref, near_ref, far_ref, halo_ref):
    del last_in, first_in
    _, layers, tiles, _, _ = halo_ref.shape
    height = last_ref.shape[1]
    one, two = even("gx"), even("gy")
    for tile in range(tiles):
        part = pl.ds(tile * DEPTH, DEPTH)
        near, far = near_in[:, :, part, :], far_in[:, :, part, :]
        halo_ref[:, :, tile, 0:DEPTH, :] = jnp.where(one, near, far)
        halo_ref[:, :, tile, DEPTH:SUB, :] = jnp.where(one, far, near)
    for index in range(2):
        part = pl.ds(height - SUB, SUB)
        last_ref[index, part, :] = pack(
            [halo_ref[index, layer, tiles - 1] for layer in range(layers)], LANES - DEPTH
        )
        first_ref[index, part, :] = pack([halo_ref[index, layer, 0] for layer in range(layers)], 0)
    near_ref[...] = jnp.where(two, last_ref[...], first_ref[...])
    far_ref[...] = jnp.where(two, first_ref[...], last_ref[...])


def place_of(block, step=0):
    return pl.ds(LO + block * SUB + step, SUB)


def close_ring(ref, index, block, blocks, value):
    ring = LO + (blocks + 1) * SUB
    if block == 0:
        ref[(*index, pl.ds(ring, 1), slice(None))] = value[0:1]
    if block == blocks:
        ref[(*index, pl.ds(LO - 1, 1), slice(None))] = value[SUB - 1 : SUB]


def rim_of(values, group):
    return pltpu.roll(values, LANES - 1 - DEPTH - group * GROUP, 1)


def x_part(face_ref, index, old, old_index, block, value):
    there = old[(*old_index, place_of(block, 1), slice(None))]
    back = old[(*old_index, place_of(block, -1), slice(None))]
    return face_ref[(*index, place_of(block), slice(None))] * (value - there) - face_ref[
        (*index, place_of(block, -1), slice(None))
    ] * (back - value)


def inside_masks():
    here_x, here_y = lax.axis_index("gx"), lax.axis_index("gy")
    past_x, before_x = here_x < lax.axis_size("gx") - 1, here_x > 0
    past_y, before_y = here_y < lax.axis_size("gy") - 1, here_y > 0
    place = lane_ids() % GROUP
    inside_rows = jnp.where(row_ids() < DEPTH, past_x.astype(jnp.int32), before_x.astype(jnp.int32)) > 0
    inside_cols = (
        jnp.where(
            (place >= DEPTH) & (place < 2 * DEPTH),
            past_y.astype(jnp.int32),
            jnp.where((place >= 2 * DEPTH) & (place < 3 * DEPTH), before_y.astype(jnp.int32), 1),
        )
        > 0
    )
    return inside_rows, inside_cols


def apply_power(number, fields_ref, face_x_ref, face_y_ref, face_z_ref, rims_ref):
    _, layers, tiles, height, _ = fields_ref.shape
    blocks = (height - 3 * SUB) // SUB
    slots = layers // (LANES // GROUP)
    groups = layers // slots
    old, new = fields_ref.at[number - 1], fields_ref.at[number]
    lanes = lane_ids()
    first_lane, last_lane = lanes == 0, lanes == LANES - 1
    inside_rows, _ = inside_masks()
    at = place_of

    def layer_range(start, count, block):
        levels = []
        for step in range(-1, count + 1):
            layer = start + step
            if step < 0:
                layer = jnp.maximum(layer, 0)
            if step == count:
                layer = jnp.minimum(layer, layers - 1)
            levels.append([old[layer, tile, at(block), :] for tile in range(tiles)])
        ups = [
            [
                face_z_ref[start + step, tile, at(block), :] * (levels[step][tile] - levels[step + 1][tile])
                for tile in range(tiles)
            ]
            for step in range(count + 1)
        ]
        for step in range(count):
            layer = start + step
            values = levels[step + 1]
            moved = [turn(value, -1) for value in values]
            flux = []
            for tile in range(tiles):
                other = moved[tile]
                if tile < tiles - 1:
                    other = jnp.where(last_lane, moved[tile + 1], other)
                flux.append(face_y_ref[layer, tile, at(block), :] * (values[tile] - other))
            rim = None
            if rims_ref is not None:
                rim = rim_of(rims_ref[number - 1, step % slots, at(block), :], start // slots + step // slots)
            moved = [turn(value, 1) for value in flux]
            moved = [moved[-1] if rim is None else rim] + moved
            if rim is not None:
                flux[-1] = jnp.where(last_lane, rim, flux[-1])
            for tile in range(tiles):
                value = values[tile]
                result = (
                    (flux[tile] - jnp.where(first_lane, moved[tile], moved[tile + 1]))
                    + x_part(face_x_ref, (layer, tile), old, (layer, tile), block, value)
                    + (ups[step + 1][tile] - ups[step][tile])
                )
                if block == blocks:
                    result = jnp.where(inside_rows, result, 0.0)
                new[layer, tile, at(block), :] = result
                if number < DEPTH:
                    close_ring(new, (layer, tile), block, blocks, result)
                yield tile, value, result

    def chunk(group, sums):
        own_sums, next_sums = list(sums[0]), list(sums[1])
        for block in range(blocks):
            for tile, value, result in layer_range(group * slots, slots, block):
                own_sums[tile] = own_sums[tile] + value * value
                next_sums[tile] = next_sums[tile] + value * result
        return tuple(own_sums), tuple(next_sums)

    def halo_chunk(part, _):
        for _ in layer_range(part * HALO_LAYERS, HALO_LAYERS, blocks):
            pass
        return 0

    start = (jnp.zeros((SUB, LANES), F32),) * tiles
    sums = lax.fori_loop(0, groups, chunk, (start, start), unroll=2)
    if number < DEPTH:
        lax.fori_loop(0, layers // HALO_LAYERS, halo_chunk, 0)
    return [functools.reduce(jnp.add, parts) for parts in sums]


def first_kernel(
    halo_ref,
    fields_in,
    inverse_in,
    face_x_in,
    face_y_in,
    face_z_in,
    fields_ref,
    inverse_ref,
    face_x_ref,
    face_y_ref,
    face_z_ref,
    parts_ref,
):
    del fields_in, inverse_in, face_x_in, face_y_in, face_z_in
    _, layers, tiles, height, _ = fields_ref.shape
    blocks = (height - 3 * SUB) // SUB
    slots = layers // (LANES // GROUP)
    last_lane = lane_ids() == LANES - 1
    at = place_of

    def fill(layer, _):
        for tile in range(tiles):
            source = halo_ref[1, layer, tile]
            fields_ref[0, layer, tile, at(blocks), :] = source
            close_ring(fields_ref, (0, layer, tile), blocks, blocks, source)
            inverse_ref[layer, tile, at(blocks), :] = 0.5 * jnp.exp(-halo_ref[0, layer, tile])
        return 0

    lax.fori_loop(0, layers, fill, 0, unroll=2 * slots)

    def faces(layer, _):
        values = [inverse_ref[layer, tile, at(blocks), :] for tile in range(tiles)]
        moved = [turn(value, -1) for value in values]
        for tile in range(tiles):
            other = moved[tile]
            if tile < tiles - 1:
                other = jnp.where(last_lane, moved[tile + 1], other)
            face = reciprocal(values[tile] + other)
            face_y_ref[layer, tile, at(blocks), :] = face if tile < tiles - 1 else jnp.where(last_lane, 0.0, face)
            for block in (blocks - 1, blocks):
                face = reciprocal(
                    inverse_ref[layer, tile, at(block), :] + inverse_ref[layer, tile, at(block, 1), :]
                )
                face_x_ref[layer, tile, at(block), :] = face
                close_ring(face_x_ref, (layer, tile), block, blocks, face)
            before = inverse_ref[jnp.maximum(layer - 1, 0), tile, at(blocks), :]
            face_z_ref[layer, tile, at(blocks), :] = jnp.where(layer > 0, reciprocal(before + values[tile]), 0.0)
        return 0

    lax.fori_loop(0, layers, faces, 0, unroll=2 * slots)
    found = apply_power(1, fields_ref, face_x_ref, face_y_ref, face_z_ref, None)
    for which, part in enumerate(found):
        parts_ref[which] = part


def basis_kernel(
    last_ref,
    first_ref,
    far_ref,
    near_ref,
    parts_ref,
    face_x_ref,
    face_y_ref,
    face_z_ref,
    fields_in,
    fields_ref,
    rims_ref,
    sums_ref,
    strip_ref,
    strip_inv_ref,
    strip_x_ref,
    strip_y_ref,
    strip_z_ref,
):
    del fields_in
    _, layers, tiles, height, _ = fields_ref.shape
    rows = height - 3 * SUB
    slots = layers // (LANES // GROUP)
    groups = layers // slots
    blocks = rows // SUB
    lanes = lane_ids()
    place = lanes % GROUP
    inside_rows, inside_cols = inside_masks()
    inside_both = inside_rows & inside_cols
    first_lane, last_lane = lanes == 0, lanes == LANES - 1
    first_y = even("gy")
    at = place_of

    def spread(index, block):
        part = pl.ds(block * SUB, SUB)
        near, far = near_ref[index, part, :], far_ref[index, part, :]
        packed = (
            last_ref[index, part, :],
            jnp.where(first_y, near, far),
            jnp.where(first_y, far, near),
            first_ref[index, part, :],
        )
        found = []
        for slot in range(slots):
            moved = [turn(value, (kind - slot) * DEPTH) for kind, value in enumerate(packed)]
            found.append(
                jnp.where(
                    place < 2 * DEPTH,
                    jnp.where(place < DEPTH, moved[0], moved[1]),
                    jnp.where(place < 3 * DEPTH, moved[2], moved[3]),
                )
            )
        return found

    def put_strip(ref, block, values):
        ref[0, at(block), :] = turn(values[-1], GROUP)
        ref[slots + 1, at(block), :] = turn(values[0], -GROUP)
        for slot, value in enumerate(values):
            ref[slot + 1, at(block), :] = value
            close_ring(ref, (slot + 1,), block, blocks, value)

    for block in range(blocks + 1):
        put_strip(strip_ref.at[0], block, spread(1, block))
        values = [0.5 * jnp.exp(-value) for value in spread(0, block)]
        put_strip(strip_inv_ref, block, values)
    top, bottom = lanes >= LANES - GROUP, lanes < GROUP
    for block in range(blocks + 1):
        for slot in range(1, slots + 1):
            value = strip_inv_ref[slot, at(block), :]
            face = reciprocal(value + strip_inv_ref[slot, at(block, 1), :])
            strip_x_ref[slot - 1, at(block), :] = face
            close_ring(strip_x_ref, (slot - 1,), block, blocks, face)
            strip_y_ref[slot - 1, at(block), :] = reciprocal(value + turn(value, -1))
        for slot in range(slots + 1):
            face = reciprocal(strip_inv_ref[slot, at(block), :] + strip_inv_ref[slot + 1, at(block), :])
            if slot == 0:
                face = jnp.where(bottom, 0.0, face)
            if slot == slots:
                face = jnp.where(top, 0.0, face)
            strip_z_ref[slot, at(block), :] = face

    for power in range(1, DEPTH + 1):
        old = strip_ref.at[power - 1]
        for block in range(blocks + 1):
            levels = [old[slot, at(block), :] for slot in range(slots + 2)]
            ups = [
                strip_z_ref[slot, at(block), :] * (levels[slot] - levels[slot + 1]) for slot in range(slots + 1)
            ]
            values = []
            for slot in range(slots):
                value = levels[slot + 1]
                flux = strip_y_ref[slot, at(block), :] * (value - turn(value, -1))
                after = turn(flux, 1)
                rims_ref[power - 1, slot, at(block), :] = jnp.where(
                    place == DEPTH, after, turn(flux, 2 - 2 * DEPTH)
                )
                if power < DEPTH:
                    result = (
                        (flux - after)
                        + x_part(strip_x_ref, (slot,), old, (slot + 1,), block, value)
                        + (ups[slot + 1] - ups[slot])
                    )
                    values.append(jnp.where(inside_both if block == blocks else inside_cols, result, 0.0))
            if power < DEPTH:
                put_strip(strip_ref.at[power], block, values)

    zero = jnp.zeros((SUB, LANES), F32)

    def complete(group, lost):
        for slot in range(slots):
            layer = group * slots + slot
            for block in range(blocks + 1):
                rim = rim_of(rims_ref[0, slot, at(block), :], group)
                for tile, part in ((0, jnp.where(first_lane, -rim, 0.0)), (tiles - 1, jnp.where(last_lane, rim, 0.0))):
                    value = fields_ref[1, layer, tile, at(block), :] + part
                    fields_ref[1, layer, tile, at(block), :] = value
                    close_ring(fields_ref, (1, layer, tile), block, blocks, value)
                    if block < blocks:
                        lost = lost + part * fields_ref[0, layer, tile, at(block), :]
        return lost

    lost = lax.fori_loop(0, groups, complete, zero, unroll=4)

    found = [parts_ref[0], parts_ref[1] + lost]
    for number in range(2, DEPTH + 1):
        found += apply_power(number, fields_ref, face_x_ref, face_y_ref, face_z_ref, rims_ref)
    total = jnp.concatenate([jnp.sum(part, axis=0, keepdims=True) for part in found], axis=0)
    total = total.T
    total, rest = pair_total([(total[k : k + SUB], None) for k in range(0, LANES, SUB)])
    row = jnp.concatenate([total[0:1], rest[0:1], jnp.zeros((1, LANES - 4 * DEPTH), F32)], axis=1)
    sums_ref[...] = jnp.broadcast_to(row, sums_ref.shape)


def two_sum(first, second):
    total = first + second
    part = total - first
    return total, (first - (total - part)) + (second - part)


def pair_total(terms):
    while len(terms) > 1:
        merged = []
        for (high, low), (other, other_low) in zip(terms[::2], terms[1::2], strict=True):
            total, lost = two_sum(high, other)
            merged.append((total, lost if low is None else lost + (low + other_low)))
        terms = merged
    total, rest = terms[0]
    step = SUB // 2
    while step:
        total, lost = two_sum(total, pltpu.roll(total, step, 0))
        rest = rest + pltpu.roll(rest, step, 0) + lost
        step //= 2
    return total, rest


def quick_sum(first, second):
    total = first + second
    return total, second - (total - first)


def halves(value):
    scaled = 4097.0 * value
    high = scaled - (scaled - value)
    return high, value - high


def two_product(first, second):
    total = first * second
    first_high, first_low = halves(first)
    second_high, second_low = halves(second)
    rest = ((first_high * second_high - total) + first_high * second_low + first_low * second_high) + (
        first_low * second_low
    )
    return total, rest


def pair_add(first, second):
    total, rest = two_sum(first[0], second[0])
    return quick_sum(total, rest + (first[1] + second[1]))


def pair_sub(first, second):
    return pair_add(first, (-second[0], -second[1]))


def pair_mul(first, second):
    total, rest = two_product(first[0], second[0])
    return quick_sum(total, rest + (first[0] * second[1] + first[1] * second[0]))


def pair_div(first, second):
    guess = first[0] / second[0]
    total, rest = two_product(guess, second[0])
    left = ((first[0] - total) - rest) + (first[1] - guess * second[1])
    return quick_sum(guess, left / second[0])


def galerkin(moments):
    count = DEPTH
    matrix = {(i, j): moments[i + j + 1] for i in range(count) for j in range(i + 1)}
    right = [moments[i] for i in range(count)]
    for pivot in range(count):
        for i in range(pivot + 1, count):
            ratio = pair_div(matrix[i, pivot], matrix[pivot, pivot])
            for j in range(pivot + 1, i + 1):
                matrix[i, j] = pair_sub(matrix[i, j], pair_mul(ratio, matrix[j, pivot]))
            right[i] = pair_sub(right[i], pair_mul(ratio, right[pivot]))
    found = [None] * count
    for i in reversed(range(count)):
        value = right[i]
        for j in range(i + 1, count):
            value = pair_sub(value, pair_mul(matrix[j, i], found[j]))
        found[i] = pair_div(value, matrix[i, i])
    return [value[0] for value in found]


def finish_kernel(
    sums_ref,
    fields_ref,
    face_x_ref,
    face_y_ref,
    rims_ref,
    pressure_hbm,
    residual_hbm,
    east_hbm,
    north_hbm,
    pressure_ref,
    residual_ref,
    east_ref,
    north_ref,
    field_ref,
    sems,
):
    _, layers, tiles, height, _ = fields_ref.shape
    rows = height - 3 * SUB
    slots = layers // (LANES // GROUP)
    blocks = rows // SUB
    last_lane = lane_ids() == LANES - 1

    peers = sums_ref.shape[0]
    total, rest = pair_total([(sums_ref[k : k + SUB, :], None) for k in range(0, peers, SUB)])
    total, rest = quick_sum(total, rest + turn(total, -2 * DEPTH))
    moments = [
        tuple(jnp.broadcast_to(value[:, k : k + 1], (SUB, LANES)) for value in (total, rest)) for k in range(2 * DEPTH)
    ]
    coefs = galerkin(moments)

    def at(block, step=0):
        return pl.ds(LO + block * SUB + step, SUB)

    def mix(values):
        return functools.reduce(jnp.add, [coef * value for coef, value in zip(coefs, values, strict=True)])

    outs = (
        (pressure_ref, pressure_hbm),
        (residual_ref, residual_hbm),
        (east_ref, east_hbm),
        (north_ref, north_hbm),
    )

    def copies(group):
        part = pl.ds(group * slots, slots)
        return [
            pltpu.make_async_copy(ref.at[part], hbm.at[0, part], sems.at[index, group])
            for index, (ref, hbm) in enumerate(outs)
        ]

    def chunk(group, _):
        for slot in range(slots):
            layer = group * slots + slot
            for block in range(blocks + 1):
                values = []
                for tile in range(tiles):
                    found = [
                        fields_ref[power, layer, tile, at(block), :] for power in range(DEPTH + (block < blocks))
                    ]
                    value = mix(found[:DEPTH])
                    values.append(value)
                    field_ref[tile, at(block), :] = value
                    if block < blocks:
                        spot = (layer, pl.ds(block * SUB, SUB), pl.ds(tile * LANES, LANES))
                        pressure_ref[spot] = value
                        residual_ref[spot] = found[0] - mix(found[1:])
                if block < blocks:
                    rim = mix([rims_ref[power, slot, at(block), :] for power in range(DEPTH)])
                    rim = rim_of(rim, group)
                    moved = [turn(value, -1) for value in values]
                    for tile in range(tiles):
                        other = moved[tile]
                        if tile < tiles - 1:
                            other = jnp.where(last_lane, moved[tile + 1], other)
                        flux = face_y_ref[layer, tile, at(block), :] * (values[tile] - other)
                        if tile == tiles - 1:
                            flux = jnp.where(last_lane, rim, flux)
                        spot = (layer, pl.ds(block * SUB, SUB), pl.ds(tile * LANES, LANES))
                        north_ref[spot] = flux
            for block in range(blocks):
                for tile in range(tiles):
                    spot = (layer, pl.ds(block * SUB, SUB), pl.ds(tile * LANES, LANES))
                    east_ref[spot] = face_x_ref[layer, tile, at(block), :] * (
                        field_ref[tile, at(block), :] - field_ref[tile, at(block, 1), :]
                    )
        for copy in copies(group):
            copy.start()
        return 0

    lax.fori_loop(0, layers // slots, chunk, 0)

    def drain(group, _):
        for copy in copies(group):
            copy.wait()
        return 0

    lax.fori_loop(0, layers // slots, drain, 0)


def exchange(value, axis, near):
    count = lax.axis_size(axis)
    pairs = []
    for i in range(count):
        other = i + 1 if (i % 2 == 0) == near else i - 1
        if 0 <= other < count:
            pairs.append((i, other))
    return lax.ppermute(value, axis, pairs)


def on_device(log_perm, source):
    _, layers, rows, cols = log_perm.shape
    tiles, slots = cols // LANES, layers // (LANES // GROUP)
    height = rows + 3 * SUB
    full = (layers, tiles, height, LANES)
    deep = (layers + 1, tiles, height, LANES)
    ends = (2, layers, tiles * DEPTH, LANES)
    edges = (2, rows + SUB, LANES)
    strip = (slots + 2, height, LANES)
    inner = (slots, height, LANES)
    peers = lax.axis_size("gx") * lax.axis_size("gy")
    cells = layers * rows * cols

    log_perm, source = (pltpu.with_memory_space_constraint(value, pltpu.HBM) for value in (log_perm, source))
    powers = (in_vmem(DEPTH + 1, *full), in_vmem(*deep)) + (in_vmem(*full),) * 2 + (in_vmem(*deep),)
    far = pl.pallas_call(
        far_kernel,
        out_shape=in_vmem(*ends),
        in_specs=[HBM_SPEC] * 2,
        out_specs=VMEM_SPEC,
        scratch_shapes=[in_vmem(2, tiles, layers, SUB, LANES), pltpu.SemaphoreType.DMA((2, tiles))],
        compiler_params=params(16),
        name="far",
    )(log_perm, source)
    far = exchange(far, "gx", False)
    log_own, fields, near = pl.pallas_call(
        load_kernel,
        out_shape=(in_vmem(*full), powers[0], in_vmem(*ends)),
        in_specs=[HBM_SPEC] * 2,
        out_specs=[VMEM_SPEC] * 3,
        scratch_shapes=[pltpu.SemaphoreType.DMA((2, tiles))],
        compiler_params=params(16),
        cost_estimate=pl.CostEstimate(flops=cells, bytes_accessed=8 * cells, transcendentals=0),
        name="load",
    )(log_perm, source)
    near = exchange(near, "gx", True)
    *fields, last, first = pl.pallas_call(
        own_kernel,
        out_shape=powers + (in_vmem(*edges),) * 2,
        in_specs=[VMEM_SPEC] * 2,
        out_specs=[VMEM_SPEC] * 7,
        input_output_aliases={1: 0},
        compiler_params=params(16),
        cost_estimate=pl.CostEstimate(flops=60 * cells, bytes_accessed=8 * cells, transcendentals=4 * cells),
        name="own",
    )(log_own, fields)
    last, first, near, far, halo = pl.pallas_call(
        edge_kernel,
        out_shape=(in_vmem(*edges),) * 4 + (in_vmem(2, layers, tiles, SUB, LANES),),
        in_specs=[VMEM_SPEC] * 4,
        out_specs=[VMEM_SPEC] * 5,
        input_output_aliases={2: 0, 3: 1},
        compiler_params=params(16),
        name="edges",
    )(far, near, last, first)
    far = exchange(far, "gy", False)
    near = exchange(near, "gy", True)
    fields, _, face_x, face_y, face_z, parts = pl.pallas_call(
        first_kernel,
        out_shape=powers + (in_vmem(2, SUB, LANES),),
        in_specs=[VMEM_SPEC] * 6,
        out_specs=[VMEM_SPEC] * 6,
        input_output_aliases={1: 0, 2: 1, 3: 2, 4: 3, 5: 4},
        compiler_params=params(16),
        cost_estimate=pl.CostEstimate(flops=40 * cells, bytes_accessed=8 * cells, transcendentals=cells),
        name="first",
    )(halo, *fields)
    fields, rims, sums = pl.pallas_call(
        basis_kernel,
        out_shape=(powers[0], in_vmem(DEPTH, *inner), in_vmem(peers, LANES)),
        in_specs=[VMEM_SPEC] * 9,
        out_specs=[VMEM_SPEC] * 3,
        input_output_aliases={8: 0},
        scratch_shapes=[
            in_vmem(DEPTH, *strip),
            in_vmem(*strip),
            in_vmem(*inner),
            in_vmem(*inner),
            in_vmem(slots + 1, height, LANES),
        ],
        compiler_params=params(16),
        name="basis",
    )(last, first, far, near, parts, face_x, face_y, face_z, fields)
    sums = lax.all_to_all(sums, ("gx", "gy"), 0, 0, tiled=True)
    block = (layers, rows, cols)
    return pl.pallas_call(
        finish_kernel,
        out_shape=(jax.ShapeDtypeStruct((1, *block), F32),) * 4,
        in_specs=[VMEM_SPEC] * 5,
        out_specs=[ANY_SPEC] * 4,
        scratch_shapes=[in_vmem(*block)] * 4
        + [in_vmem(tiles, height, LANES), pltpu.SemaphoreType.DMA((4, layers // slots))],
        compiler_params=params(16),
        name="finish",
    )(sums, fields, face_x, face_y, rims)


def solution(mesh):
    spec = P(None, None, "gx", "gy")
    return jax.shard_map(on_device, mesh=mesh, in_specs=(spec,) * 2, out_specs=(spec,) * 4, check_vma=False)
```

```python
import functools

import jax
import jax.numpy as jnp
from jax import lax
from jax.experimental import pallas as pl
from jax.experimental.pallas import tpu as pltpu
from jax.sharding import PartitionSpec as P

DEPTH = 4
LANES = 128
SUB = 8
LO = 8
GROUP = 4 * DEPTH
HALO_LAYERS = 16
SPARE = 3
F32 = jnp.float32
HBM_SPEC = pl.BlockSpec(memory_space=pltpu.HBM)
VMEM_SPEC = pl.BlockSpec(memory_space=pltpu.VMEM)
ANY_SPEC = pl.BlockSpec(memory_space=pl.ANY)


def in_vmem(*shape):
    return pltpu.VMEM(shape, F32)


def params(limit):
    return pltpu.CompilerParams(vmem_limit_bytes=limit * 1024 * 1024)


def lane_ids():
    return lax.broadcasted_iota(jnp.int32, (SUB, LANES), 1)


def row_ids():
    return lax.broadcasted_iota(jnp.int32, (SUB, LANES), 0)


def turn(value, shift):
    return pltpu.roll(value, shift % LANES, 1) if shift % LANES else value


def reciprocal(value):
    return 1.0 / value


def even(axis):
    return lax.rem(lax.axis_index(axis), 2) == 0


def far_kernel(log_hbm, src_hbm, far_ref, rows_ref, sems):
    _, _, rows, cols = log_hbm.shape
    first = even("gx")
    start = pl.multiple_of(jnp.where(first, 0, rows - SUB), SUB)
    copies = []
    for index, hbm in enumerate((log_hbm, src_hbm)):
        for tile in range(cols // LANES):
            copies.append(
                pltpu.make_async_copy(
                    hbm.at[0, :, pl.ds(start, SUB), pl.ds(tile * LANES, LANES)],
                    rows_ref.at[index, tile],
                    sems.at[index, tile],
                )
            )
            copies[-1].start()
    for copy in copies:
        copy.wait()
    for tile in range(cols // LANES):
        head = rows_ref[:, tile, :, 0:DEPTH, :]
        tail = rows_ref[:, tile, :, SUB - DEPTH : SUB, :]
        far_ref[:, :, pl.ds(tile * DEPTH, DEPTH), :] = jnp.where(first, head, tail)


def load_kernel(log_hbm, src_hbm, log_ref, fields_ref, near_ref, sems):
    _, _, rows, cols = log_hbm.shape
    tiles = cols // LANES
    first = even("gx")
    copies = []
    refs = (log_ref, fields_ref.at[0])
    for index, (hbm, ref) in enumerate(zip((log_hbm, src_hbm), refs, strict=True)):
        for tile in range(tiles):
            copies.append(
                pltpu.make_async_copy(
                    hbm.at[0, :, :, pl.ds(tile * LANES, LANES)],
                    ref.at[:, tile, pl.ds(LO, rows), :],
                    sems.at[index, tile],
                )
            )
            copies[-1].start()
    for copy in copies:
        copy.wait()
    for index, ref in enumerate(refs):
        for tile in range(tiles):
            head = ref[:, tile, LO : LO + DEPTH, :]
            tail = ref[:, tile, LO + rows - DEPTH : LO + rows, :]
            near_ref[index, :, pl.ds(tile * DEPTH, DEPTH), :] = jnp.where(first, tail, head)


def pack(blocks_of, lane):
    lanes = lane_ids()
    total = None
    for layer, value in enumerate(blocks_of):
        moved = turn(value, layer * DEPTH - lane)
        total = moved if total is None else jnp.where(lanes // DEPTH == layer, moved, total)
    return total


def put_column_faces(face_y_ref, face_w_ref, layer, place, values):
    lanes = lane_ids()
    first_lane, last_lane = lanes == 0, lanes == LANES - 1
    tiles = len(values)
    moved = [turn(value, -1) for value in values]
    others = [jnp.where(last_lane, moved[tile + 1], moved[tile]) for tile in range(tiles - 1)] + [moved[-1]]
    faces = [reciprocal(value + other) for value, other in zip(values, others, strict=True)]
    faces[-1] = jnp.where(last_lane, 0.0, faces[-1])
    moved = [jnp.zeros((SUB, LANES), F32)] + [turn(face, 1) for face in faces]
    for tile in range(tiles):
        face_y_ref[layer, tile, place, :] = faces[tile]
        face_w_ref[layer, tile, place, :] = jnp.where(first_lane, moved[tile], moved[tile + 1])


def own_kernel(
    log_ref,
    fields_in,
    fields_ref,
    inverse_ref,
    face_x_ref,
    face_y_ref,
    face_z_ref,
    face_w_ref,
    last_ref,
    first_ref,
):
    del fields_in
    layers, tiles, height, _ = log_ref.shape
    rows = height - 3 * SUB
    blocks = rows // SUB
    slots = layers // (LANES // GROUP)
    ring = LO + rows + SUB
    base_ref = fields_ref.at[0]

    def at(block, step=0):
        return pl.ds(LO + block * SUB + step, SUB)

    def fill(layer, _):
        for tile in range(tiles):
            for block in range(blocks):
                value = 0.5 * jnp.exp(-log_ref[layer, tile, at(block), :])
                inverse_ref[layer, tile, at(block), :] = value
                if block == 0:
                    inverse_ref[layer, tile, pl.ds(ring, 1), :] = value[0:1]
        return 0

    lax.fori_loop(0, layers, fill, 0, unroll=slots)

    zero = jnp.zeros((SUB, LANES), F32)
    for tile in range(tiles):
        for block in range(blocks + 1):
            face_z_ref[0, tile, at(block), :] = zero
            face_z_ref[layers, tile, at(block), :] = zero

    def faces(layer, _):
        for block in range(blocks):
            values = [inverse_ref[layer, tile, at(block), :] for tile in range(tiles)]
            put_column_faces(face_y_ref, face_w_ref, layer, at(block), values)
            for tile in range(tiles):
                face_x_ref[layer, tile, at(block), :] = reciprocal(
                    values[tile] + inverse_ref[layer, tile, at(block, 1), :]
                )
        return 0

    lax.fori_loop(0, layers, faces, 0, unroll=slots)

    def faces_z(layer, _):
        for tile in range(tiles):
            for block in range(blocks):
                face_z_ref[layer, tile, at(block), :] = reciprocal(
                    inverse_ref[layer - 1, tile, at(block), :] + inverse_ref[layer, tile, at(block), :]
                )
        return 0

    lax.fori_loop(1, layers, faces_z, 0, unroll=slots)

    base_ref[:, :, pl.ds(ring, 1), :] = base_ref[:, :, pl.ds(LO, 1), :]
    for index, ref in enumerate((log_ref, base_ref)):
        for block in range(blocks):
            part = pl.ds(block * SUB, SUB)
            last_ref[index, part, :] = pack(
                [ref[layer, tiles - 1, at(block), :] for layer in range(layers)], LANES - DEPTH
            )
            first_ref[index, part, :] = pack([ref[layer, 0, at(block), :] for layer in range(layers)], 0)


def edge_kernel(far_in, near_in, last_in, first_in, last_ref, first_ref, near_ref, far_ref, halo_ref):
    del last_in, first_in
    _, layers, tiles, _, _ = halo_ref.shape
    height = last_ref.shape[1]
    one, two = even("gx"), even("gy")
    for tile in range(tiles):
        part = pl.ds(tile * DEPTH, DEPTH)
        near, far = near_in[:, :, part, :], far_in[:, :, part, :]
        halo_ref[:, :, tile, 0:DEPTH, :] = jnp.where(one, near, far)
        halo_ref[:, :, tile, DEPTH:SUB, :] = jnp.where(one, far, near)
    for index in range(2):
        part = pl.ds(height - SUB, SUB)
        last_ref[index, part, :] = pack(
            [halo_ref[index, layer, tiles - 1] for layer in range(layers)], LANES - DEPTH
        )
        first_ref[index, part, :] = pack([halo_ref[index, layer, 0] for layer in range(layers)], 0)
    near_ref[...] = jnp.where(two, last_ref[...], first_ref[...])
    far_ref[...] = jnp.where(two, first_ref[...], last_ref[...])


def place_of(block, step=0):
    return pl.ds(LO + block * SUB + step, SUB)


def close_ring(ref, index, block, blocks, value):
    ring = LO + (blocks + 1) * SUB
    if block == 0:
        ref[(*index, pl.ds(ring, 1), slice(None))] = value[0:1]
    if block == blocks:
        ref[(*index, pl.ds(LO - 1, 1), slice(None))] = value[SUB - 1 : SUB]


def rim_of(values, group):
    return pltpu.roll(values, LANES - 1 - DEPTH - group * GROUP, 1)


def x_part(face_ref, index, old, old_index, block, value):
    there = old[(*old_index, place_of(block, 1), slice(None))]
    back = old[(*old_index, place_of(block, -1), slice(None))]
    return face_ref[(*index, place_of(block), slice(None))] * (value - there) - face_ref[
        (*index, place_of(block, -1), slice(None))
    ] * (back - value)


def inside_masks():
    here_x, here_y = lax.axis_index("gx"), lax.axis_index("gy")
    past_x, before_x = here_x < lax.axis_size("gx") - 1, here_x > 0
    past_y, before_y = here_y < lax.axis_size("gy") - 1, here_y > 0
    place = lane_ids() % GROUP
    inside_rows = jnp.where(row_ids() < DEPTH, past_x.astype(jnp.int32), before_x.astype(jnp.int32)) > 0
    inside_cols = (
        jnp.where(
            (place >= DEPTH) & (place < 2 * DEPTH),
            past_y.astype(jnp.int32),
            jnp.where((place >= 2 * DEPTH) & (place < 3 * DEPTH), before_y.astype(jnp.int32), 1),
        )
        > 0
    )
    return inside_rows, inside_cols


def apply_power(number, fields_ref, face_x_ref, face_y_ref, face_z_ref, face_w_ref, rims_ref):
    _, layers, tiles, height, _ = fields_ref.shape
    blocks = (height - 3 * SUB) // SUB
    slots = layers // (LANES // GROUP)
    groups = layers // slots
    old, new = fields_ref.at[number - 1], fields_ref.at[number]
    lanes = lane_ids()
    first_lane, last_lane = lanes == 0, lanes == LANES - 1
    inside_rows, _ = inside_masks()
    at = place_of

    def layer_range(start, count, block):
        levels = []
        for step in range(-1, count + 1):
            layer = start + step
            if step < 0:
                layer = jnp.maximum(layer, 0)
            if step == count:
                layer = jnp.minimum(layer, layers - 1)
            levels.append([old[layer, tile, at(block), :] for tile in range(tiles)])
        ups = [
            [
                face_z_ref[start + step, tile, at(block), :] * (levels[step][tile] - levels[step + 1][tile])
                for tile in range(tiles)
            ]
            for step in range(count + 1)
        ]
        for step in range(count):
            layer = start + step
            values = levels[step + 1]
            ahead = [turn(value, -1) for value in values]
            behind = [turn(value, 1) for value in values]
            rim = None
            if rims_ref is not None:
                rim = rim_of(rims_ref[number - 1, step % slots, at(block), :], start // slots + step // slots)
            out, back = [], []
            for tile in range(tiles):
                other = ahead[tile] if tile == tiles - 1 else jnp.where(last_lane, ahead[tile + 1], ahead[tile])
                out.append(face_y_ref[layer, tile, at(block), :] * (values[tile] - other))
                other = behind[tile] if tile == 0 else jnp.where(first_lane, behind[tile - 1], behind[tile])
                back.append(face_w_ref[layer, tile, at(block), :] * (other - values[tile]))
            if rim is not None:
                out[-1] = jnp.where(last_lane, rim, out[-1])
                back[0] = jnp.where(first_lane, rim, back[0])
            for tile in range(tiles):
                value = values[tile]
                result = (
                    (out[tile] - back[tile])
                    + x_part(face_x_ref, (layer, tile), old, (layer, tile), block, value)
                    + (ups[step + 1][tile] - ups[step][tile])
                )
                if block == blocks:
                    result = jnp.where(inside_rows, result, 0.0)
                new[layer, tile, at(block), :] = result
                if number < DEPTH:
                    close_ring(new, (layer, tile), block, blocks, result)
                yield tile, value, result

    def chunk(group, sums):
        own_sums, next_sums = list(sums[0]), list(sums[1])
        for block in range(blocks):
            for tile, value, result in layer_range(group * slots, slots, block):
                own_sums[tile] = own_sums[tile] + value * value
                next_sums[tile] = next_sums[tile] + value * result
        return tuple(own_sums), tuple(next_sums)

    def halo_chunk(part, _):
        for _ in layer_range(part * HALO_LAYERS, HALO_LAYERS, blocks):
            pass
        return 0

    start = (jnp.zeros((SUB, LANES), F32),) * tiles
    sums = lax.fori_loop(0, groups, chunk, (start, start), unroll=2)
    if number < DEPTH:
        lax.fori_loop(0, layers // HALO_LAYERS, halo_chunk, 0)
    return [functools.reduce(jnp.add, parts) for parts in sums]


def first_kernel(
    halo_ref,
    fields_in,
    inverse_in,
    face_x_in,
    face_y_in,
    face_z_in,
    face_w_in,
    fields_ref,
    inverse_ref,
    face_x_ref,
    face_y_ref,
    face_z_ref,
    face_w_ref,
    parts_ref,
):
    del fields_in, inverse_in, face_x_in, face_y_in, face_z_in, face_w_in
    _, layers, tiles, height, _ = fields_ref.shape
    blocks = (height - 3 * SUB) // SUB
    slots = layers // (LANES // GROUP)
    at = place_of

    def fill(layer, _):
        for tile in range(tiles):
            source = halo_ref[1, layer, tile]
            fields_ref[0, layer, tile, at(blocks), :] = source
            close_ring(fields_ref, (0, layer, tile), blocks, blocks, source)
            inverse_ref[layer, tile, at(blocks), :] = 0.5 * jnp.exp(-halo_ref[0, layer, tile])
        return 0

    lax.fori_loop(0, layers, fill, 0, unroll=2 * slots)

    def faces(layer, _):
        values = [inverse_ref[layer, tile, at(blocks), :] for tile in range(tiles)]
        put_column_faces(face_y_ref, face_w_ref, layer, at(blocks), values)
        for tile in range(tiles):
            for block in (blocks - 1, blocks):
                face = reciprocal(
                    inverse_ref[layer, tile, at(block), :] + inverse_ref[layer, tile, at(block, 1), :]
                )
                face_x_ref[layer, tile, at(block), :] = face
                close_ring(face_x_ref, (layer, tile), block, blocks, face)
            before = inverse_ref[jnp.maximum(layer - 1, 0), tile, at(blocks), :]
            face_z_ref[layer, tile, at(blocks), :] = jnp.where(layer > 0, reciprocal(before + values[tile]), 0.0)
        return 0

    lax.fori_loop(0, layers, faces, 0, unroll=2 * slots)
    found = apply_power(1, fields_ref, face_x_ref, face_y_ref, face_z_ref, face_w_ref, None)
    for which, part in enumerate(found):
        parts_ref[which] = part


def basis_kernel(
    last_ref,
    first_ref,
    far_ref,
    near_ref,
    parts_ref,
    face_x_ref,
    face_y_ref,
    face_z_ref,
    face_w_ref,
    fields_in,
    fields_ref,
    rims_ref,
    sums_ref,
    strip_ref,
    strip_inv_ref,
    strip_x_ref,
    strip_y_ref,
    strip_z_ref,
):
    del fields_in
    _, layers, tiles, height, _ = fields_ref.shape
    rows = height - 3 * SUB
    slots = layers // (LANES // GROUP)
    groups = layers // slots
    blocks = rows // SUB
    lanes = lane_ids()
    place = lanes % GROUP
    inside_rows, inside_cols = inside_masks()
    inside_both = inside_rows & inside_cols
    first_lane, last_lane = lanes == 0, lanes == LANES - 1
    first_y = even("gy")
    at = place_of

    def spread(index, block):
        part = pl.ds(block * SUB, SUB)
        near, far = near_ref[index, part, :], far_ref[index, part, :]
        packed = (
            last_ref[index, part, :],
            jnp.where(first_y, near, far),
            jnp.where(first_y, far, near),
            first_ref[index, part, :],
        )
        found = []
        for slot in range(slots):
            moved = [turn(value, (kind - slot) * DEPTH) for kind, value in enumerate(packed)]
            found.append(
                jnp.where(
                    place < 2 * DEPTH,
                    jnp.where(place < DEPTH, moved[0], moved[1]),
                    jnp.where(place < 3 * DEPTH, moved[2], moved[3]),
                )
            )
        return found

    def put_strip(ref, block, values):
        ref[0, at(block), :] = turn(values[-1], GROUP)
        ref[slots + 1, at(block), :] = turn(values[0], -GROUP)
        for slot, value in enumerate(values):
            ref[slot + 1, at(block), :] = value
            close_ring(ref, (slot + 1,), block, blocks, value)

    for block in range(blocks + 1):
        put_strip(strip_ref.at[0], block, spread(1, block))
        values = [0.5 * jnp.exp(-value) for value in spread(0, block)]
        put_strip(strip_inv_ref, block, values)
    top, bottom = lanes >= LANES - GROUP, lanes < GROUP
    for block in range(blocks + 1):
        for slot in range(1, slots + 1):
            value = strip_inv_ref[slot, at(block), :]
            face = reciprocal(value + strip_inv_ref[slot, at(block, 1), :])
            strip_x_ref[slot - 1, at(block), :] = face
            close_ring(strip_x_ref, (slot - 1,), block, blocks, face)
            strip_y_ref[slot - 1, at(block), :] = reciprocal(value + turn(value, -1))
        for slot in range(slots + 1):
            face = reciprocal(strip_inv_ref[slot, at(block), :] + strip_inv_ref[slot + 1, at(block), :])
            if slot == 0:
                face = jnp.where(bottom, 0.0, face)
            if slot == slots:
                face = jnp.where(top, 0.0, face)
            strip_z_ref[slot, at(block), :] = face

    for power in range(1, DEPTH + 1):
        old = strip_ref.at[power - 1]
        for block in range(blocks + 1):
            levels = [old[slot, at(block), :] for slot in range(slots + 2)]
            ups = [
                strip_z_ref[slot, at(block), :] * (levels[slot] - levels[slot + 1]) for slot in range(slots + 1)
            ]
            values = []
            for slot in range(slots):
                value = levels[slot + 1]
                flux = strip_y_ref[slot, at(block), :] * (value - turn(value, -1))
                after = turn(flux, 1)
                rims_ref[power - 1, slot, at(block), :] = jnp.where(
                    place == DEPTH, after, turn(flux, 2 - 2 * DEPTH)
                )
                if power < DEPTH:
                    result = (
                        (flux - after)
                        + x_part(strip_x_ref, (slot,), old, (slot + 1,), block, value)
                        + (ups[slot + 1] - ups[slot])
                    )
                    values.append(jnp.where(inside_both if block == blocks else inside_cols, result, 0.0))
            if power < DEPTH:
                put_strip(strip_ref.at[power], block, values)

    zero = jnp.zeros((SUB, LANES), F32)

    def complete(group, lost):
        for slot in range(slots):
            layer = group * slots + slot
            for block in range(blocks + 1):
                rim = rim_of(rims_ref[0, slot, at(block), :], group)
                for tile, part in ((0, jnp.where(first_lane, -rim, 0.0)), (tiles - 1, jnp.where(last_lane, rim, 0.0))):
                    value = fields_ref[1, layer, tile, at(block), :] + part
                    fields_ref[1, layer, tile, at(block), :] = value
                    close_ring(fields_ref, (1, layer, tile), block, blocks, value)
                    if block < blocks:
                        lost = lost + part * fields_ref[0, layer, tile, at(block), :]
        return lost

    lost = lax.fori_loop(0, groups, complete, zero, unroll=4)

    found = [parts_ref[0], parts_ref[1] + lost]
    for number in range(2, DEPTH + 1):
        found += apply_power(number, fields_ref, face_x_ref, face_y_ref, face_z_ref, face_w_ref, rims_ref)
    total = jnp.concatenate([jnp.sum(part, axis=0, keepdims=True) for part in found], axis=0)
    total = total.T
    total, rest = pair_total([(total[k : k + SUB], None) for k in range(0, LANES, SUB)])
    row = jnp.concatenate([total[0:1], rest[0:1], jnp.zeros((1, LANES - 4 * DEPTH), F32)], axis=1)
    sums_ref[...] = jnp.broadcast_to(row, sums_ref.shape)


def two_sum(first, second):
    total = first + second
    part = total - first
    return total, (first - (total - part)) + (second - part)


def pair_total(terms):
    while len(terms) > 1:
        merged = []
        for (high, low), (other, other_low) in zip(terms[::2], terms[1::2], strict=True):
            total, lost = two_sum(high, other)
            merged.append((total, lost if low is None else lost + (low + other_low)))
        terms = merged
    total, rest = terms[0]
    step = SUB // 2
    while step:
        total, lost = two_sum(total, pltpu.roll(total, step, 0))
        rest = rest + pltpu.roll(rest, step, 0) + lost
        step //= 2
    return total, rest


def quick_sum(first, second):
    total = first + second
    return total, second - (total - first)


def halves(value):
    scaled = 4097.0 * value
    high = scaled - (scaled - value)
    return high, value - high


def two_product(first, second):
    total = first * second
    first_high, first_low = halves(first)
    second_high, second_low = halves(second)
    rest = ((first_high * second_high - total) + first_high * second_low + first_low * second_high) + (
        first_low * second_low
    )
    return total, rest


def pair_add(first, second):
    total, rest = two_sum(first[0], second[0])
    return quick_sum(total, rest + (first[1] + second[1]))


def pair_sub(first, second):
    return pair_add(first, (-second[0], -second[1]))


def pair_mul(first, second):
    total, rest = two_product(first[0], second[0])
    return quick_sum(total, rest + (first[0] * second[1] + first[1] * second[0]))


def pair_div(first, second):
    guess = first[0] / second[0]
    total, rest = two_product(guess, second[0])
    left = ((first[0] - total) - rest) + (first[1] - guess * second[1])
    return quick_sum(guess, left / second[0])


def galerkin(moments):
    count = DEPTH
    matrix = {(i, j): moments[i + j + 1] for i in range(count) for j in range(i + 1)}
    right = [moments[i] for i in range(count)]
    for pivot in range(count):
        for i in range(pivot + 1, count):
            ratio = pair_div(matrix[i, pivot], matrix[pivot, pivot])
            for j in range(pivot + 1, i + 1):
                matrix[i, j] = pair_sub(matrix[i, j], pair_mul(ratio, matrix[j, pivot]))
            right[i] = pair_sub(right[i], pair_mul(ratio, right[pivot]))
    found = [None] * count
    for i in reversed(range(count)):
        value = right[i]
        for j in range(i + 1, count):
            value = pair_sub(value, pair_mul(matrix[j, i], found[j]))
        found[i] = pair_div(value, matrix[i, i])
    return [value[0] for value in found]


def finish_kernel(
    sums_ref,
    fields_ref,
    face_x_ref,
    face_y_ref,
    rims_ref,
    pressure_hbm,
    residual_hbm,
    east_hbm,
    north_hbm,
    pressure_ref,
    residual_ref,
    east_ref,
    north_ref,
    field_ref,
    sems,
):
    _, layers, tiles, height, _ = fields_ref.shape
    rows = height - 3 * SUB
    slots = layers // (LANES // GROUP)
    blocks = rows // SUB
    last_lane = lane_ids() == LANES - 1

    peers = sums_ref.shape[0]
    total, rest = pair_total([(sums_ref[k : k + SUB, :], None) for k in range(0, peers, SUB)])
    total, rest = quick_sum(total, rest + turn(total, -2 * DEPTH))
    moments = [
        tuple(jnp.broadcast_to(value[:, k : k + 1], (SUB, LANES)) for value in (total, rest)) for k in range(2 * DEPTH)
    ]
    coefs = galerkin(moments)

    def at(block, step=0):
        return pl.ds(LO + block * SUB + step, SUB)

    def mix(values):
        return functools.reduce(jnp.add, [coef * value for coef, value in zip(coefs, values, strict=True)])

    outs = (
        (pressure_ref, pressure_hbm),
        (residual_ref, residual_hbm),
        (east_ref, east_hbm),
        (north_ref, north_hbm),
    )

    def copies(group):
        part = pl.ds(group * slots, slots)
        return [
            pltpu.make_async_copy(ref.at[part], hbm.at[0, part], sems.at[index, group])
            for index, (ref, hbm) in enumerate(outs)
        ]

    def chunk(group, _):
        for slot in range(slots):
            layer = group * slots + slot
            for block in range(blocks + 1):
                values = []
                for tile in range(tiles):
                    found = [
                        fields_ref[power, layer, tile, at(block), :] for power in range(DEPTH + (block < blocks))
                    ]
                    value = mix(found[:DEPTH])
                    values.append(value)
                    field_ref[tile, at(block), :] = value
                    if block < blocks:
                        spot = (layer, pl.ds(block * SUB, SUB), pl.ds(tile * LANES, LANES))
                        pressure_ref[spot] = value
                        residual_ref[spot] = found[0] - mix(found[1:])
                if block < blocks:
                    rim = mix([rims_ref[power, slot, at(block), :] for power in range(DEPTH)])
                    rim = rim_of(rim, group)
                    moved = [turn(value, -1) for value in values]
                    for tile in range(tiles):
                        other = moved[tile]
                        if tile < tiles - 1:
                            other = jnp.where(last_lane, moved[tile + 1], other)
                        flux = face_y_ref[layer, tile, at(block), :] * (values[tile] - other)
                        if tile == tiles - 1:
                            flux = jnp.where(last_lane, rim, flux)
                        spot = (layer, pl.ds(block * SUB, SUB), pl.ds(tile * LANES, LANES))
                        north_ref[spot] = flux
            for block in range(blocks):
                for tile in range(tiles):
                    spot = (layer, pl.ds(block * SUB, SUB), pl.ds(tile * LANES, LANES))
                    east_ref[spot] = face_x_ref[layer, tile, at(block), :] * (
                        field_ref[tile, at(block), :] - field_ref[tile, at(block, 1), :]
                    )
        for copy in copies(group):
            copy.start()
        return 0

    lax.fori_loop(0, layers // slots, chunk, 0)

    def drain(group, _):
        for copy in copies(group):
            copy.wait()
        return 0

    lax.fori_loop(0, layers // slots, drain, 0)


def exchange(value, axis, near):
    count = lax.axis_size(axis)
    pairs = []
    for i in range(count):
        other = i + 1 if (i % 2 == 0) == near else i - 1
        if 0 <= other < count:
            pairs.append((i, other))
    return lax.ppermute(value, axis, pairs)


def on_device(log_perm, source):
    _, layers, rows, cols = log_perm.shape
    tiles, slots = cols // LANES, layers // (LANES // GROUP)
    height = rows + 3 * SUB
    full = (layers, tiles, height, LANES)
    deep = (layers + 1, tiles, height, LANES)
    spare = (layers + SPARE, tiles, height, LANES)
    ends = (2, layers, tiles * DEPTH, LANES)
    edges = (2, rows + SUB, LANES)
    strip = (slots + 2, height, LANES)
    inner = (slots, height, LANES)
    peers = lax.axis_size("gx") * lax.axis_size("gy")
    cells = layers * rows * cols

    log_perm, source = (pltpu.with_memory_space_constraint(value, pltpu.HBM) for value in (log_perm, source))
    powers = (in_vmem(DEPTH + 1, *full), in_vmem(*spare)) + (in_vmem(*full),) * 2 + (in_vmem(*deep), in_vmem(*full))
    far = pl.pallas_call(
        far_kernel,
        out_shape=in_vmem(*ends),
        in_specs=[HBM_SPEC] * 2,
        out_specs=VMEM_SPEC,
        scratch_shapes=[in_vmem(2, tiles, layers, SUB, LANES), pltpu.SemaphoreType.DMA((2, tiles))],
        compiler_params=params(16),
        name="far",
    )(log_perm, source)
    far = exchange(far, "gx", False)
    log_own, fields, near = pl.pallas_call(
        load_kernel,
        out_shape=(in_vmem(*full), powers[0], in_vmem(*ends)),
        in_specs=[HBM_SPEC] * 2,
        out_specs=[VMEM_SPEC] * 3,
        scratch_shapes=[pltpu.SemaphoreType.DMA((2, tiles))],
        compiler_params=params(16),
        cost_estimate=pl.CostEstimate(flops=cells, bytes_accessed=8 * cells, transcendentals=0),
        name="load",
    )(log_perm, source)
    near = exchange(near, "gx", True)
    *fields, last, first = pl.pallas_call(
        own_kernel,
        out_shape=powers + (in_vmem(*edges),) * 2,
        in_specs=[VMEM_SPEC] * 2,
        out_specs=[VMEM_SPEC] * 8,
        input_output_aliases={1: 0},
        compiler_params=params(16),
        cost_estimate=pl.CostEstimate(flops=60 * cells, bytes_accessed=8 * cells, transcendentals=4 * cells),
        name="own",
    )(log_own, fields)
    last, first, near, far, halo = pl.pallas_call(
        edge_kernel,
        out_shape=(in_vmem(*edges),) * 4 + (in_vmem(2, layers, tiles, SUB, LANES),),
        in_specs=[VMEM_SPEC] * 4,
        out_specs=[VMEM_SPEC] * 5,
        input_output_aliases={2: 0, 3: 1},
        compiler_params=params(16),
        name="edges",
    )(far, near, last, first)
    far = exchange(far, "gy", False)
    near = exchange(near, "gy", True)
    fields, _, face_x, face_y, face_z, face_w, parts = pl.pallas_call(
        first_kernel,
        out_shape=powers + (in_vmem(2, SUB, LANES),),
        in_specs=[VMEM_SPEC] * 7,
        out_specs=[VMEM_SPEC] * 7,
        input_output_aliases={1: 0, 2: 1, 3: 2, 4: 3, 5: 4, 6: 5},
        compiler_params=params(16),
        cost_estimate=pl.CostEstimate(flops=40 * cells, bytes_accessed=8 * cells, transcendentals=cells),
        name="first",
    )(halo, *fields)
    fields, rims, sums = pl.pallas_call(
        basis_kernel,
        out_shape=(powers[0], in_vmem(DEPTH, *inner), in_vmem(peers, LANES)),
        in_specs=[VMEM_SPEC] * 10,
        out_specs=[VMEM_SPEC] * 3,
        input_output_aliases={9: 0},
        scratch_shapes=[
            in_vmem(DEPTH, *strip),
            in_vmem(*strip),
            in_vmem(*inner),
            in_vmem(*inner),
            in_vmem(slots + 1, height, LANES),
        ],
        compiler_params=params(16),
        name="basis",
    )(last, first, far, near, parts, face_x, face_y, face_z, face_w, fields)
    sums = lax.all_to_all(sums, ("gx", "gy"), 0, 0, tiled=True)
    block = (layers, rows, cols)
    return pl.pallas_call(
        finish_kernel,
        out_shape=(jax.ShapeDtypeStruct((1, *block), F32),) * 4,
        in_specs=[VMEM_SPEC] * 5,
        out_specs=[ANY_SPEC] * 4,
        scratch_shapes=[in_vmem(*block)] * 4
        + [in_vmem(tiles, height, LANES), pltpu.SemaphoreType.DMA((4, layers // slots))],
        compiler_params=params(16),
        name="finish",
    )(sums, fields, face_x, face_y, rims)


def solution(mesh):
    spec = P(None, None, "gx", "gy")
    return jax.shard_map(on_device, mesh=mesh, in_specs=(spec,) * 2, out_specs=(spec,) * 4, check_vma=False)
```

```python
import functools

import jax
import jax.numpy as jnp
from jax import lax
from jax.experimental import pallas as pl
from jax.experimental.pallas import tpu as pltpu
from jax.sharding import PartitionSpec as P

DEPTH = 4
LANES = 128
SUB = 8
LO = 8
GROUP = 4 * DEPTH
CHUNK = 8
SPARE = 3
F32 = jnp.float32
HBM_SPEC = pl.BlockSpec(memory_space=pltpu.HBM)
VMEM_SPEC = pl.BlockSpec(memory_space=pltpu.VMEM)
ANY_SPEC = pl.BlockSpec(memory_space=pl.ANY)


def in_vmem(*shape):
    return pltpu.VMEM(shape, F32)


def params(limit):
    return pltpu.CompilerParams(vmem_limit_bytes=limit * 1024 * 1024)


def lane_ids():
    return lax.broadcasted_iota(jnp.int32, (SUB, LANES), 1)


def row_ids():
    return lax.broadcasted_iota(jnp.int32, (SUB, LANES), 0)


def turn(value, shift):
    return pltpu.roll(value, shift % LANES, 1) if shift % LANES else value


def reciprocal(value):
    return 1.0 / value


def even(axis):
    return lax.rem(lax.axis_index(axis), 2) == 0


def far_kernel(log_hbm, src_hbm, far_ref, rows_ref, sems):
    _, _, rows, cols = log_hbm.shape
    first = even("gx")
    start = pl.multiple_of(jnp.where(first, 0, rows - SUB), SUB)
    copies = []
    for index, hbm in enumerate((log_hbm, src_hbm)):
        for tile in range(cols // LANES):
            copies.append(
                pltpu.make_async_copy(
                    hbm.at[0, :, pl.ds(start, SUB), pl.ds(tile * LANES, LANES)],
                    rows_ref.at[index, tile],
                    sems.at[index, tile],
                )
            )
            copies[-1].start()
    for copy in copies:
        copy.wait()
    for tile in range(cols // LANES):
        head = rows_ref[:, tile, :, 0:DEPTH, :]
        tail = rows_ref[:, tile, :, SUB - DEPTH : SUB, :]
        far_ref[:, :, pl.ds(tile * DEPTH, DEPTH), :] = jnp.where(first, head, tail)


def load_kernel(log_hbm, src_hbm, log_ref, fields_ref, near_ref, sems):
    _, _, rows, cols = log_hbm.shape
    tiles = cols // LANES
    first = even("gx")
    copies = []
    refs = (log_ref, fields_ref.at[0])
    for index, (hbm, ref) in enumerate(zip((log_hbm, src_hbm), refs, strict=True)):
        for tile in range(tiles):
            copies.append(
                pltpu.make_async_copy(
                    hbm.at[0, :, :, pl.ds(tile * LANES, LANES)],
                    ref.at[:, tile, pl.ds(LO, rows), :],
                    sems.at[index, tile],
                )
            )
            copies[-1].start()
    for copy in copies:
        copy.wait()
    for index, ref in enumerate(refs):
        for tile in range(tiles):
            head = ref[:, tile, LO : LO + DEPTH, :]
            tail = ref[:, tile, LO + rows - DEPTH : LO + rows, :]
            near_ref[index, :, pl.ds(tile * DEPTH, DEPTH), :] = jnp.where(first, tail, head)


def pack(blocks_of, lane):
    lanes = lane_ids()
    total = None
    for layer, value in enumerate(blocks_of):
        moved = turn(value, layer * DEPTH - lane)
        total = moved if total is None else jnp.where(lanes // DEPTH == layer, moved, total)
    return total


def put_column_faces(face_y_ref, face_w_ref, layer, place, values):
    lanes = lane_ids()
    first_lane, last_lane = lanes == 0, lanes == LANES - 1
    tiles = len(values)
    moved = [turn(value, -1) for value in values]
    others = [jnp.where(last_lane, moved[tile + 1], moved[tile]) for tile in range(tiles - 1)] + [moved[-1]]
    faces = [reciprocal(value + other) for value, other in zip(values, others, strict=True)]
    faces[-1] = jnp.where(last_lane, 0.0, faces[-1])
    moved = [jnp.zeros((SUB, LANES), F32)] + [turn(face, 1) for face in faces]
    for tile in range(tiles):
        face_y_ref[layer, tile, place, :] = faces[tile]
        face_w_ref[layer, tile, place, :] = jnp.where(first_lane, moved[tile], moved[tile + 1])


def own_kernel(
    log_ref,
    fields_in,
    fields_ref,
    inverse_ref,
    face_x_ref,
    face_y_ref,
    face_z_ref,
    face_w_ref,
    last_ref,
    first_ref,
):
    del fields_in
    layers, tiles, height, _ = log_ref.shape
    rows = height - 3 * SUB
    blocks = rows // SUB
    slots = layers // (LANES // GROUP)
    ring = LO + rows + SUB
    base_ref = fields_ref.at[0]

    def at(block, step=0):
        return pl.ds(LO + block * SUB + step, SUB)

    def fill(layer, _):
        for tile in range(tiles):
            for block in range(blocks):
                value = 0.5 * jnp.exp(-log_ref[layer, tile, at(block), :])
                inverse_ref[layer, tile, at(block), :] = value
                if block == 0:
                    inverse_ref[layer, tile, pl.ds(ring, 1), :] = value[0:1]
        return 0

    lax.fori_loop(0, layers, fill, 0, unroll=slots)

    zero = jnp.zeros((SUB, LANES), F32)
    for tile in range(tiles):
        for block in range(blocks + 1):
            face_z_ref[0, tile, at(block), :] = zero
            face_z_ref[layers, tile, at(block), :] = zero

    def faces(layer, _):
        for block in range(blocks):
            values = [inverse_ref[layer, tile, at(block), :] for tile in range(tiles)]
            put_column_faces(face_y_ref, face_w_ref, layer, at(block), values)
            for tile in range(tiles):
                face_x_ref[layer, tile, at(block), :] = reciprocal(
                    values[tile] + inverse_ref[layer, tile, at(block, 1), :]
                )
        return 0

    lax.fori_loop(0, layers, faces, 0, unroll=slots)

    def faces_z(layer, _):
        for tile in range(tiles):
            for block in range(blocks):
                face_z_ref[layer, tile, at(block), :] = reciprocal(
                    inverse_ref[layer - 1, tile, at(block), :] + inverse_ref[layer, tile, at(block), :]
                )
        return 0

    lax.fori_loop(1, layers, faces_z, 0, unroll=slots)

    base_ref[:, :, pl.ds(ring, 1), :] = base_ref[:, :, pl.ds(LO, 1), :]
    for index, ref in enumerate((log_ref, base_ref)):
        for block in range(blocks):
            part = pl.ds(block * SUB, SUB)
            last_ref[index, part, :] = pack(
                [ref[layer, tiles - 1, at(block), :] for layer in range(layers)], LANES - DEPTH
            )
            first_ref[index, part, :] = pack([ref[layer, 0, at(block), :] for layer in range(layers)], 0)


def edge_kernel(far_in, near_in, last_in, first_in, last_ref, first_ref, near_ref, far_ref, halo_ref):
    del last_in, first_in
    _, layers, tiles, _, _ = halo_ref.shape
    height = last_ref.shape[1]
    one, two = even("gx"), even("gy")
    for tile in range(tiles):
        part = pl.ds(tile * DEPTH, DEPTH)
        near, far = near_in[:, :, part, :], far_in[:, :, part, :]
        halo_ref[:, :, tile, 0:DEPTH, :] = jnp.where(one, near, far)
        halo_ref[:, :, tile, DEPTH:SUB, :] = jnp.where(one, far, near)
    for index in range(2):
        part = pl.ds(height - SUB, SUB)
        last_ref[index, part, :] = pack(
            [halo_ref[index, layer, tiles - 1] for layer in range(layers)], LANES - DEPTH
        )
        first_ref[index, part, :] = pack([halo_ref[index, layer, 0] for layer in range(layers)], 0)
    near_ref[...] = jnp.where(two, last_ref[...], first_ref[...])
    far_ref[...] = jnp.where(two, first_ref[...], last_ref[...])


def place_of(block, step=0):
    return pl.ds(LO + block * SUB + step, SUB)


def close_ring(ref, index, block, blocks, value):
    ring = LO + (blocks + 1) * SUB
    if block == 0:
        ref[(*index, pl.ds(ring, 1), slice(None))] = value[0:1]
    if block == blocks:
        ref[(*index, pl.ds(LO - 1, 1), slice(None))] = value[SUB - 1 : SUB]


def rim_of(values, group):
    return pltpu.roll(values, LANES - 1 - DEPTH - group * GROUP, 1)


def x_part(face_ref, index, old, old_index, block, value):
    there = old[(*old_index, place_of(block, 1), slice(None))]
    back = old[(*old_index, place_of(block, -1), slice(None))]
    return face_ref[(*index, place_of(block), slice(None))] * (value - there) - face_ref[
        (*index, place_of(block, -1), slice(None))
    ] * (back - value)


def inside_masks():
    here_x, here_y = lax.axis_index("gx"), lax.axis_index("gy")
    past_x, before_x = here_x < lax.axis_size("gx") - 1, here_x > 0
    past_y, before_y = here_y < lax.axis_size("gy") - 1, here_y > 0
    place = lane_ids() % GROUP
    inside_rows = jnp.where(row_ids() < DEPTH, past_x.astype(jnp.int32), before_x.astype(jnp.int32)) > 0
    inside_cols = (
        jnp.where(
            (place >= DEPTH) & (place < 2 * DEPTH),
            past_y.astype(jnp.int32),
            jnp.where((place >= 2 * DEPTH) & (place < 3 * DEPTH), before_y.astype(jnp.int32), 1),
        )
        > 0
    )
    return inside_rows, inside_cols


def apply_power(number, fields_ref, face_x_ref, face_y_ref, face_z_ref, face_w_ref, rims_ref):
    _, layers, tiles, height, _ = fields_ref.shape
    blocks = (height - 3 * SUB) // SUB
    slots = layers // (LANES // GROUP)
    old, new = fields_ref.at[number - 1], fields_ref.at[number]
    lanes = lane_ids()
    first_lane, last_lane = lanes == 0, lanes == LANES - 1
    inside_rows, _ = inside_masks()
    at = place_of

    def layer_range(start, count, block):
        levels = []
        for step in range(-1, count + 1):
            layer = start + step
            if step < 0:
                layer = jnp.maximum(layer, 0)
            if step == count:
                layer = jnp.minimum(layer, layers - 1)
            levels.append([old[layer, tile, at(block), :] for tile in range(tiles)])
        ups = [
            [
                face_z_ref[start + step, tile, at(block), :] * (levels[step][tile] - levels[step + 1][tile])
                for tile in range(tiles)
            ]
            for step in range(count + 1)
        ]
        for step in range(count):
            layer = start + step
            values = levels[step + 1]
            ahead = [turn(value, -1) for value in values]
            behind = [turn(value, 1) for value in values]
            rim = None
            if rims_ref is not None:
                rim = rim_of(rims_ref[number - 1, step % slots, at(block), :], start // slots + step // slots)
            out, back = [], []
            for tile in range(tiles):
                other = ahead[tile] if tile == tiles - 1 else jnp.where(last_lane, ahead[tile + 1], ahead[tile])
                out.append(face_y_ref[layer, tile, at(block), :] * (values[tile] - other))
                other = behind[tile] if tile == 0 else jnp.where(first_lane, behind[tile - 1], behind[tile])
                back.append(face_w_ref[layer, tile, at(block), :] * (other - values[tile]))
            if rim is not None:
                out[-1] = jnp.where(last_lane, rim, out[-1])
                back[0] = jnp.where(first_lane, rim, back[0])
            for tile in range(tiles):
                value = values[tile]
                result = (
                    (out[tile] - back[tile])
                    + x_part(face_x_ref, (layer, tile), old, (layer, tile), block, value)
                    + (ups[step + 1][tile] - ups[step][tile])
                )
                if block == blocks:
                    result = jnp.where(inside_rows, result, 0.0)
                new[layer, tile, at(block), :] = result
                if number < DEPTH:
                    close_ring(new, (layer, tile), block, blocks, result)
                yield tile, value, result

    def chunk(group, sums):
        own_sums, next_sums = list(sums[0]), list(sums[1])
        for block in range(blocks):
            for tile, value, result in layer_range(group * CHUNK, CHUNK, block):
                own_sums[tile] = own_sums[tile] + value * value
                next_sums[tile] = next_sums[tile] + value * result
        return tuple(own_sums), tuple(next_sums)

    start = (jnp.zeros((SUB, LANES), F32),) * tiles
    sums = lax.fori_loop(0, layers // CHUNK, chunk, (start, start))
    if number < DEPTH:
        for _ in layer_range(0, layers, blocks):
            pass
    return [functools.reduce(jnp.add, parts) for parts in sums]


def first_kernel(
    halo_ref,
    fields_in,
    inverse_in,
    face_x_in,
    face_y_in,
    face_z_in,
    face_w_in,
    fields_ref,
    inverse_ref,
    face_x_ref,
    face_y_ref,
    face_z_ref,
    face_w_ref,
    parts_ref,
):
    del fields_in, inverse_in, face_x_in, face_y_in, face_z_in, face_w_in
    _, layers, tiles, height, _ = fields_ref.shape
    blocks = (height - 3 * SUB) // SUB
    slots = layers // (LANES // GROUP)
    at = place_of

    def fill(layer, _):
        for tile in range(tiles):
            source = halo_ref[1, layer, tile]
            fields_ref[0, layer, tile, at(blocks), :] = source
            close_ring(fields_ref, (0, layer, tile), blocks, blocks, source)
            inverse_ref[layer, tile, at(blocks), :] = 0.5 * jnp.exp(-halo_ref[0, layer, tile])
        return 0

    lax.fori_loop(0, layers, fill, 0, unroll=2 * slots)

    def faces(layer, _):
        values = [inverse_ref[layer, tile, at(blocks), :] for tile in range(tiles)]
        put_column_faces(face_y_ref, face_w_ref, layer, at(blocks), values)
        for tile in range(tiles):
            for block in (blocks - 1, blocks):
                face = reciprocal(
                    inverse_ref[layer, tile, at(block), :] + inverse_ref[layer, tile, at(block, 1), :]
                )
                face_x_ref[layer, tile, at(block), :] = face
                close_ring(face_x_ref, (layer, tile), block, blocks, face)
            before = inverse_ref[jnp.maximum(layer - 1, 0), tile, at(blocks), :]
            face_z_ref[layer, tile, at(blocks), :] = jnp.where(layer > 0, reciprocal(before + values[tile]), 0.0)
        return 0

    lax.fori_loop(0, layers, faces, 0, unroll=2 * slots)
    found = apply_power(1, fields_ref, face_x_ref, face_y_ref, face_z_ref, face_w_ref, None)
    for which, part in enumerate(found):
        parts_ref[which] = part


def basis_kernel(
    last_ref,
    first_ref,
    far_ref,
    near_ref,
    parts_ref,
    face_x_ref,
    face_y_ref,
    face_z_ref,
    face_w_ref,
    fields_in,
    fields_ref,
    rims_ref,
    sums_ref,
    strip_ref,
    strip_inv_ref,
    strip_x_ref,
    strip_y_ref,
    strip_z_ref,
):
    del fields_in
    _, layers, tiles, height, _ = fields_ref.shape
    rows = height - 3 * SUB
    slots = layers // (LANES // GROUP)
    groups = layers // slots
    blocks = rows // SUB
    lanes = lane_ids()
    place = lanes % GROUP
    inside_rows, inside_cols = inside_masks()
    inside_both = inside_rows & inside_cols
    first_lane, last_lane = lanes == 0, lanes == LANES - 1
    first_y = even("gy")
    at = place_of

    def spread(index, block):
        part = pl.ds(block * SUB, SUB)
        near, far = near_ref[index, part, :], far_ref[index, part, :]
        packed = (
            last_ref[index, part, :],
            jnp.where(first_y, near, far),
            jnp.where(first_y, far, near),
            first_ref[index, part, :],
        )
        found = []
        for slot in range(slots):
            moved = [turn(value, (kind - slot) * DEPTH) for kind, value in enumerate(packed)]
            found.append(
                jnp.where(
                    place < 2 * DEPTH,
                    jnp.where(place < DEPTH, moved[0], moved[1]),
                    jnp.where(place < 3 * DEPTH, moved[2], moved[3]),
                )
            )
        return found

    def put_strip(ref, block, values):
        ref[0, at(block), :] = turn(values[-1], GROUP)
        ref[slots + 1, at(block), :] = turn(values[0], -GROUP)
        for slot, value in enumerate(values):
            ref[slot + 1, at(block), :] = value
            close_ring(ref, (slot + 1,), block, blocks, value)

    for block in range(blocks + 1):
        put_strip(strip_ref.at[0], block, spread(1, block))
        values = [0.5 * jnp.exp(-value) for value in spread(0, block)]
        put_strip(strip_inv_ref, block, values)
    top, bottom = lanes >= LANES - GROUP, lanes < GROUP
    for block in range(blocks + 1):
        for slot in range(1, slots + 1):
            value = strip_inv_ref[slot, at(block), :]
            face = reciprocal(value + strip_inv_ref[slot, at(block, 1), :])
            strip_x_ref[slot - 1, at(block), :] = face
            close_ring(strip_x_ref, (slot - 1,), block, blocks, face)
            strip_y_ref[slot - 1, at(block), :] = reciprocal(value + turn(value, -1))
        for slot in range(slots + 1):
            face = reciprocal(strip_inv_ref[slot, at(block), :] + strip_inv_ref[slot + 1, at(block), :])
            if slot == 0:
                face = jnp.where(bottom, 0.0, face)
            if slot == slots:
                face = jnp.where(top, 0.0, face)
            strip_z_ref[slot, at(block), :] = face

    for power in range(1, DEPTH + 1):
        old = strip_ref.at[power - 1]
        for block in range(blocks + 1):
            levels = [old[slot, at(block), :] for slot in range(slots + 2)]
            ups = [
                strip_z_ref[slot, at(block), :] * (levels[slot] - levels[slot + 1]) for slot in range(slots + 1)
            ]
            values = []
            for slot in range(slots):
                value = levels[slot + 1]
                flux = strip_y_ref[slot, at(block), :] * (value - turn(value, -1))
                after = turn(flux, 1)
                rims_ref[power - 1, slot, at(block), :] = jnp.where(
                    place == DEPTH, after, turn(flux, 2 - 2 * DEPTH)
                )
                if power < DEPTH:
                    result = (
                        (flux - after)
                        + x_part(strip_x_ref, (slot,), old, (slot + 1,), block, value)
                        + (ups[slot + 1] - ups[slot])
                    )
                    values.append(jnp.where(inside_both if block == blocks else inside_cols, result, 0.0))
            if power < DEPTH:
                put_strip(strip_ref.at[power], block, values)

    zero = jnp.zeros((SUB, LANES), F32)

    def complete(group, lost):
        for slot in range(slots):
            layer = group * slots + slot
            for block in range(blocks + 1):
                rim = rim_of(rims_ref[0, slot, at(block), :], group)
                for tile, part in ((0, jnp.where(first_lane, -rim, 0.0)), (tiles - 1, jnp.where(last_lane, rim, 0.0))):
                    value = fields_ref[1, layer, tile, at(block), :] + part
                    fields_ref[1, layer, tile, at(block), :] = value
                    close_ring(fields_ref, (1, layer, tile), block, blocks, value)
                    if block < blocks:
                        lost = lost + part * fields_ref[0, layer, tile, at(block), :]
        return lost

    lost = lax.fori_loop(0, groups, complete, zero, unroll=4)

    found = [parts_ref[0], parts_ref[1] + lost]
    for number in range(2, DEPTH + 1):
        found += apply_power(number, fields_ref, face_x_ref, face_y_ref, face_z_ref, face_w_ref, rims_ref)
    total = jnp.concatenate([jnp.sum(part, axis=0, keepdims=True) for part in found], axis=0)
    total = total.T
    total, rest = pair_total([(total[k : k + SUB], None) for k in range(0, LANES, SUB)])
    row = jnp.concatenate([total[0:1], rest[0:1], jnp.zeros((1, LANES - 4 * DEPTH), F32)], axis=1)
    sums_ref[...] = jnp.broadcast_to(row, sums_ref.shape)


def two_sum(first, second):
    total = first + second
    part = total - first
    return total, (first - (total - part)) + (second - part)


def pair_total(terms):
    while len(terms) > 1:
        merged = []
        for (high, low), (other, other_low) in zip(terms[::2], terms[1::2], strict=True):
            total, lost = two_sum(high, other)
            merged.append((total, lost if low is None else lost + (low + other_low)))
        terms = merged
    total, rest = terms[0]
    step = SUB // 2
    while step:
        total, lost = two_sum(total, pltpu.roll(total, step, 0))
        rest = rest + pltpu.roll(rest, step, 0) + lost
        step //= 2
    return total, rest


def quick_sum(first, second):
    total = first + second
    return total, second - (total - first)


def halves(value):
    scaled = 4097.0 * value
    high = scaled - (scaled - value)
    return high, value - high


def two_product(first, second):
    total = first * second
    first_high, first_low = halves(first)
    second_high, second_low = halves(second)
    rest = ((first_high * second_high - total) + first_high * second_low + first_low * second_high) + (
        first_low * second_low
    )
    return total, rest


def pair_add(first, second):
    total, rest = two_sum(first[0], second[0])
    return quick_sum(total, rest + (first[1] + second[1]))


def pair_sub(first, second):
    return pair_add(first, (-second[0], -second[1]))


def pair_mul(first, second):
    total, rest = two_product(first[0], second[0])
    return quick_sum(total, rest + (first[0] * second[1] + first[1] * second[0]))


def pair_div(first, second):
    guess = first[0] / second[0]
    total, rest = two_product(guess, second[0])
    left = ((first[0] - total) - rest) + (first[1] - guess * second[1])
    return quick_sum(guess, left / second[0])


def galerkin(moments):
    count = DEPTH
    matrix = {(i, j): moments[i + j + 1] for i in range(count) for j in range(i + 1)}
    right = [moments[i] for i in range(count)]
    for pivot in range(count):
        for i in range(pivot + 1, count):
            ratio = pair_div(matrix[i, pivot], matrix[pivot, pivot])
            for j in range(pivot + 1, i + 1):
                matrix[i, j] = pair_sub(matrix[i, j], pair_mul(ratio, matrix[j, pivot]))
            right[i] = pair_sub(right[i], pair_mul(ratio, right[pivot]))
    found = [None] * count
    for i in reversed(range(count)):
        value = right[i]
        for j in range(i + 1, count):
            value = pair_sub(value, pair_mul(matrix[j, i], found[j]))
        found[i] = pair_div(value, matrix[i, i])
    return [value[0] for value in found]


def finish_kernel(
    sums_ref,
    fields_ref,
    face_x_ref,
    face_y_ref,
    rims_ref,
    pressure_hbm,
    residual_hbm,
    east_hbm,
    north_hbm,
    pressure_ref,
    residual_ref,
    east_ref,
    north_ref,
    field_ref,
    sems,
):
    _, layers, tiles, height, _ = fields_ref.shape
    rows = height - 3 * SUB
    slots = layers // (LANES // GROUP)
    blocks = rows // SUB
    last_lane = lane_ids() == LANES - 1

    peers = sums_ref.shape[0]
    total, rest = pair_total([(sums_ref[k : k + SUB, :], None) for k in range(0, peers, SUB)])
    total, rest = quick_sum(total, rest + turn(total, -2 * DEPTH))
    moments = [
        tuple(jnp.broadcast_to(value[:, k : k + 1], (SUB, LANES)) for value in (total, rest)) for k in range(2 * DEPTH)
    ]
    coefs = galerkin(moments)

    def at(block, step=0):
        return pl.ds(LO + block * SUB + step, SUB)

    def mix(values):
        return functools.reduce(jnp.add, [coef * value for coef, value in zip(coefs, values, strict=True)])

    outs = (
        (pressure_ref, pressure_hbm),
        (residual_ref, residual_hbm),
        (east_ref, east_hbm),
        (north_ref, north_hbm),
    )

    def copies(group):
        part = pl.ds(group * slots, slots)
        return [
            pltpu.make_async_copy(ref.at[part], hbm.at[0, part], sems.at[index, group])
            for index, (ref, hbm) in enumerate(outs)
        ]

    def chunk(group, _):
        for slot in range(slots):
            layer = group * slots + slot
            for block in range(blocks + 1):
                values = []
                for tile in range(tiles):
                    found = [
                        fields_ref[power, layer, tile, at(block), :] for power in range(DEPTH + (block < blocks))
                    ]
                    value = mix(found[:DEPTH])
                    values.append(value)
                    field_ref[tile, at(block), :] = value
                    if block < blocks:
                        spot = (layer, pl.ds(block * SUB, SUB), pl.ds(tile * LANES, LANES))
                        pressure_ref[spot] = value
                        residual_ref[spot] = found[0] - mix(found[1:])
                if block < blocks:
                    rim = mix([rims_ref[power, slot, at(block), :] for power in range(DEPTH)])
                    rim = rim_of(rim, group)
                    moved = [turn(value, -1) for value in values]
                    for tile in range(tiles):
                        other = moved[tile]
                        if tile < tiles - 1:
                            other = jnp.where(last_lane, moved[tile + 1], other)
                        flux = face_y_ref[layer, tile, at(block), :] * (values[tile] - other)
                        if tile == tiles - 1:
                            flux = jnp.where(last_lane, rim, flux)
                        spot = (layer, pl.ds(block * SUB, SUB), pl.ds(tile * LANES, LANES))
                        north_ref[spot] = flux
            for block in range(blocks):
                for tile in range(tiles):
                    spot = (layer, pl.ds(block * SUB, SUB), pl.ds(tile * LANES, LANES))
                    east_ref[spot] = face_x_ref[layer, tile, at(block), :] * (
                        field_ref[tile, at(block), :] - field_ref[tile, at(block, 1), :]
                    )
        for copy in copies(group):
            copy.start()
        return 0

    lax.fori_loop(0, layers // slots, chunk, 0)

    def drain(group, _):
        for copy in copies(group):
            copy.wait()
        return 0

    lax.fori_loop(0, layers // slots, drain, 0)


def exchange(value, axis, near):
    count = lax.axis_size(axis)
    pairs = []
    for i in range(count):
        other = i + 1 if (i % 2 == 0) == near else i - 1
        if 0 <= other < count:
            pairs.append((i, other))
    return lax.ppermute(value, axis, pairs)


def on_device(log_perm, source):
    _, layers, rows, cols = log_perm.shape
    tiles, slots = cols // LANES, layers // (LANES // GROUP)
    height = rows + 3 * SUB
    full = (layers, tiles, height, LANES)
    deep = (layers + 1, tiles, height, LANES)
    spare = (layers + SPARE, tiles, height, LANES)
    ends = (2, layers, tiles * DEPTH, LANES)
    edges = (2, rows + SUB, LANES)
    strip = (slots + 2, height, LANES)
    inner = (slots, height, LANES)
    peers = lax.axis_size("gx") * lax.axis_size("gy")
    cells = layers * rows * cols

    log_perm, source = (pltpu.with_memory_space_constraint(value, pltpu.HBM) for value in (log_perm, source))
    powers = (in_vmem(DEPTH + 1, *full), in_vmem(*spare)) + (in_vmem(*full),) * 2 + (in_vmem(*deep), in_vmem(*full))
    far = pl.pallas_call(
        far_kernel,
        out_shape=in_vmem(*ends),
        in_specs=[HBM_SPEC] * 2,
        out_specs=VMEM_SPEC,
        scratch_shapes=[in_vmem(2, tiles, layers, SUB, LANES), pltpu.SemaphoreType.DMA((2, tiles))],
        compiler_params=params(16),
        name="far",
    )(log_perm, source)
    far = exchange(far, "gx", False)
    log_own, fields, near = pl.pallas_call(
        load_kernel,
        out_shape=(in_vmem(*full), powers[0], in_vmem(*ends)),
        in_specs=[HBM_SPEC] * 2,
        out_specs=[VMEM_SPEC] * 3,
        scratch_shapes=[pltpu.SemaphoreType.DMA((2, tiles))],
        compiler_params=params(16),
        cost_estimate=pl.CostEstimate(flops=cells, bytes_accessed=8 * cells, transcendentals=0),
        name="load",
    )(log_perm, source)
    near = exchange(near, "gx", True)
    *fields, last, first = pl.pallas_call(
        own_kernel,
        out_shape=powers + (in_vmem(*edges),) * 2,
        in_specs=[VMEM_SPEC] * 2,
        out_specs=[VMEM_SPEC] * 8,
        input_output_aliases={1: 0},
        compiler_params=params(16),
        cost_estimate=pl.CostEstimate(flops=60 * cells, bytes_accessed=8 * cells, transcendentals=4 * cells),
        name="own",
    )(log_own, fields)
    last, first, near, far, halo = pl.pallas_call(
        edge_kernel,
        out_shape=(in_vmem(*edges),) * 4 + (in_vmem(2, layers, tiles, SUB, LANES),),
        in_specs=[VMEM_SPEC] * 4,
        out_specs=[VMEM_SPEC] * 5,
        input_output_aliases={2: 0, 3: 1},
        compiler_params=params(16),
        name="edges",
    )(far, near, last, first)
    far = exchange(far, "gy", False)
    near = exchange(near, "gy", True)
    fields, _, face_x, face_y, face_z, face_w, parts = pl.pallas_call(
        first_kernel,
        out_shape=powers + (in_vmem(2, SUB, LANES),),
        in_specs=[VMEM_SPEC] * 7,
        out_specs=[VMEM_SPEC] * 7,
        input_output_aliases={1: 0, 2: 1, 3: 2, 4: 3, 5: 4, 6: 5},
        compiler_params=params(16),
        cost_estimate=pl.CostEstimate(flops=40 * cells, bytes_accessed=8 * cells, transcendentals=cells),
        name="first",
    )(halo, *fields)
    fields, rims, sums = pl.pallas_call(
        basis_kernel,
        out_shape=(powers[0], in_vmem(DEPTH, *inner), in_vmem(peers, LANES)),
        in_specs=[VMEM_SPEC] * 10,
        out_specs=[VMEM_SPEC] * 3,
        input_output_aliases={9: 0},
        scratch_shapes=[
            in_vmem(DEPTH, *strip),
            in_vmem(*strip),
            in_vmem(*inner),
            in_vmem(*inner),
            in_vmem(slots + 1, height, LANES),
        ],
        compiler_params=params(16),
        name="basis",
    )(last, first, far, near, parts, face_x, face_y, face_z, face_w, fields)
    sums = lax.all_to_all(sums, ("gx", "gy"), 0, 0, tiled=True)
    block = (layers, rows, cols)
    return pl.pallas_call(
        finish_kernel,
        out_shape=(jax.ShapeDtypeStruct((1, *block), F32),) * 4,
        in_specs=[VMEM_SPEC] * 5,
        out_specs=[ANY_SPEC] * 4,
        scratch_shapes=[in_vmem(*block)] * 4
        + [in_vmem(tiles, height, LANES), pltpu.SemaphoreType.DMA((4, layers // slots))],
        compiler_params=params(16),
        name="finish",
    )(sums, fields, face_x, face_y, rims)


def solution(mesh):
    spec = P(None, None, "gx", "gy")
    return jax.shard_map(on_device, mesh=mesh, in_specs=(spec,) * 2, out_specs=(spec,) * 4, check_vma=False)
```

```python
import functools

import jax
import jax.numpy as jnp
from jax import lax
from jax.experimental import pallas as pl
from jax.experimental.pallas import tpu as pltpu
from jax.sharding import PartitionSpec as P

DEPTH = 4
LANES = 128
SUB = 8
LO = 8
GROUP = 4 * DEPTH
CHUNK = 8
SPARE = 3
F32 = jnp.float32
HBM_SPEC = pl.BlockSpec(memory_space=pltpu.HBM)
VMEM_SPEC = pl.BlockSpec(memory_space=pltpu.VMEM)
ANY_SPEC = pl.BlockSpec(memory_space=pl.ANY)


def in_vmem(*shape):
    return pltpu.VMEM(shape, F32)


def params(limit):
    return pltpu.CompilerParams(vmem_limit_bytes=limit * 1024 * 1024)


def lane_ids():
    return lax.broadcasted_iota(jnp.int32, (SUB, LANES), 1)


def row_ids():
    return lax.broadcasted_iota(jnp.int32, (SUB, LANES), 0)


def turn(value, shift):
    return pltpu.roll(value, shift % LANES, 1) if shift % LANES else value


def reciprocal(value):
    return 1.0 / value


def even(axis):
    return lax.rem(lax.axis_index(axis), 2) == 0


def far_kernel(log_hbm, src_hbm, far_ref, rows_ref, sems):
    _, _, rows, cols = log_hbm.shape
    first = even("gx")
    start = pl.multiple_of(jnp.where(first, 0, rows - SUB), SUB)
    copies = []
    for index, hbm in enumerate((log_hbm, src_hbm)):
        for tile in range(cols // LANES):
            copies.append(
                pltpu.make_async_copy(
                    hbm.at[0, :, pl.ds(start, SUB), pl.ds(tile * LANES, LANES)],
                    rows_ref.at[index, tile],
                    sems.at[index, tile],
                )
            )
            copies[-1].start()
    for copy in copies:
        copy.wait()
    for tile in range(cols // LANES):
        head = rows_ref[:, tile, :, 0:DEPTH, :]
        tail = rows_ref[:, tile, :, SUB - DEPTH : SUB, :]
        far_ref[:, :, pl.ds(tile * DEPTH, DEPTH), :] = jnp.where(first, head, tail)


def load_kernel(log_hbm, src_hbm, log_ref, fields_ref, near_ref, sems):
    _, _, rows, cols = log_hbm.shape
    tiles = cols // LANES
    first = even("gx")
    copies = []
    refs = (log_ref, fields_ref.at[0])
    for index, (hbm, ref) in enumerate(zip((log_hbm, src_hbm), refs, strict=True)):
        for tile in range(tiles):
            copies.append(
                pltpu.make_async_copy(
                    hbm.at[0, :, :, pl.ds(tile * LANES, LANES)],
                    ref.at[:, tile, pl.ds(LO, rows), :],
                    sems.at[index, tile],
                )
            )
            copies[-1].start()
    for copy in copies:
        copy.wait()
    for index, ref in enumerate(refs):
        for tile in range(tiles):
            head = ref[:, tile, LO : LO + DEPTH, :]
            tail = ref[:, tile, LO + rows - DEPTH : LO + rows, :]
            near_ref[index, :, pl.ds(tile * DEPTH, DEPTH), :] = jnp.where(first, tail, head)


def pack(blocks_of, lane):
    lanes = lane_ids()
    total = None
    for layer, value in enumerate(blocks_of):
        moved = turn(value, layer * DEPTH - lane)
        total = moved if total is None else jnp.where(lanes // DEPTH == layer, moved, total)
    return total


def put_column_faces(face_y_ref, face_w_ref, layer, place, values):
    lanes = lane_ids()
    first_lane, last_lane = lanes == 0, lanes == LANES - 1
    tiles = len(values)
    moved = [turn(value, -1) for value in values]
    others = [jnp.where(last_lane, moved[tile + 1], moved[tile]) for tile in range(tiles - 1)] + [moved[-1]]
    faces = [reciprocal(value + other) for value, other in zip(values, others, strict=True)]
    faces[-1] = jnp.where(last_lane, 0.0, faces[-1])
    moved = [jnp.zeros((SUB, LANES), F32)] + [turn(face, 1) for face in faces]
    for tile in range(tiles):
        face_y_ref[layer, tile, place, :] = faces[tile]
        face_w_ref[layer, tile, place, :] = jnp.where(first_lane, moved[tile], moved[tile + 1])


def own_kernel(
    log_ref,
    fields_in,
    fields_ref,
    inverse_ref,
    face_x_ref,
    face_y_ref,
    face_z_ref,
    face_w_ref,
    last_ref,
    first_ref,
):
    del fields_in
    layers, tiles, height, _ = log_ref.shape
    rows = height - 3 * SUB
    blocks = rows // SUB
    slots = layers // (LANES // GROUP)
    ring = LO + rows + SUB
    base_ref = fields_ref.at[0]

    def at(block, step=0):
        return pl.ds(LO + block * SUB + step, SUB)

    def fill(layer, _):
        for tile in range(tiles):
            for block in range(blocks):
                value = 0.5 * jnp.exp(-log_ref[layer, tile, at(block), :])
                inverse_ref[layer, tile, at(block), :] = value
                if block == 0:
                    inverse_ref[layer, tile, pl.ds(ring, 1), :] = value[0:1]
        return 0

    lax.fori_loop(0, layers, fill, 0, unroll=slots)

    zero = jnp.zeros((SUB, LANES), F32)
    for tile in range(tiles):
        for block in range(blocks + 1):
            face_z_ref[0, tile, at(block), :] = zero
            face_z_ref[layers, tile, at(block), :] = zero

    def faces(layer, _):
        for block in range(blocks):
            values = [inverse_ref[layer, tile, at(block), :] for tile in range(tiles)]
            put_column_faces(face_y_ref, face_w_ref, layer, at(block), values)
            for tile in range(tiles):
                face_x_ref[layer, tile, at(block), :] = reciprocal(
                    values[tile] + inverse_ref[layer, tile, at(block, 1), :]
                )
        return 0

    lax.fori_loop(0, layers, faces, 0, unroll=slots)

    def faces_z(layer, _):
        for tile in range(tiles):
            for block in range(blocks):
                face_z_ref[layer, tile, at(block), :] = reciprocal(
                    inverse_ref[layer - 1, tile, at(block), :] + inverse_ref[layer, tile, at(block), :]
                )
        return 0

    lax.fori_loop(1, layers, faces_z, 0, unroll=slots)

    base_ref[:, :, pl.ds(ring, 1), :] = base_ref[:, :, pl.ds(LO, 1), :]
    for index, ref in enumerate((log_ref, base_ref)):
        for block in range(blocks):
            part = pl.ds(block * SUB, SUB)
            last_ref[index, part, :] = pack(
                [ref[layer, tiles - 1, at(block), :] for layer in range(layers)], LANES - DEPTH
            )
            first_ref[index, part, :] = pack([ref[layer, 0, at(block), :] for layer in range(layers)], 0)


def edge_kernel(far_in, near_in, last_in, first_in, last_ref, first_ref, near_ref, far_ref, halo_ref):
    del last_in, first_in
    _, layers, tiles, _, _ = halo_ref.shape
    height = last_ref.shape[1]
    one, two = even("gx"), even("gy")
    for tile in range(tiles):
        part = pl.ds(tile * DEPTH, DEPTH)
        near, far = near_in[:, :, part, :], far_in[:, :, part, :]
        halo_ref[:, :, tile, 0:DEPTH, :] = jnp.where(one, near, far)
        halo_ref[:, :, tile, DEPTH:SUB, :] = jnp.where(one, far, near)
    for index in range(2):
        part = pl.ds(height - SUB, SUB)
        last_ref[index, part, :] = pack(
            [halo_ref[index, layer, tiles - 1] for layer in range(layers)], LANES - DEPTH
        )
        first_ref[index, part, :] = pack([halo_ref[index, layer, 0] for layer in range(layers)], 0)
    near_ref[...] = jnp.where(two, last_ref[...], first_ref[...])
    far_ref[...] = jnp.where(two, first_ref[...], last_ref[...])


def place_of(block, step=0):
    return pl.ds(LO + block * SUB + step, SUB)


def close_ring(ref, index, block, blocks, value):
    ring = LO + (blocks + 1) * SUB
    if block == 0:
        ref[(*index, pl.ds(ring, 1), slice(None))] = value[0:1]
    if block == blocks:
        ref[(*index, pl.ds(LO - 1, 1), slice(None))] = value[SUB - 1 : SUB]


def rim_of(values, group):
    return pltpu.roll(values, LANES - 1 - DEPTH - group * GROUP, 1)


def x_part(face_ref, index, old, old_index, block, value):
    there = old[(*old_index, place_of(block, 1), slice(None))]
    back = old[(*old_index, place_of(block, -1), slice(None))]
    return face_ref[(*index, place_of(block), slice(None))] * (value - there) - face_ref[
        (*index, place_of(block, -1), slice(None))
    ] * (back - value)


def inside_masks():
    here_x, here_y = lax.axis_index("gx"), lax.axis_index("gy")
    past_x, before_x = here_x < lax.axis_size("gx") - 1, here_x > 0
    past_y, before_y = here_y < lax.axis_size("gy") - 1, here_y > 0
    place = lane_ids() % GROUP
    inside_rows = jnp.where(row_ids() < DEPTH, past_x.astype(jnp.int32), before_x.astype(jnp.int32)) > 0
    inside_cols = (
        jnp.where(
            (place >= DEPTH) & (place < 2 * DEPTH),
            past_y.astype(jnp.int32),
            jnp.where((place >= 2 * DEPTH) & (place < 3 * DEPTH), before_y.astype(jnp.int32), 1),
        )
        > 0
    )
    return inside_rows, inside_cols


def apply_power(number, fields_ref, face_x_ref, face_y_ref, face_z_ref, face_w_ref, rims_ref):
    _, layers, tiles, height, _ = fields_ref.shape
    blocks = (height - 3 * SUB) // SUB
    slots = layers // (LANES // GROUP)
    old, new = fields_ref.at[number - 1], fields_ref.at[number]
    lanes = lane_ids()
    first_lane, last_lane = lanes == 0, lanes == LANES - 1
    inside_rows, _ = inside_masks()
    at = place_of

    def layer_range(start, count, block):
        levels = []
        for step in range(-1, count + 1):
            layer = start + step
            if step < 0:
                layer = jnp.maximum(layer, 0)
            if step == count:
                layer = jnp.minimum(layer, layers - 1)
            levels.append([old[layer, tile, at(block), :] for tile in range(tiles)])
        ups = [
            [
                face_z_ref[start + step, tile, at(block), :] * (levels[step][tile] - levels[step + 1][tile])
                for tile in range(tiles)
            ]
            for step in range(count + 1)
        ]
        for step in range(count):
            layer = start + step
            values = levels[step + 1]
            ahead = [turn(value, -1) for value in values]
            behind = [turn(value, 1) for value in values]
            rim = None
            if rims_ref is not None:
                rim = rim_of(rims_ref[number - 1, step % slots, at(block), :], start // slots + step // slots)
            out, back = [], []
            for tile in range(tiles):
                other = ahead[tile] if tile == tiles - 1 else jnp.where(last_lane, ahead[tile + 1], ahead[tile])
                out.append(face_y_ref[layer, tile, at(block), :] * (values[tile] - other))
                other = behind[tile] if tile == 0 else jnp.where(first_lane, behind[tile - 1], behind[tile])
                back.append(face_w_ref[layer, tile, at(block), :] * (other - values[tile]))
            if rim is not None:
                out[-1] = jnp.where(last_lane, rim, out[-1])
                back[0] = jnp.where(first_lane, rim, back[0])
            for tile in range(tiles):
                value = values[tile]
                result = (
                    (out[tile] - back[tile])
                    + x_part(face_x_ref, (layer, tile), old, (layer, tile), block, value)
                    + (ups[step + 1][tile] - ups[step][tile])
                )
                if block == blocks:
                    result = jnp.where(inside_rows, result, 0.0)
                new[layer, tile, at(block), :] = result
                if number < DEPTH:
                    close_ring(new, (layer, tile), block, blocks, result)
                yield tile, value, result

    def chunk(group, sums):
        own_sums, next_sums = list(sums[0]), list(sums[1])
        for block in range(blocks):
            for tile, value, result in layer_range(group * CHUNK, CHUNK, block):
                own_sums[tile] = own_sums[tile] + value * value
                next_sums[tile] = next_sums[tile] + value * result
        return tuple(own_sums), tuple(next_sums)

    start = (jnp.zeros((SUB, LANES), F32),) * tiles
    sums = lax.fori_loop(0, layers // CHUNK, chunk, (start, start))
    if number < DEPTH:
        for _ in layer_range(0, layers, blocks):
            pass
    return [functools.reduce(jnp.add, parts) for parts in sums]


def first_kernel(
    halo_ref,
    fields_in,
    inverse_in,
    face_x_in,
    face_y_in,
    face_z_in,
    face_w_in,
    fields_ref,
    inverse_ref,
    face_x_ref,
    face_y_ref,
    face_z_ref,
    face_w_ref,
    parts_ref,
):
    del fields_in, inverse_in, face_x_in, face_y_in, face_z_in, face_w_in
    _, layers, tiles, height, _ = fields_ref.shape
    blocks = (height - 3 * SUB) // SUB
    slots = layers // (LANES // GROUP)
    at = place_of

    def fill(layer, _):
        for tile in range(tiles):
            source = halo_ref[1, layer, tile]
            fields_ref[0, layer, tile, at(blocks), :] = source
            close_ring(fields_ref, (0, layer, tile), blocks, blocks, source)
            inverse_ref[layer, tile, at(blocks), :] = 0.5 * jnp.exp(-halo_ref[0, layer, tile])
        return 0

    lax.fori_loop(0, layers, fill, 0, unroll=layers)

    def faces(layer, _):
        values = [inverse_ref[layer, tile, at(blocks), :] for tile in range(tiles)]
        put_column_faces(face_y_ref, face_w_ref, layer, at(blocks), values)
        for tile in range(tiles):
            for block in (blocks - 1, blocks):
                face = reciprocal(
                    inverse_ref[layer, tile, at(block), :] + inverse_ref[layer, tile, at(block, 1), :]
                )
                face_x_ref[layer, tile, at(block), :] = face
                close_ring(face_x_ref, (layer, tile), block, blocks, face)
            before = inverse_ref[jnp.maximum(layer - 1, 0), tile, at(blocks), :]
            face_z_ref[layer, tile, at(blocks), :] = jnp.where(layer > 0, reciprocal(before + values[tile]), 0.0)
        return 0

    lax.fori_loop(0, layers, faces, 0, unroll=4 * slots)
    found = apply_power(1, fields_ref, face_x_ref, face_y_ref, face_z_ref, face_w_ref, None)
    for which, part in enumerate(found):
        parts_ref[which] = part


def basis_kernel(
    last_ref,
    first_ref,
    far_ref,
    near_ref,
    parts_ref,
    face_x_ref,
    face_y_ref,
    face_z_ref,
    face_w_ref,
    fields_in,
    fields_ref,
    rims_ref,
    sums_ref,
    strip_ref,
    strip_inv_ref,
    strip_x_ref,
    strip_y_ref,
    strip_z_ref,
):
    del fields_in
    _, layers, tiles, height, _ = fields_ref.shape
    rows = height - 3 * SUB
    slots = layers // (LANES // GROUP)
    groups = layers // slots
    blocks = rows // SUB
    lanes = lane_ids()
    place = lanes % GROUP
    inside_rows, inside_cols = inside_masks()
    inside_both = inside_rows & inside_cols
    first_lane, last_lane = lanes == 0, lanes == LANES - 1
    first_y = even("gy")
    at = place_of

    def spread(index, block):
        part = pl.ds(block * SUB, SUB)
        near, far = near_ref[index, part, :], far_ref[index, part, :]
        packed = (
            last_ref[index, part, :],
            jnp.where(first_y, near, far),
            jnp.where(first_y, far, near),
            first_ref[index, part, :],
        )
        found = []
        for slot in range(slots):
            moved = [turn(value, (kind - slot) * DEPTH) for kind, value in enumerate(packed)]
            found.append(
                jnp.where(
                    place < 2 * DEPTH,
                    jnp.where(place < DEPTH, moved[0], moved[1]),
                    jnp.where(place < 3 * DEPTH, moved[2], moved[3]),
                )
            )
        return found

    def put_strip(ref, block, values):
        ref[0, at(block), :] = turn(values[-1], GROUP)
        ref[slots + 1, at(block), :] = turn(values[0], -GROUP)
        for slot, value in enumerate(values):
            ref[slot + 1, at(block), :] = value
            close_ring(ref, (slot + 1,), block, blocks, value)

    for block in range(blocks + 1):
        put_strip(strip_ref.at[0], block, spread(1, block))
        values = [0.5 * jnp.exp(-value) for value in spread(0, block)]
        put_strip(strip_inv_ref, block, values)
    top, bottom = lanes >= LANES - GROUP, lanes < GROUP
    for block in range(blocks + 1):
        for slot in range(1, slots + 1):
            value = strip_inv_ref[slot, at(block), :]
            face = reciprocal(value + strip_inv_ref[slot, at(block, 1), :])
            strip_x_ref[slot - 1, at(block), :] = face
            close_ring(strip_x_ref, (slot - 1,), block, blocks, face)
            strip_y_ref[slot - 1, at(block), :] = reciprocal(value + turn(value, -1))
        for slot in range(slots + 1):
            face = reciprocal(strip_inv_ref[slot, at(block), :] + strip_inv_ref[slot + 1, at(block), :])
            if slot == 0:
                face = jnp.where(bottom, 0.0, face)
            if slot == slots:
                face = jnp.where(top, 0.0, face)
            strip_z_ref[slot, at(block), :] = face

    for power in range(1, DEPTH + 1):
        old = strip_ref.at[power - 1]
        for block in range(blocks + 1):
            levels = [old[slot, at(block), :] for slot in range(slots + 2)]
            ups = [
                strip_z_ref[slot, at(block), :] * (levels[slot] - levels[slot + 1]) for slot in range(slots + 1)
            ]
            values = []
            for slot in range(slots):
                value = levels[slot + 1]
                flux = strip_y_ref[slot, at(block), :] * (value - turn(value, -1))
                after = turn(flux, 1)
                rims_ref[power - 1, slot, at(block), :] = jnp.where(
                    place == DEPTH, after, turn(flux, 2 - 2 * DEPTH)
                )
                if power < DEPTH:
                    result = (
                        (flux - after)
                        + x_part(strip_x_ref, (slot,), old, (slot + 1,), block, value)
                        + (ups[slot + 1] - ups[slot])
                    )
                    values.append(jnp.where(inside_both if block == blocks else inside_cols, result, 0.0))
            if power < DEPTH:
                put_strip(strip_ref.at[power], block, values)

    zero = jnp.zeros((SUB, LANES), F32)

    def complete(group, lost):
        for slot in range(slots):
            layer = group * slots + slot
            for block in range(blocks + 1):
                rim = rim_of(rims_ref[0, slot, at(block), :], group)
                for tile, part in ((0, jnp.where(first_lane, -rim, 0.0)), (tiles - 1, jnp.where(last_lane, rim, 0.0))):
                    value = fields_ref[1, layer, tile, at(block), :] + part
                    fields_ref[1, layer, tile, at(block), :] = value
                    close_ring(fields_ref, (1, layer, tile), block, blocks, value)
                    if block < blocks:
                        lost = lost + part * fields_ref[0, layer, tile, at(block), :]
        return lost

    lost = lax.fori_loop(0, groups, complete, zero, unroll=4)

    found = [parts_ref[0], parts_ref[1] + lost]
    for number in range(2, DEPTH + 1):
        found += apply_power(number, fields_ref, face_x_ref, face_y_ref, face_z_ref, face_w_ref, rims_ref)
    total = jnp.concatenate([jnp.sum(part, axis=0, keepdims=True) for part in found], axis=0)
    total = total.T
    total, rest = pair_total([(total[k : k + SUB], None) for k in range(0, LANES, SUB)])
    row = jnp.concatenate([total[0:1], rest[0:1], jnp.zeros((1, LANES - 4 * DEPTH), F32)], axis=1)
    sums_ref[...] = jnp.broadcast_to(row, sums_ref.shape)


def two_sum(first, second):
    total = first + second
    part = total - first
    return total, (first - (total - part)) + (second - part)


def pair_total(terms):
    while len(terms) > 1:
        merged = []
        for (high, low), (other, other_low) in zip(terms[::2], terms[1::2], strict=True):
            total, lost = two_sum(high, other)
            merged.append((total, lost if low is None else lost + (low + other_low)))
        terms = merged
    total, rest = terms[0]
    step = SUB // 2
    while step:
        total, lost = two_sum(total, pltpu.roll(total, step, 0))
        rest = rest + pltpu.roll(rest, step, 0) + lost
        step //= 2
    return total, rest


def quick_sum(first, second):
    total = first + second
    return total, second - (total - first)


def halves(value):
    scaled = 4097.0 * value
    high = scaled - (scaled - value)
    return high, value - high


def two_product(first, second):
    total = first * second
    first_high, first_low = halves(first)
    second_high, second_low = halves(second)
    rest = ((first_high * second_high - total) + first_high * second_low + first_low * second_high) + (
        first_low * second_low
    )
    return total, rest


def pair_add(first, second):
    total, rest = two_sum(first[0], second[0])
    return quick_sum(total, rest + (first[1] + second[1]))


def pair_sub(first, second):
    return pair_add(first, (-second[0], -second[1]))


def pair_mul(first, second):
    total, rest = two_product(first[0], second[0])
    return quick_sum(total, rest + (first[0] * second[1] + first[1] * second[0]))


def pair_div(first, second):
    guess = first[0] / second[0]
    total, rest = two_product(guess, second[0])
    left = ((first[0] - total) - rest) + (first[1] - guess * second[1])
    return quick_sum(guess, left / second[0])


def galerkin(moments):
    count = DEPTH
    matrix = {(i, j): moments[i + j + 1] for i in range(count) for j in range(i + 1)}
    right = [moments[i] for i in range(count)]
    for pivot in range(count):
        for i in range(pivot + 1, count):
            ratio = pair_div(matrix[i, pivot], matrix[pivot, pivot])
            for j in range(pivot + 1, i + 1):
                matrix[i, j] = pair_sub(matrix[i, j], pair_mul(ratio, matrix[j, pivot]))
            right[i] = pair_sub(right[i], pair_mul(ratio, right[pivot]))
    found = [None] * count
    for i in reversed(range(count)):
        value = right[i]
        for j in range(i + 1, count):
            value = pair_sub(value, pair_mul(matrix[j, i], found[j]))
        found[i] = pair_div(value, matrix[i, i])
    return [value[0] for value in found]


def finish_kernel(
    sums_ref,
    fields_ref,
    face_x_ref,
    face_y_ref,
    rims_ref,
    pressure_hbm,
    residual_hbm,
    east_hbm,
    north_hbm,
    pressure_ref,
    residual_ref,
    east_ref,
    north_ref,
    field_ref,
    sems,
):
    _, layers, tiles, height, _ = fields_ref.shape
    rows = height - 3 * SUB
    slots = layers // (LANES // GROUP)
    blocks = rows // SUB
    last_lane = lane_ids() == LANES - 1

    peers = sums_ref.shape[0]
    total, rest = pair_total([(sums_ref[k : k + SUB, :], None) for k in range(0, peers, SUB)])
    total, rest = quick_sum(total, rest + turn(total, -2 * DEPTH))
    moments = [
        tuple(jnp.broadcast_to(value[:, k : k + 1], (SUB, LANES)) for value in (total, rest)) for k in range(2 * DEPTH)
    ]
    coefs = galerkin(moments)

    def at(block, step=0):
        return pl.ds(LO + block * SUB + step, SUB)

    def mix(values):
        return functools.reduce(jnp.add, [coef * value for coef, value in zip(coefs, values, strict=True)])

    outs = (
        (pressure_ref, pressure_hbm),
        (residual_ref, residual_hbm),
        (east_ref, east_hbm),
        (north_ref, north_hbm),
    )

    def copies(group):
        part = pl.ds(group * slots, slots)
        return [
            pltpu.make_async_copy(ref.at[part], hbm.at[0, part], sems.at[index, group])
            for index, (ref, hbm) in enumerate(outs)
        ]

    def chunk(group, _):
        for slot in range(slots):
            layer = group * slots + slot
            for block in range(blocks + 1):
                values = []
                for tile in range(tiles):
                    found = [
                        fields_ref[power, layer, tile, at(block), :] for power in range(DEPTH + (block < blocks))
                    ]
                    value = mix(found[:DEPTH])
                    values.append(value)
                    field_ref[tile, at(block), :] = value
                    if block < blocks:
                        spot = (layer, pl.ds(block * SUB, SUB), pl.ds(tile * LANES, LANES))
                        pressure_ref[spot] = value
                        residual_ref[spot] = found[0] - mix(found[1:])
                if block < blocks:
                    rim = mix([rims_ref[power, slot, at(block), :] for power in range(DEPTH)])
                    rim = rim_of(rim, group)
                    moved = [turn(value, -1) for value in values]
                    for tile in range(tiles):
                        other = moved[tile]
                        if tile < tiles - 1:
                            other = jnp.where(last_lane, moved[tile + 1], other)
                        flux = face_y_ref[layer, tile, at(block), :] * (values[tile] - other)
                        if tile == tiles - 1:
                            flux = jnp.where(last_lane, rim, flux)
                        spot = (layer, pl.ds(block * SUB, SUB), pl.ds(tile * LANES, LANES))
                        north_ref[spot] = flux
            for block in range(blocks):
                for tile in range(tiles):
                    spot = (layer, pl.ds(block * SUB, SUB), pl.ds(tile * LANES, LANES))
                    east_ref[spot] = face_x_ref[layer, tile, at(block), :] * (
                        field_ref[tile, at(block), :] - field_ref[tile, at(block, 1), :]
                    )
        for copy in copies(group):
            copy.start()
        return 0

    lax.fori_loop(0, layers // slots, chunk, 0)

    def drain(group, _):
        for copy in copies(group):
            copy.wait()
        return 0

    lax.fori_loop(0, layers // slots, drain, 0)


def exchange(value, axis, near):
    count = lax.axis_size(axis)
    pairs = []
    for i in range(count):
        other = i + 1 if (i % 2 == 0) == near else i - 1
        if 0 <= other < count:
            pairs.append((i, other))
    return lax.ppermute(value, axis, pairs)


def on_device(log_perm, source):
    _, layers, rows, cols = log_perm.shape
    tiles, slots = cols // LANES, layers // (LANES // GROUP)
    height = rows + 3 * SUB
    full = (layers, tiles, height, LANES)
    deep = (layers + 1, tiles, height, LANES)
    spare = (layers + SPARE, tiles, height, LANES)
    ends = (2, layers, tiles * DEPTH, LANES)
    edges = (2, rows + SUB, LANES)
    strip = (slots + 2, height, LANES)
    inner = (slots, height, LANES)
    peers = lax.axis_size("gx") * lax.axis_size("gy")
    cells = layers * rows * cols

    log_perm, source = (pltpu.with_memory_space_constraint(value, pltpu.HBM) for value in (log_perm, source))
    powers = (in_vmem(DEPTH + 1, *full), in_vmem(*spare)) + (in_vmem(*full),) * 2 + (in_vmem(*deep), in_vmem(*full))
    far = pl.pallas_call(
        far_kernel,
        out_shape=in_vmem(*ends),
        in_specs=[HBM_SPEC] * 2,
        out_specs=VMEM_SPEC,
        scratch_shapes=[in_vmem(2, tiles, layers, SUB, LANES), pltpu.SemaphoreType.DMA((2, tiles))],
        compiler_params=params(16),
        name="far",
    )(log_perm, source)
    far = exchange(far, "gx", False)
    log_own, fields, near = pl.pallas_call(
        load_kernel,
        out_shape=(in_vmem(*full), powers[0], in_vmem(*ends)),
        in_specs=[HBM_SPEC] * 2,
        out_specs=[VMEM_SPEC] * 3,
        scratch_shapes=[pltpu.SemaphoreType.DMA((2, tiles))],
        compiler_params=params(16),
        cost_estimate=pl.CostEstimate(flops=cells, bytes_accessed=8 * cells, transcendentals=0),
        name="load",
    )(log_perm, source)
    near = exchange(near, "gx", True)
    *fields, last, first = pl.pallas_call(
        own_kernel,
        out_shape=powers + (in_vmem(*edges),) * 2,
        in_specs=[VMEM_SPEC] * 2,
        out_specs=[VMEM_SPEC] * 8,
        input_output_aliases={1: 0},
        compiler_params=params(16),
        cost_estimate=pl.CostEstimate(flops=60 * cells, bytes_accessed=8 * cells, transcendentals=4 * cells),
        name="own",
    )(log_own, fields)
    last, first, near, far, halo = pl.pallas_call(
        edge_kernel,
        out_shape=(in_vmem(*edges),) * 4 + (in_vmem(2, layers, tiles, SUB, LANES),),
        in_specs=[VMEM_SPEC] * 4,
        out_specs=[VMEM_SPEC] * 5,
        input_output_aliases={2: 0, 3: 1},
        compiler_params=params(16),
        name="edges",
    )(far, near, last, first)
    far = exchange(far, "gy", False)
    near = exchange(near, "gy", True)
    fields, _, face_x, face_y, face_z, face_w, parts = pl.pallas_call(
        first_kernel,
        out_shape=powers + (in_vmem(2, SUB, LANES),),
        in_specs=[VMEM_SPEC] * 7,
        out_specs=[VMEM_SPEC] * 7,
        input_output_aliases={1: 0, 2: 1, 3: 2, 4: 3, 5: 4, 6: 5},
        compiler_params=params(16),
        cost_estimate=pl.CostEstimate(flops=40 * cells, bytes_accessed=8 * cells, transcendentals=cells),
        name="first",
    )(halo, *fields)
    fields, rims, sums = pl.pallas_call(
        basis_kernel,
        out_shape=(powers[0], in_vmem(DEPTH, *inner), in_vmem(peers, LANES)),
        in_specs=[VMEM_SPEC] * 10,
        out_specs=[VMEM_SPEC] * 3,
        input_output_aliases={9: 0},
        scratch_shapes=[
            in_vmem(DEPTH, *strip),
            in_vmem(*strip),
            in_vmem(*inner),
            in_vmem(*inner),
            in_vmem(slots + 1, height, LANES),
        ],
        compiler_params=params(16),
        name="basis",
    )(last, first, far, near, parts, face_x, face_y, face_z, face_w, fields)
    sums = lax.all_to_all(sums, ("gx", "gy"), 0, 0, tiled=True)
    block = (layers, rows, cols)
    return pl.pallas_call(
        finish_kernel,
        out_shape=(jax.ShapeDtypeStruct((1, *block), F32),) * 4,
        in_specs=[VMEM_SPEC] * 5,
        out_specs=[ANY_SPEC] * 4,
        scratch_shapes=[in_vmem(*block)] * 4
        + [in_vmem(tiles, height, LANES), pltpu.SemaphoreType.DMA((4, layers // slots))],
        compiler_params=params(16),
        name="finish",
    )(sums, fields, face_x, face_y, rims)


def solution(mesh):
    spec = P(None, None, "gx", "gy")
    return jax.shard_map(on_device, mesh=mesh, in_specs=(spec,) * 2, out_specs=(spec,) * 4, check_vma=False)
```

```python
import functools

import jax
import jax.numpy as jnp
from jax import lax
from jax.experimental import pallas as pl
from jax.experimental.pallas import tpu as pltpu
from jax.sharding import PartitionSpec as P

DEPTH = 4
LANES = 128
SUB = 8
LO = 8
GROUP = 4 * DEPTH
CHUNK = 8
SPARE = 3
F32 = jnp.float32
HBM_SPEC = pl.BlockSpec(memory_space=pltpu.HBM)
VMEM_SPEC = pl.BlockSpec(memory_space=pltpu.VMEM)
ANY_SPEC = pl.BlockSpec(memory_space=pl.ANY)


def in_vmem(*shape):
    return pltpu.VMEM(shape, F32)


def params(limit):
    return pltpu.CompilerParams(vmem_limit_bytes=limit * 1024 * 1024)


def lane_ids():
    return lax.broadcasted_iota(jnp.int32, (SUB, LANES), 1)


def row_ids():
    return lax.broadcasted_iota(jnp.int32, (SUB, LANES), 0)


def turn(value, shift):
    return pltpu.roll(value, shift % LANES, 1) if shift % LANES else value


def reciprocal(value):
    return 1.0 / value


def even(axis):
    return lax.rem(lax.axis_index(axis), 2) == 0


def far_kernel(log_hbm, src_hbm, far_ref, rows_ref, sems):
    _, _, rows, cols = log_hbm.shape
    first = even("gx")
    start = pl.multiple_of(jnp.where(first, 0, rows - SUB), SUB)
    copies = []
    for index, hbm in enumerate((log_hbm, src_hbm)):
        for tile in range(cols // LANES):
            copies.append(
                pltpu.make_async_copy(
                    hbm.at[0, :, pl.ds(start, SUB), pl.ds(tile * LANES, LANES)],
                    rows_ref.at[index, tile],
                    sems.at[index, tile],
                )
            )
            copies[-1].start()
    for copy in copies:
        copy.wait()
    for tile in range(cols // LANES):
        head = rows_ref[:, tile, :, 0:DEPTH, :]
        tail = rows_ref[:, tile, :, SUB - DEPTH : SUB, :]
        far_ref[:, :, pl.ds(tile * DEPTH, DEPTH), :] = jnp.where(first, head, tail)


def load_kernel(log_hbm, src_hbm, log_ref, fields_ref, near_ref, sems):
    _, _, rows, cols = log_hbm.shape
    tiles = cols // LANES
    first = even("gx")
    copies = []
    refs = (log_ref, fields_ref.at[0])
    for index, (hbm, ref) in enumerate(zip((log_hbm, src_hbm), refs, strict=True)):
        for tile in range(tiles):
            copies.append(
                pltpu.make_async_copy(
                    hbm.at[0, :, :, pl.ds(tile * LANES, LANES)],
                    ref.at[:, tile, pl.ds(LO, rows), :],
                    sems.at[index, tile],
                )
            )
            copies[-1].start()
    for copy in copies:
        copy.wait()
    for index, ref in enumerate(refs):
        for tile in range(tiles):
            head = ref[:, tile, LO : LO + DEPTH, :]
            tail = ref[:, tile, LO + rows - DEPTH : LO + rows, :]
            near_ref[index, :, pl.ds(tile * DEPTH, DEPTH), :] = jnp.where(first, tail, head)


def pack(blocks_of, lane):
    lanes = lane_ids()
    total = None
    for layer, value in enumerate(blocks_of):
        moved = turn(value, layer * DEPTH - lane)
        total = moved if total is None else jnp.where(lanes // DEPTH == layer, moved, total)
    return total


def put_column_faces(face_y_ref, face_w_ref, layer, place, values):
    lanes = lane_ids()
    first_lane, last_lane = lanes == 0, lanes == LANES - 1
    tiles = len(values)
    moved = [turn(value, -1) for value in values]
    others = [jnp.where(last_lane, moved[tile + 1], moved[tile]) for tile in range(tiles - 1)] + [moved[-1]]
    faces = [reciprocal(value + other) for value, other in zip(values, others, strict=True)]
    faces[-1] = jnp.where(last_lane, 0.0, faces[-1])
    moved = [jnp.zeros((SUB, LANES), F32)] + [turn(face, 1) for face in faces]
    for tile in range(tiles):
        face_y_ref[layer, tile, place, :] = faces[tile]
        face_w_ref[layer, tile, place, :] = jnp.where(first_lane, moved[tile], moved[tile + 1])


def own_kernel(
    log_ref,
    fields_in,
    fields_ref,
    inverse_ref,
    face_x_ref,
    face_y_ref,
    face_z_ref,
    face_w_ref,
    last_ref,
    first_ref,
):
    del fields_in
    layers, tiles, height, _ = log_ref.shape
    rows = height - 3 * SUB
    blocks = rows // SUB
    slots = layers // (LANES // GROUP)
    ring = LO + rows + SUB
    base_ref = fields_ref.at[0]

    def at(block, step=0):
        return pl.ds(LO + block * SUB + step, SUB)

    def fill(layer, _):
        for tile in range(tiles):
            for block in range(blocks):
                value = 0.5 * jnp.exp(-log_ref[layer, tile, at(block), :])
                inverse_ref[layer, tile, at(block), :] = value
                if block == 0:
                    inverse_ref[layer, tile, pl.ds(ring, 1), :] = value[0:1]
        return 0

    lax.fori_loop(0, layers, fill, 0, unroll=2 * slots)

    zero = jnp.zeros((SUB, LANES), F32)
    for tile in range(tiles):
        for block in range(blocks + 1):
            face_z_ref[0, tile, at(block), :] = zero
            face_z_ref[layers, tile, at(block), :] = zero

    def faces(layer, _):
        for block in range(blocks):
            values = [inverse_ref[layer, tile, at(block), :] for tile in range(tiles)]
            put_column_faces(face_y_ref, face_w_ref, layer, at(block), values)
            for tile in range(tiles):
                face_x_ref[layer, tile, at(block), :] = reciprocal(
                    values[tile] + inverse_ref[layer, tile, at(block, 1), :]
                )
        return 0

    lax.fori_loop(0, layers, faces, 0, unroll=2 * slots)

    def faces_z(layer, _):
        for tile in range(tiles):
            for block in range(blocks):
                face_z_ref[layer, tile, at(block), :] = reciprocal(
                    inverse_ref[layer - 1, tile, at(block), :] + inverse_ref[layer, tile, at(block), :]
                )
        return 0

    lax.fori_loop(1, layers, faces_z, 0, unroll=2 * slots)

    base_ref[:, :, pl.ds(ring, 1), :] = base_ref[:, :, pl.ds(LO, 1), :]
    for index, ref in enumerate((log_ref, base_ref)):
        for block in range(blocks):
            part = pl.ds(block * SUB, SUB)
            last_ref[index, part, :] = pack(
                [ref[layer, tiles - 1, at(block), :] for layer in range(layers)], LANES - DEPTH
            )
            first_ref[index, part, :] = pack([ref[layer, 0, at(block), :] for layer in range(layers)], 0)


def edge_kernel(far_in, near_in, last_in, first_in, last_ref, first_ref, near_ref, far_ref, halo_ref):
    del last_in, first_in
    _, layers, tiles, _, _ = halo_ref.shape
    height = last_ref.shape[1]
    one, two = even("gx"), even("gy")
    for tile in range(tiles):
        part = pl.ds(tile * DEPTH, DEPTH)
        near, far = near_in[:, :, part, :], far_in[:, :, part, :]
        halo_ref[:, :, tile, 0:DEPTH, :] = jnp.where(one, near, far)
        halo_ref[:, :, tile, DEPTH:SUB, :] = jnp.where(one, far, near)
    for index in range(2):
        part = pl.ds(height - SUB, SUB)
        last_ref[index, part, :] = pack(
            [halo_ref[index, layer, tiles - 1] for layer in range(layers)], LANES - DEPTH
        )
        first_ref[index, part, :] = pack([halo_ref[index, layer, 0] for layer in range(layers)], 0)
    near_ref[...] = jnp.where(two, last_ref[...], first_ref[...])
    far_ref[...] = jnp.where(two, first_ref[...], last_ref[...])


def place_of(block, step=0):
    return pl.ds(LO + block * SUB + step, SUB)


def close_ring(ref, index, block, blocks, value):
    ring = LO + (blocks + 1) * SUB
    if block == 0:
        ref[(*index, pl.ds(ring, 1), slice(None))] = value[0:1]
    if block == blocks:
        ref[(*index, pl.ds(LO - 1, 1), slice(None))] = value[SUB - 1 : SUB]


def rim_of(values, group):
    return pltpu.roll(values, LANES - 1 - DEPTH - group * GROUP, 1)


def x_part(face_ref, index, old, old_index, block, value):
    there = old[(*old_index, place_of(block, 1), slice(None))]
    back = old[(*old_index, place_of(block, -1), slice(None))]
    return face_ref[(*index, place_of(block), slice(None))] * (value - there) - face_ref[
        (*index, place_of(block, -1), slice(None))
    ] * (back - value)


def inside_masks():
    here_x, here_y = lax.axis_index("gx"), lax.axis_index("gy")
    past_x, before_x = here_x < lax.axis_size("gx") - 1, here_x > 0
    past_y, before_y = here_y < lax.axis_size("gy") - 1, here_y > 0
    place = lane_ids() % GROUP
    inside_rows = jnp.where(row_ids() < DEPTH, past_x.astype(jnp.int32), before_x.astype(jnp.int32)) > 0
    inside_cols = (
        jnp.where(
            (place >= DEPTH) & (place < 2 * DEPTH),
            past_y.astype(jnp.int32),
            jnp.where((place >= 2 * DEPTH) & (place < 3 * DEPTH), before_y.astype(jnp.int32), 1),
        )
        > 0
    )
    return inside_rows, inside_cols


def apply_power(number, fields_ref, face_x_ref, face_y_ref, face_z_ref, face_w_ref, rims_ref):
    _, layers, tiles, height, _ = fields_ref.shape
    blocks = (height - 3 * SUB) // SUB
    slots = layers // (LANES // GROUP)
    old, new = fields_ref.at[number - 1], fields_ref.at[number]
    lanes = lane_ids()
    first_lane, last_lane = lanes == 0, lanes == LANES - 1
    inside_rows, _ = inside_masks()
    at = place_of

    def layer_range(start, count, block):
        levels = []
        for step in range(-1, count + 1):
            layer = start + step
            if step < 0:
                layer = jnp.maximum(layer, 0)
            if step == count:
                layer = jnp.minimum(layer, layers - 1)
            levels.append([old[layer, tile, at(block), :] for tile in range(tiles)])
        ups = [
            [
                face_z_ref[start + step, tile, at(block), :] * (levels[step][tile] - levels[step + 1][tile])
                for tile in range(tiles)
            ]
            for step in range(count + 1)
        ]
        for step in range(count):
            layer = start + step
            values = levels[step + 1]
            ahead = [turn(value, -1) for value in values]
            behind = [turn(value, 1) for value in values]
            rim = None
            if rims_ref is not None:
                rim = rim_of(rims_ref[number - 1, step % slots, at(block), :], start // slots + step // slots)
            out, back = [], []
            for tile in range(tiles):
                other = ahead[tile] if tile == tiles - 1 else jnp.where(last_lane, ahead[tile + 1], ahead[tile])
                out.append(face_y_ref[layer, tile, at(block), :] * (values[tile] - other))
                other = behind[tile] if tile == 0 else jnp.where(first_lane, behind[tile - 1], behind[tile])
                back.append(face_w_ref[layer, tile, at(block), :] * (other - values[tile]))
            if rim is not None:
                out[-1] = jnp.where(last_lane, rim, out[-1])
                back[0] = jnp.where(first_lane, rim, back[0])
            for tile in range(tiles):
                value = values[tile]
                result = (
                    (out[tile] - back[tile])
                    + x_part(face_x_ref, (layer, tile), old, (layer, tile), block, value)
                    + (ups[step + 1][tile] - ups[step][tile])
                )
                if block == blocks:
                    result = jnp.where(inside_rows, result, 0.0)
                new[layer, tile, at(block), :] = result
                if number < DEPTH:
                    close_ring(new, (layer, tile), block, blocks, result)
                yield tile, value, result

    def chunk(group, sums):
        own_sums, next_sums = list(sums[0]), list(sums[1])
        for block in range(blocks):
            for tile, value, result in layer_range(group * CHUNK, CHUNK, block):
                own_sums[tile] = own_sums[tile] + value * value
                next_sums[tile] = next_sums[tile] + value * result
        return tuple(own_sums), tuple(next_sums)

    start = (jnp.zeros((SUB, LANES), F32),) * tiles
    sums = lax.fori_loop(0, layers // CHUNK, chunk, (start, start))
    if number < DEPTH:
        for _ in layer_range(0, layers, blocks):
            pass
    return [functools.reduce(jnp.add, parts) for parts in sums]


def first_kernel(
    halo_ref,
    fields_in,
    inverse_in,
    face_x_in,
    face_y_in,
    face_z_in,
    face_w_in,
    fields_ref,
    inverse_ref,
    face_x_ref,
    face_y_ref,
    face_z_ref,
    face_w_ref,
    parts_ref,
):
    del fields_in, inverse_in, face_x_in, face_y_in, face_z_in, face_w_in
    _, layers, tiles, height, _ = fields_ref.shape
    blocks = (height - 3 * SUB) // SUB
    slots = layers // (LANES // GROUP)
    at = place_of

    def fill(layer, _):
        for tile in range(tiles):
            source = halo_ref[1, layer, tile]
            fields_ref[0, layer, tile, at(blocks), :] = source
            close_ring(fields_ref, (0, layer, tile), blocks, blocks, source)
            inverse_ref[layer, tile, at(blocks), :] = 0.5 * jnp.exp(-halo_ref[0, layer, tile])
        return 0

    lax.fori_loop(0, layers, fill, 0, unroll=layers)

    def faces(layer, _):
        values = [inverse_ref[layer, tile, at(blocks), :] for tile in range(tiles)]
        put_column_faces(face_y_ref, face_w_ref, layer, at(blocks), values)
        for tile in range(tiles):
            for block in (blocks - 1, blocks):
                face = reciprocal(
                    inverse_ref[layer, tile, at(block), :] + inverse_ref[layer, tile, at(block, 1), :]
                )
                face_x_ref[layer, tile, at(block), :] = face
                close_ring(face_x_ref, (layer, tile), block, blocks, face)
            before = inverse_ref[jnp.maximum(layer - 1, 0), tile, at(blocks), :]
            face_z_ref[layer, tile, at(blocks), :] = jnp.where(layer > 0, reciprocal(before + values[tile]), 0.0)
        return 0

    lax.fori_loop(0, layers, faces, 0, unroll=4 * slots)
    found = apply_power(1, fields_ref, face_x_ref, face_y_ref, face_z_ref, face_w_ref, None)
    for which, part in enumerate(found):
        parts_ref[which] = part


def basis_kernel(
    last_ref,
    first_ref,
    far_ref,
    near_ref,
    parts_ref,
    face_x_ref,
    face_y_ref,
    face_z_ref,
    face_w_ref,
    fields_in,
    fields_ref,
    rims_ref,
    sums_ref,
    strip_ref,
    strip_inv_ref,
    strip_x_ref,
    strip_y_ref,
    strip_z_ref,
):
    del fields_in
    _, layers, tiles, height, _ = fields_ref.shape
    rows = height - 3 * SUB
    slots = layers // (LANES // GROUP)
    groups = layers // slots
    blocks = rows // SUB
    lanes = lane_ids()
    place = lanes % GROUP
    inside_rows, inside_cols = inside_masks()
    inside_both = inside_rows & inside_cols
    first_lane, last_lane = lanes == 0, lanes == LANES - 1
    first_y = even("gy")
    at = place_of

    def spread(index, block):
        part = pl.ds(block * SUB, SUB)
        near, far = near_ref[index, part, :], far_ref[index, part, :]
        packed = (
            last_ref[index, part, :],
            jnp.where(first_y, near, far),
            jnp.where(first_y, far, near),
            first_ref[index, part, :],
        )
        found = []
        for slot in range(slots):
            moved = [turn(value, (kind - slot) * DEPTH) for kind, value in enumerate(packed)]
            found.append(
                jnp.where(
                    place < 2 * DEPTH,
                    jnp.where(place < DEPTH, moved[0], moved[1]),
                    jnp.where(place < 3 * DEPTH, moved[2], moved[3]),
                )
            )
        return found

    def put_strip(ref, block, values):
        ref[0, at(block), :] = turn(values[-1], GROUP)
        ref[slots + 1, at(block), :] = turn(values[0], -GROUP)
        for slot, value in enumerate(values):
            ref[slot + 1, at(block), :] = value
            close_ring(ref, (slot + 1,), block, blocks, value)

    for block in range(blocks + 1):
        put_strip(strip_ref.at[0], block, spread(1, block))
        values = [0.5 * jnp.exp(-value) for value in spread(0, block)]
        put_strip(strip_inv_ref, block, values)
    top, bottom = lanes >= LANES - GROUP, lanes < GROUP
    for block in range(blocks + 1):
        for slot in range(1, slots + 1):
            value = strip_inv_ref[slot, at(block), :]
            face = reciprocal(value + strip_inv_ref[slot, at(block, 1), :])
            strip_x_ref[slot - 1, at(block), :] = face
            close_ring(strip_x_ref, (slot - 1,), block, blocks, face)
            strip_y_ref[slot - 1, at(block), :] = reciprocal(value + turn(value, -1))
        for slot in range(slots + 1):
            face = reciprocal(strip_inv_ref[slot, at(block), :] + strip_inv_ref[slot + 1, at(block), :])
            if slot == 0:
                face = jnp.where(bottom, 0.0, face)
            if slot == slots:
                face = jnp.where(top, 0.0, face)
            strip_z_ref[slot, at(block), :] = face

    for power in range(1, DEPTH + 1):
        old = strip_ref.at[power - 1]
        for block in range(blocks + 1):
            levels = [old[slot, at(block), :] for slot in range(slots + 2)]
            ups = [
                strip_z_ref[slot, at(block), :] * (levels[slot] - levels[slot + 1]) for slot in range(slots + 1)
            ]
            values = []
            for slot in range(slots):
                value = levels[slot + 1]
                flux = strip_y_ref[slot, at(block), :] * (value - turn(value, -1))
                after = turn(flux, 1)
                rims_ref[power - 1, slot, at(block), :] = jnp.where(
                    place == DEPTH, after, turn(flux, 2 - 2 * DEPTH)
                )
                if power < DEPTH:
                    result = (
                        (flux - after)
                        + x_part(strip_x_ref, (slot,), old, (slot + 1,), block, value)
                        + (ups[slot + 1] - ups[slot])
                    )
                    values.append(jnp.where(inside_both if block == blocks else inside_cols, result, 0.0))
            if power < DEPTH:
                put_strip(strip_ref.at[power], block, values)

    zero = jnp.zeros((SUB, LANES), F32)

    def complete(group, lost):
        for slot in range(slots):
            layer = group * slots + slot
            for block in range(blocks + 1):
                rim = rim_of(rims_ref[0, slot, at(block), :], group)
                for tile, part in ((0, jnp.where(first_lane, -rim, 0.0)), (tiles - 1, jnp.where(last_lane, rim, 0.0))):
                    value = fields_ref[1, layer, tile, at(block), :] + part
                    fields_ref[1, layer, tile, at(block), :] = value
                    close_ring(fields_ref, (1, layer, tile), block, blocks, value)
                    if block < blocks:
                        lost = lost + part * fields_ref[0, layer, tile, at(block), :]
        return lost

    lost = lax.fori_loop(0, groups, complete, zero, unroll=4)

    found = [parts_ref[0], parts_ref[1] + lost]
    for number in range(2, DEPTH + 1):
        found += apply_power(number, fields_ref, face_x_ref, face_y_ref, face_z_ref, face_w_ref, rims_ref)
    total = jnp.concatenate([jnp.sum(part, axis=0, keepdims=True) for part in found], axis=0)
    total = total.T
    total, rest = pair_total([(total[k : k + SUB], None) for k in range(0, LANES, SUB)])
    row = jnp.concatenate([total[0:1], rest[0:1], jnp.zeros((1, LANES - 4 * DEPTH), F32)], axis=1)
    sums_ref[...] = jnp.broadcast_to(row, sums_ref.shape)


def two_sum(first, second):
    total = first + second
    part = total - first
    return total, (first - (total - part)) + (second - part)


def pair_total(terms):
    while len(terms) > 1:
        merged = []
        for (high, low), (other, other_low) in zip(terms[::2], terms[1::2], strict=True):
            total, lost = two_sum(high, other)
            merged.append((total, lost if low is None else lost + (low + other_low)))
        terms = merged
    total, rest = terms[0]
    step = SUB // 2
    while step:
        total, lost = two_sum(total, pltpu.roll(total, step, 0))
        rest = rest + pltpu.roll(rest, step, 0) + lost
        step //= 2
    return total, rest


def quick_sum(first, second):
    total = first + second
    return total, second - (total - first)


def halves(value):
    scaled = 4097.0 * value
    high = scaled - (scaled - value)
    return high, value - high


def two_product(first, second):
    total = first * second
    first_high, first_low = halves(first)
    second_high, second_low = halves(second)
    rest = ((first_high * second_high - total) + first_high * second_low + first_low * second_high) + (
        first_low * second_low
    )
    return total, rest


def pair_add(first, second):
    total, rest = two_sum(first[0], second[0])
    return quick_sum(total, rest + (first[1] + second[1]))


def pair_sub(first, second):
    return pair_add(first, (-second[0], -second[1]))


def pair_mul(first, second):
    total, rest = two_product(first[0], second[0])
    return quick_sum(total, rest + (first[0] * second[1] + first[1] * second[0]))


def pair_div(first, second):
    guess = first[0] / second[0]
    total, rest = two_product(guess, second[0])
    left = ((first[0] - total) - rest) + (first[1] - guess * second[1])
    return quick_sum(guess, left / second[0])


def galerkin(moments):
    count = DEPTH
    matrix = {(i, j): moments[i + j + 1] for i in range(count) for j in range(i + 1)}
    right = [moments[i] for i in range(count)]
    for pivot in range(count):
        for i in range(pivot + 1, count):
            ratio = pair_div(matrix[i, pivot], matrix[pivot, pivot])
            for j in range(pivot + 1, i + 1):
                matrix[i, j] = pair_sub(matrix[i, j], pair_mul(ratio, matrix[j, pivot]))
            right[i] = pair_sub(right[i], pair_mul(ratio, right[pivot]))
    found = [None] * count
    for i in reversed(range(count)):
        value = right[i]
        for j in range(i + 1, count):
            value = pair_sub(value, pair_mul(matrix[j, i], found[j]))
        found[i] = pair_div(value, matrix[i, i])
    return [value[0] for value in found]


def finish_kernel(
    sums_ref,
    fields_ref,
    face_x_ref,
    face_y_ref,
    rims_ref,
    pressure_hbm,
    residual_hbm,
    east_hbm,
    north_hbm,
    pressure_ref,
    residual_ref,
    east_ref,
    north_ref,
    field_ref,
    sems,
):
    _, layers, tiles, height, _ = fields_ref.shape
    rows = height - 3 * SUB
    slots = layers // (LANES // GROUP)
    blocks = rows // SUB
    last_lane = lane_ids() == LANES - 1

    peers = sums_ref.shape[0]
    total, rest = pair_total([(sums_ref[k : k + SUB, :], None) for k in range(0, peers, SUB)])
    total, rest = quick_sum(total, rest + turn(total, -2 * DEPTH))
    moments = [
        tuple(jnp.broadcast_to(value[:, k : k + 1], (SUB, LANES)) for value in (total, rest)) for k in range(2 * DEPTH)
    ]
    coefs = galerkin(moments)

    def at(block, step=0):
        return pl.ds(LO + block * SUB + step, SUB)

    def mix(values):
        return functools.reduce(jnp.add, [coef * value for coef, value in zip(coefs, values, strict=True)])

    outs = (
        (pressure_ref, pressure_hbm),
        (residual_ref, residual_hbm),
        (east_ref, east_hbm),
        (north_ref, north_hbm),
    )

    def copies(group):
        part = pl.ds(group * slots, slots)
        return [
            pltpu.make_async_copy(ref.at[part], hbm.at[0, part], sems.at[index, group])
            for index, (ref, hbm) in enumerate(outs)
        ]

    def chunk(group, _):
        for slot in range(slots):
            layer = group * slots + slot
            for block in range(blocks + 1):
                values = []
                for tile in range(tiles):
                    found = [
                        fields_ref[power, layer, tile, at(block), :] for power in range(DEPTH + (block < blocks))
                    ]
                    value = mix(found[:DEPTH])
                    values.append(value)
                    field_ref[tile, at(block), :] = value
                    if block < blocks:
                        spot = (layer, pl.ds(block * SUB, SUB), pl.ds(tile * LANES, LANES))
                        pressure_ref[spot] = value
                        residual_ref[spot] = found[0] - mix(found[1:])
                if block < blocks:
                    rim = mix([rims_ref[power, slot, at(block), :] for power in range(DEPTH)])
                    rim = rim_of(rim, group)
                    moved = [turn(value, -1) for value in values]
                    for tile in range(tiles):
                        other = moved[tile]
                        if tile < tiles - 1:
                            other = jnp.where(last_lane, moved[tile + 1], other)
                        flux = face_y_ref[layer, tile, at(block), :] * (values[tile] - other)
                        if tile == tiles - 1:
                            flux = jnp.where(last_lane, rim, flux)
                        spot = (layer, pl.ds(block * SUB, SUB), pl.ds(tile * LANES, LANES))
                        north_ref[spot] = flux
            for block in range(blocks):
                for tile in range(tiles):
                    spot = (layer, pl.ds(block * SUB, SUB), pl.ds(tile * LANES, LANES))
                    east_ref[spot] = face_x_ref[layer, tile, at(block), :] * (
                        field_ref[tile, at(block), :] - field_ref[tile, at(block, 1), :]
                    )
        for copy in copies(group):
            copy.start()
        return 0

    lax.fori_loop(0, layers // slots, chunk, 0)

    def drain(group, _):
        for copy in copies(group):
            copy.wait()
        return 0

    lax.fori_loop(0, layers // slots, drain, 0)


def exchange(value, axis, near):
    count = lax.axis_size(axis)
    pairs = []
    for i in range(count):
        other = i + 1 if (i % 2 == 0) == near else i - 1
        if 0 <= other < count:
            pairs.append((i, other))
    return lax.ppermute(value, axis, pairs)


def on_device(log_perm, source):
    _, layers, rows, cols = log_perm.shape
    tiles, slots = cols // LANES, layers // (LANES // GROUP)
    height = rows + 3 * SUB
    full = (layers, tiles, height, LANES)
    deep = (layers + 1, tiles, height, LANES)
    spare = (layers + SPARE, tiles, height, LANES)
    ends = (2, layers, tiles * DEPTH, LANES)
    edges = (2, rows + SUB, LANES)
    strip = (slots + 2, height, LANES)
    inner = (slots, height, LANES)
    peers = lax.axis_size("gx") * lax.axis_size("gy")
    cells = layers * rows * cols

    log_perm, source = (pltpu.with_memory_space_constraint(value, pltpu.HBM) for value in (log_perm, source))
    powers = (in_vmem(DEPTH + 1, *full), in_vmem(*spare)) + (in_vmem(*full),) * 2 + (in_vmem(*deep), in_vmem(*full))
    far = pl.pallas_call(
        far_kernel,
        out_shape=in_vmem(*ends),
        in_specs=[HBM_SPEC] * 2,
        out_specs=VMEM_SPEC,
        scratch_shapes=[in_vmem(2, tiles, layers, SUB, LANES), pltpu.SemaphoreType.DMA((2, tiles))],
        compiler_params=params(16),
        name="far",
    )(log_perm, source)
    far = exchange(far, "gx", False)
    log_own, fields, near = pl.pallas_call(
        load_kernel,
        out_shape=(in_vmem(*full), powers[0], in_vmem(*ends)),
        in_specs=[HBM_SPEC] * 2,
        out_specs=[VMEM_SPEC] * 3,
        scratch_shapes=[pltpu.SemaphoreType.DMA((2, tiles))],
        compiler_params=params(16),
        cost_estimate=pl.CostEstimate(flops=cells, bytes_accessed=8 * cells, transcendentals=0),
        name="load",
    )(log_perm, source)
    near = exchange(near, "gx", True)
    *fields, last, first = pl.pallas_call(
        own_kernel,
        out_shape=powers + (in_vmem(*edges),) * 2,
        in_specs=[VMEM_SPEC] * 2,
        out_specs=[VMEM_SPEC] * 8,
        input_output_aliases={1: 0},
        compiler_params=params(16),
        cost_estimate=pl.CostEstimate(flops=60 * cells, bytes_accessed=8 * cells, transcendentals=4 * cells),
        name="own",
    )(log_own, fields)
    last, first, near, far, halo = pl.pallas_call(
        edge_kernel,
        out_shape=(in_vmem(*edges),) * 4 + (in_vmem(2, layers, tiles, SUB, LANES),),
        in_specs=[VMEM_SPEC] * 4,
        out_specs=[VMEM_SPEC] * 5,
        input_output_aliases={2: 0, 3: 1},
        compiler_params=params(16),
        name="edges",
    )(far, near, last, first)
    far = exchange(far, "gy", False)
    near = exchange(near, "gy", True)
    fields, _, face_x, face_y, face_z, face_w, parts = pl.pallas_call(
        first_kernel,
        out_shape=powers + (in_vmem(2, SUB, LANES),),
        in_specs=[VMEM_SPEC] * 7,
        out_specs=[VMEM_SPEC] * 7,
        input_output_aliases={1: 0, 2: 1, 3: 2, 4: 3, 5: 4, 6: 5},
        compiler_params=params(16),
        cost_estimate=pl.CostEstimate(flops=40 * cells, bytes_accessed=8 * cells, transcendentals=cells),
        name="first",
    )(halo, *fields)
    fields, rims, sums = pl.pallas_call(
        basis_kernel,
        out_shape=(powers[0], in_vmem(DEPTH, *inner), in_vmem(peers, LANES)),
        in_specs=[VMEM_SPEC] * 10,
        out_specs=[VMEM_SPEC] * 3,
        input_output_aliases={9: 0},
        scratch_shapes=[
            in_vmem(DEPTH, *strip),
            in_vmem(*strip),
            in_vmem(*inner),
            in_vmem(*inner),
            in_vmem(slots + 1, height, LANES),
        ],
        compiler_params=params(16),
        name="basis",
    )(last, first, far, near, parts, face_x, face_y, face_z, face_w, fields)
    sums = lax.all_to_all(sums, ("gx", "gy"), 0, 0, tiled=True)
    block = (layers, rows, cols)
    return pl.pallas_call(
        finish_kernel,
        out_shape=(jax.ShapeDtypeStruct((1, *block), F32),) * 4,
        in_specs=[VMEM_SPEC] * 5,
        out_specs=[ANY_SPEC] * 4,
        scratch_shapes=[in_vmem(*block)] * 4
        + [in_vmem(tiles, height, LANES), pltpu.SemaphoreType.DMA((4, layers // slots))],
        compiler_params=params(16),
        name="finish",
    )(sums, fields, face_x, face_y, rims)


def solution(mesh):
    spec = P(None, None, "gx", "gy")
    return jax.shard_map(on_device, mesh=mesh, in_specs=(spec,) * 2, out_specs=(spec,) * 4, check_vma=False)
```
